32 devices in a mesh: dp: 4 (over y, x), fsdp: 8 (over z, core).
Axes of the slice: x: 2, y: 2, z: 4, core: 2. Of those that a mesh axis runs over, the one named last changes fastest.
Arguments:
- tokens: bfloat16 [32768, 768], P(('dp', 'fsdp')), may hold values from -6 to 6
- cotangent: bfloat16 [32768, 768], P(('dp', 'fsdp')), may hold values from -6 to 6
- image_ids: int32 [32768], P(('dp', 'fsdp')), may hold values from -1 to 4, as said below
- patch_grid: int32 [2, 32768], P(None, ('dp', 'fsdp')), may hold values from 0 to 23, as said below
- qkv_weight: float32 [768, 2304], P('fsdp')
- out_weight: float32 [768, 768], P('fsdp')
- up_weight: float32 [768, 3072], P('fsdp')
- down_weight: float32 [3072, 768], P('fsdp')
- vectors: float32 [10752], P('fsdp')
- qkv_first: float32 [768, 2304], P('fsdp'), may hold values from -80 to 80
- out_first: float32 [768, 768], P('fsdp'), may hold values from -12 to 12
- up_first: float32 [768, 3072], P('fsdp'), may hold values from -40 to 40
- down_first: float32 [3072, 768], P('fsdp'), may hold values from -64 to 64
- vector_first: float32 [10752], P('fsdp'), may hold values from -64 to 64
- qkv_second: float32 [768, 2304], P('fsdp')
- out_second: float32 [768, 768], P('fsdp')
- up_second: float32 [768, 3072], P('fsdp')
- down_second: float32 [3072, 768], P('fsdp')
- vector_second: float32 [10752], P('fsdp'), may hold values from 11.79648 to 47.18592
Outputs:
- output: bfloat16 [32768, 768], P(('dp', 'fsdp'))
- tokens_grad: bfloat16 [32768, 768], P(('dp', 'fsdp'))
- qkv_grad: float32 [768, 2304], P('fsdp')
- out_grad: float32 [768, 768], P('fsdp')
- up_grad: float32 [768, 3072], P('fsdp')
- down_grad: float32 [3072, 768], P('fsdp')
- vector_grad: float32 [10752], P('fsdp')
- down_bias_grad: float32 [768], replicated
- qkv_first_new: float32 [768, 2304], P('fsdp')
- out_first_new: float32 [768, 768], P('fsdp')
- up_first_new: float32 [768, 3072], P('fsdp')
- down_first_new: float32 [3072, 768], P('fsdp')
- vector_first_new: float32 [10752], P('fsdp')
- qkv_second_new: float32 [768, 2304], P('fsdp')
- out_second_new: float32 [768, 768], P('fsdp')
- up_second_new: float32 [768, 3072], P('fsdp')
- down_second_new: float32 [3072, 768], P('fsdp')
- vector_second_new: float32 [10752], P('fsdp')
- qkv_weight_new: float32 [768, 2304], P('fsdp')
- out_weight_new: float32 [768, 768], P('fsdp')
- up_weight_new: float32 [768, 3072], P('fsdp')
- down_weight_new: float32 [3072, 768], P('fsdp')
- vectors_new: float32 [10752], P('fsdp')
- weight_norms: float32 [4], replicated
- update_norms: float32 [4], replicated
The draws below stay inside these ranges and needn't reach their ends.
Inputs may be any that keep to these rules, and one draw needn't show every extreme that they name: `image_ids`: each device's 1024 slots form one unit of 1024 slots. A unit holds whole images in a row from its first slot, one of four sets that is the same in all units of a device: five of 14 x 14 patches; two of 20 x 20 and one of 14 x 14; one of 24 x 24 and one of 20 x 20; one of 24 x 24 and two of 14 x 14. Image k of unit u has id 5u + k; the rest of every unit is padding with id -1. `patch_grid`: row 0 holds each patch's row and row 1 its column in its image's square grid, patches in row-major order; padding has 0 in both.
All inputs are finite; a program needn't handle non-finite values.
Results may differ from the reference program's by a relative error of at most 0.013.
The reference program's roundings to bfloat16 on the way count: a program that leaves them out, or rounds other values in their place, can miss the bound.
Values may be sent and summed in bfloat16 or wider, within the bound.
No kernel may reach another device: no remote copies, remote signals or barrier semaphores. Data moves between devices by JAX's collectives and lax.ppermute only.
A program may use at most 192 MiB of HBM per device.

```python
import math
import jax
import jax.numpy as jnp
import numpy as np
from jax import lax

D = 768
H = 12
HD = 64
FF = 3072
TOK_DEV = 1024
PACK = 1024
S_SMALL = 14
S_MID = 20
S_LARGE = 24
STEP = 10
TOKENS = 32768
VEC = 10752


def ramp(count, low_end, high_end):
    return low_end + (high_end - low_end) * jnp.arange(count, dtype=jnp.float32) / max(count - 1, 1)


def matrix_law(key, rows, columns, fan_in, low_end, high_end):
    base = jax.random.normal(key, (rows, columns), jnp.float32)
    return base * ramp(rows, low_end, high_end)[:, None] * float(fan_in) ** (-0.5)


def second_law(key, rows, columns, grad_square, top_end, bottom_end):
    factor = jax.random.uniform(key, (rows, columns), jnp.float32, 1.0, 4.0)
    return factor * ramp(rows, top_end, bottom_end)[:, None] * (grad_square * 0.001)


def draw_qkv_weight(key, part):
    return matrix_law(key, D, 3 * D, D, 0.75, 1.3)


def draw_out_weight(key, part):
    return matrix_law(key, D, D, max(D // 64, 1), 0.75, 1.3)


def draw_up_weight(key, part):
    return matrix_law(key, D, FF, D, 0.75, 1.3)


def draw_down_weight(key, part):
    return matrix_law(key, FF, D, FF, 0.75, 1.3)


def draw_qkv_second(key, part):
    return second_law(key, D, 3 * D, 0.49 * TOKENS, 2.0, 0.5)


def draw_out_second(key, part):
    return second_law(key, D, D, 0.01 * TOKENS, 2.0, 0.5)


def draw_up_second(key, part):
    return second_law(key, D, FF, 0.12 * TOKENS, 2.0, 0.5)


def draw_down_second(key, part):
    return second_law(key, FF, D, 0.36 * TOKENS, 2.0, 0.5)


def draw_vectors(key, part):
    keys = jax.random.split(key, 5)
    shift_count = 7 * D + FF
    low_end = 0.7
    high_end = 1.4
    shifts = 0.3 * jax.random.normal(keys[0], (shift_count,), jnp.float32)
    gain_one = ramp(D, low_end, high_end) * jax.random.uniform(keys[1], (D,), jnp.float32, 0.85, 1.15)
    gain_two = ramp(D, low_end, high_end) * jax.random.uniform(keys[2], (D,), jnp.float32, 0.85, 1.15)
    magnitude = jnp.exp(jax.random.uniform(keys[3], (H, HD // 2), jnp.float32, math.log(0.05), 0.0))
    phase = jax.random.uniform(keys[4], (H, HD // 2), jnp.float32, -math.pi, math.pi)
    freqs = jnp.stack([magnitude * jnp.cos(phase), magnitude * jnp.sin(phase)]).reshape(-1)
    return jnp.concatenate([gain_one, shifts[0:D], gain_two, shifts[D:2 * D], shifts[2 * D:5 * D], shifts[5 * D:6 * D], shifts[6 * D:6 * D + FF], shifts[6 * D + FF:7 * D + FF], freqs])


def pack_tables():
    patterns = [[S_SMALL] * 5, [S_MID, S_MID, S_SMALL], [S_LARGE, S_MID], [S_LARGE, S_SMALL, S_SMALL]]
    units = TOK_DEV // PACK
    id_table = np.full((4, TOK_DEV), -1, np.int32)
    row_table = np.zeros((4, TOK_DEV), np.int32)
    col_table = np.zeros((4, TOK_DEV), np.int32)
    for pattern, sides in enumerate(patterns):
        for unit in range(units):
            offset = unit * PACK
            for index, side in enumerate(sides):
                count = side * side
                id_table[pattern, offset:offset + count] = unit * 5 + index
                row_table[pattern, offset:offset + count] = np.arange(count) // side
                col_table[pattern, offset:offset + count] = np.arange(count) % side
                offset += count
    return (id_table, row_table, col_table)


def device_patterns(key):
    devices = TOKENS // TOK_DEV
    chosen = jax.random.randint(jax.random.fold_in(key, 7), (devices,), 0, 4).astype(jnp.int32)
    order = jax.random.permutation(jax.random.fold_in(key, 11), devices)
    large_kind = (2 + jax.random.randint(jax.random.fold_in(key, 13), (), 0, 2)).astype(jnp.int32)
    chosen = chosen.at[order[0]].set(jnp.int32(0))
    chosen = chosen.at[order[1]].set(large_kind)
    return chosen


def draw_image_ids(key, part):
    tables = pack_tables()
    return jnp.asarray(tables[0])[device_patterns(key)].reshape(-1)


def draw_patch_grid(key, part):
    tables = pack_tables()
    chosen = device_patterns(key)
    rows = jnp.asarray(tables[1])[chosen].reshape(-1)
    columns = jnp.asarray(tables[2])[chosen].reshape(-1)
    return jnp.stack([rows, columns])


def shard_levels(key, dims, cuts, smallest, largest):
    def one(position, shards_of):
        heights = jax.random.uniform(jax.random.fold_in(jax.random.fold_in(key, 6), position), (shards_of,), jnp.float32, smallest / len(cuts), largest / len(cuts))
        return jnp.repeat(jnp.exp(heights), dims[position] // shards_of).reshape((-1,) + (1,) * (len(dims) - position - 1))

    loudness = one(*cuts[0])
    for cut in cuts[1:]:
        loudness = loudness * one(*cut)
    return loudness


def scatter_about(own_key, shape, scale, bound, cuts=(), held_as=jnp.bfloat16):
    drawn = scale * jax.random.normal(own_key, shape, jnp.float32)
    if cuts:
        drawn = drawn * shard_levels(own_key, shape, cuts, -0.22, 0.18)
    return jnp.clip(drawn, -bound, bound).astype(held_as)


def setup_inputs(seed: int = 0) -> dict:
    seeds = jax.random.split(jax.random.key(seed), 20)
    return {
        "tokens": scatter_about(seeds[0], (TOKENS, D), 1.0, 6.0, ((0, 32),)),
        "cotangent": scatter_about(seeds[1], (TOKENS, D), 1.0, 6.0, ((0, 32),)),
        "image_ids": draw_image_ids(jax.random.fold_in(seeds[19], 71), 0),
        "patch_grid": draw_patch_grid(jax.random.fold_in(seeds[19], 71), 0),
        "qkv_weight": draw_qkv_weight(jax.random.fold_in(seeds[19], 71), 0),
        "out_weight": draw_out_weight(jax.random.fold_in(seeds[19], 71), 0),
        "up_weight": draw_up_weight(jax.random.fold_in(seeds[19], 71), 0),
        "down_weight": draw_down_weight(jax.random.fold_in(seeds[19], 71), 0),
        "vectors": draw_vectors(jax.random.fold_in(seeds[19], 71), 0),
        "qkv_first": scatter_about(seeds[9], (D, 3 * D), (0.077 * TOKENS ** 0.5), 80.0, ((0, 8),), jnp.float32),
        "out_first": scatter_about(seeds[10], (D, D), (0.011 * TOKENS ** 0.5), 12.0, ((0, 8),), jnp.float32),
        "up_first": scatter_about(seeds[11], (D, FF), (0.0385 * TOKENS ** 0.5), 40.0, ((0, 8),), jnp.float32),
        "down_first": scatter_about(seeds[12], (FF, D), (0.066 * TOKENS ** 0.5), 64.0, ((0, 8),), jnp.float32),
        "vector_first": scatter_about(seeds[13], (VEC,), (0.066 * TOKENS ** 0.5), 64.0, ((0, 8),), jnp.float32),
        "qkv_second": draw_qkv_second(jax.random.fold_in(seeds[19], 71), 0),
        "out_second": draw_out_second(jax.random.fold_in(seeds[19], 71), 0),
        "up_second": draw_up_second(jax.random.fold_in(seeds[19], 71), 0),
        "down_second": draw_down_second(jax.random.fold_in(seeds[19], 71), 0),
        "vector_second": jnp.clip(jnp.exp(math.log(47.18592) - 1.3862944 * jax.random.uniform(seeds[18], (VEC,), jnp.float32) ** shard_levels(seeds[18], (VEC,), ((0, 8),), -0.2, 0.2)), 11.79648, 47.18592),
    }


@jax.custom_vjp
def low(v):
    return lax.optimization_barrier(v.astype(jnp.bfloat16)).astype(jnp.float32)

@jax.custom_vjp
def low_back(v):
    return v

def low_keep(v):
    return (low(v), None)

def low_pass(kept, grad):
    return (grad,)

def back_keep(v):
    return (v, None)

def back_low(kept, grad):
    return (low(grad),)
low.defvjp(low_keep, low_pass)
low_back.defvjp(back_keep, back_low)
highest = lax.Precision.HIGHEST
norm_eps = 1e-06
masked_fill = -1e+30

def layer_norm(values, norm_gain, norm_shift):
    centre = lax.optimization_barrier(jnp.mean(values, axis=-1, keepdims=True))
    centred = values - centre
    spread = lax.optimization_barrier(jnp.mean(centred * centred, axis=-1, keepdims=True))
    return centred * lax.rsqrt(spread + norm_eps) * norm_gain + norm_shift

def rotate(head_rows, angles):
    half = head_rows.shape[-1] // 2
    lower_half = head_rows[..., :half]
    upper_half = head_rows[..., half:]
    cosine = jnp.cos(angles)
    sine_part = jnp.sin(angles)
    return jnp.concatenate([lower_half * cosine - upper_half * sine_part, lower_half * sine_part + upper_half * cosine], axis=-1)

def split_vector(packed, width, hidden_width):
    lengths = [width, width, width, width, 3 * width, width, hidden_width, width, width]
    pieces = []
    offset = 0
    for length in lengths:
        pieces.append(packed[offset:offset + length])
        offset += length
    return pieces

def matmul(left, right):
    return jnp.dot(left, right, precision=highest, preferred_element_type=jnp.float32)

def block_forward(inputs, id_block, grid_block, matrices, pieces):
    qkv_w, out_w, up_w, down_w = matrices
    gain_one, shift_one, gain_two, shift_two, bias_qkv, bias_out, bias_up, bias_down, freq_flat = pieces
    count = inputs.shape[0]
    freqs = freq_flat.reshape(2, H, HD // 2)
    normed_one = low(layer_norm(inputs, gain_one, shift_one))
    projected = low_back(matmul(normed_one, qkv_w) + bias_qkv)
    queries = projected[:, :D].reshape(count, H, HD)
    keys = projected[:, D:2 * D].reshape(count, H, HD)
    values = low(projected[:, 2 * D:].reshape(count, H, HD))
    angles = grid_block[0][:, None, None] * freqs[0][None] + grid_block[1][:, None, None] * freqs[1][None]
    queries_rot = low(rotate(queries, angles))
    keys_rot = low(rotate(keys, angles))
    scores = low_back(jnp.einsum('shd,thd->hst', queries_rot, keys_rot, precision=highest, preferred_element_type=jnp.float32) * HD ** (-0.5))
    same_image = id_block[:, None] == id_block[None, :]
    masked = jnp.where(same_image[None], scores, masked_fill)
    peak = lax.optimization_barrier(jnp.max(masked, axis=-1, keepdims=True))
    weights = jnp.exp(masked - peak)
    probs = low(weights / lax.optimization_barrier(jnp.sum(weights, axis=-1, keepdims=True)))
    mixed = jnp.einsum('hst,thd->shd', probs, values, precision=highest, preferred_element_type=jnp.float32)
    mixed = low(low_back(mixed)).reshape(count, D)
    branch = low_back(matmul(mixed, out_w) + bias_out)
    resid = inputs + branch
    normed_two = low(layer_norm(resid, gain_two, shift_two))
    hidden = low_back(matmul(normed_two, up_w) + bias_up)
    active = low(jax.nn.gelu(hidden, approximate=False))
    return resid + matmul(active, down_w) + bias_down

def adam_terms(grad, first, second, master, decay):
    first_new = 0.9 * first + 0.1 * grad
    second_new = 0.999 * second + 0.001 * grad * grad
    first_hat = first_new / (1.0 - 0.9 ** STEP)
    second_hat = second_new / (1.0 - 0.999 ** STEP)
    update = first_hat / (jnp.sqrt(second_hat) + 1e-06) + decay * master
    return (first_new, second_new, update)

def reference(tokens, cotangent, image_ids, patch_grid, qkv_weight, out_weight, up_weight, down_weight, vectors, qkv_first, out_first, up_first, down_first, vector_first, qkv_second, out_second, up_second, down_second, vector_second):
    blocks = TOKENS // TOK_DEV
    valid = (image_ids >= 0).astype(jnp.float32)[:, None]
    given = cotangent.astype(jnp.float32) * valid
    id_blocks = image_ids.reshape(blocks, TOK_DEV)
    grid_blocks = patch_grid.astype(jnp.float32).reshape(2, blocks, TOK_DEV).transpose(1, 0, 2)

    def forward(inputs, qkv_w, out_w, up_w, down_w, packed):
        matrices = (low(qkv_w), low(out_w), low(up_w), low(down_w))
        pieces = split_vector(low(packed), D, FF)

        def one_block(item):
            return block_forward(item[0], item[1], item[2], matrices, pieces)
        outs = lax.map(jax.checkpoint(one_block), (inputs.reshape(blocks, TOK_DEV, D), id_blocks, grid_blocks))
        return outs.reshape(TOKENS, D)
    masters = (qkv_weight, out_weight, up_weight, down_weight)
    result, pull = jax.vjp(forward, tokens.astype(jnp.float32), qkv_weight, out_weight, up_weight, down_weight, vectors)
    grads = pull(given)
    output = result.astype(jnp.bfloat16)
    tokens_grad = grads[0].astype(jnp.bfloat16)
    bias_start = 8 * D + FF
    down_bias_grad = grads[5][bias_start:bias_start + D]
    firsts = (qkv_first, out_first, up_first, down_first)
    seconds = (qkv_second, out_second, up_second, down_second)
    first_list = []
    second_list = []
    update_list = []
    for index in range(4):
        first_new, second_new, update = adam_terms(grads[1 + index], firsts[index], seconds[index], masters[index], 0.01)
        first_list.append(first_new)
        second_list.append(second_new)
        update_list.append(update)
    weight_norms = jnp.stack([jnp.sqrt(jnp.sum(master * master)) for master in masters])
    update_norms = jnp.stack([jnp.sqrt(jnp.sum(update * update)) for update in update_list])
    new_list = []
    for index in range(4):
        ratio = weight_norms[index] / (update_norms[index] + 1e-06)
        new_list.append(masters[index] - 0.3 * ratio * update_list[index])
    vector_first_new, vector_second_new, vector_update = adam_terms(grads[5], vector_first, vector_second, vectors, 0.0)
    vectors_new = vectors - 0.2 * vector_update
    return (output, tokens_grad, grads[1], grads[2], grads[3], grads[4], grads[5], down_bias_grad, first_list[0], first_list[1], first_list[2], first_list[3], vector_first_new, second_list[0], second_list[1], second_list[2], second_list[3], vector_second_new, new_list[0], new_list[1], new_list[2], new_list[3], vectors_new, weight_norms, update_norms)
```

```python
from functools import partial

import jax
import jax.numpy as jnp
from jax import lax
from jax.sharding import PartitionSpec as P

H = 12
HD = 64
STEP = 10


norm_eps = 1e-06
masked_fill = -1e30


def layer_norm(values, norm_gain, norm_shift):
    centre = jnp.mean(values, axis=-1, keepdims=True)
    centred = values - centre
    spread = jnp.mean(centred * centred, axis=-1, keepdims=True)
    return centred * lax.rsqrt(spread + norm_eps) * norm_gain + norm_shift


def rotate(head_rows, angles):
    half = head_rows.shape[-1] // 2
    lower_half = head_rows[..., :half]
    upper_half = head_rows[..., half:]
    cosine = jnp.cos(angles)
    sine_part = jnp.sin(angles)
    return jnp.concatenate(
        [
            lower_half * cosine - upper_half * sine_part,
            lower_half * sine_part + upper_half * cosine,
        ],
        axis=-1,
    )


def split_vector(packed, width, hidden_width):
    lengths = [width, width, width, width, 3 * width, width, hidden_width, width, width]
    pieces = []
    offset = 0
    for length in lengths:
        pieces.append(packed[offset : offset + length])
        offset += length
    return pieces


def exact_gelu(values):
    return jax.nn.gelu(values, approximate=False)


def across_rows(left, right):
    return lax.dot_general(
        left, right, (((0,), (0,)), ((), ())), preferred_element_type=jnp.float32
    )


def against_columns(left, right):
    return lax.dot_general(
        left, right, (((1,), (1,)), ((), ())), preferred_element_type=jnp.float32
    )


def attend_forward(inputs, same_image, scale):
    query, key_rows, value_rows = inputs
    scores = against_columns(query, key_rows) * scale
    masked = jnp.where(same_image, scores, masked_fill)
    peak = jnp.max(masked, axis=1, keepdims=True)
    weights = jnp.exp(masked - peak)
    total = jnp.sum(weights, axis=1, keepdims=True)
    probs = (weights / total).astype(jnp.bfloat16)
    mixed = jnp.dot(probs, value_rows, preferred_element_type=jnp.float32).astype(jnp.bfloat16)
    return (mixed, (peak + jnp.log(total))[:, 0])


def attend_backward(inputs, same_image, scale):
    query, key_rows, value_rows, grad_mixed, log_total = inputs
    scores = against_columns(query, key_rows) * scale
    masked = jnp.where(same_image, scores, masked_fill)
    probs = jnp.exp(masked - log_total[:, None])
    grad_probs = against_columns(grad_mixed, value_rows)
    delta = jnp.sum(probs * grad_probs, axis=1, keepdims=True)
    grad_scores = jnp.where(same_image, probs * (grad_probs - delta), 0.0).astype(jnp.bfloat16)
    grad_query = jnp.dot(grad_scores, key_rows, preferred_element_type=jnp.float32) * scale
    grad_key = across_rows(grad_scores, query) * scale
    grad_value = across_rows(probs.astype(jnp.bfloat16), grad_mixed)
    return (grad_query, grad_key, grad_value)


def adam_terms(grad, first, second, master, decay):
    first_new = 0.9 * first + 0.1 * grad
    second_new = 0.999 * second + 0.001 * grad * grad
    first_hat = first_new / (1.0 - 0.9**STEP)
    second_hat = second_new / (1.0 - 0.999**STEP)
    update = first_hat / (jnp.sqrt(second_hat) + 1e-06) + decay * master
    return (first_new, second_new, update)


def px(x): return lax.ppermute(x,"dp",[(i,i^1) for i in range(4)])
def py(x): return lax.ppermute(x,"dp",[(i,i^2) for i in range(4)])
def pd(x): return lax.ppermute(x,"dp",[(i,i^3) for i in range(4)])
def pc(x): return lax.ppermute(x,"fsdp",[(i,i^1) for i in range(8)])
def pz(x,s): return lax.ppermute(x,"fsdp",[(i,(i+2*s)%8) for i in range(8)])
def place():
    d=lax.axis_index("dp"); f=lax.axis_index("fsdp")
    return d%2, d//2, f//2, f%2
def pick(flag,a,b):
    return jnp.where(flag==0,a,b)
def order_z(own, got, z):
    out=[]
    cand=[own]+got
    for k in range(4):
        rel=(z-k)%4
        v=cand[3]
        for s in (2,1,0): v=jnp.where(rel==s,cand[s],v)
        out.append(v)
    return out
def gather(shard):
    x,y,z,c=place()
    r,C=shard.shape
    h,w=r//2,C//2
    part=lax.dynamic_slice(shard,(x*h,y*w),(h,w))
    got=[pz(part,s) for s in (1,2,3)]
    Z=jnp.stack(order_z(part,got,z))
    zx=px(Z); zy=py(Z)
    fy=py(zx[:2]); fx=px(zy[2:])
    zd=jnp.concatenate([fy,fx],0)
    top=jnp.concatenate([pick(y,pick(x,Z,zx),pick(x,zy,zd)),pick(y,pick(x,zy,zd),pick(x,Z,zx))],2)
    bot=jnp.concatenate([pick(y,pick(x,zx,Z),pick(x,zd,zy)),pick(y,pick(x,zd,zy),pick(x,zx,Z))],2)
    full=jnp.concatenate([top,bot],1)
    other=pc(full)
    both=jnp.stack([pick(c,full,other),pick(c,other,full)],1)
    return both.reshape(8*r,C)
def rnd(v): return v.astype(jnp.bfloat16)
def up(v): return v.astype(jnp.float32)
def reduce(G):
    x,y,z,c=place()
    R,C=G.shape; r=R//8; h,w=r//2,C//2
    G=G.reshape(4,2,r,C)
    mine=pick(c,G[:,0],G[:,1]); theirs=pick(c,G[:,1],G[:,0])
    S=rnd(up(mine)+up(pc(theirs)))
    q=lambda a,b: lax.dynamic_slice(S,(0,a*h,b*w),(4,h,w))
    own,qx,qy,qd=q(x,y),q(1-x,y),q(x,1-y),q(1-x,1-y)
    d0=px(qd[:2]); d1=py(qd[2:])
    sx=jnp.concatenate([qx[:2],rnd(up(qx[2:])+up(d1))],0)
    sy=jnp.concatenate([rnd(up(qy[:2])+up(d0)),qy[2:]],0)
    gx=px(sx); gy=py(sy)
    D=rnd(up(own)+up(gx)+up(gy))
    send=lambda s: lax.dynamic_index_in_dim(D,(z+s)%4,0,keepdims=False)
    got=[pz(send(s),s) for s in (1,2,3)]
    F=rnd(up(send(0))+up(got[0])+up(got[1])+up(got[2]))
    rx,ry,rd=px(F),py(F),pd(F)
    tl=pick(y,pick(x,F,rx),pick(x,ry,rd)); tr=pick(y,pick(x,ry,rd),pick(x,F,rx))
    bl=pick(y,pick(x,rx,F),pick(x,rd,ry)); br=pick(y,pick(x,rd,ry),pick(x,rx,F))
    return up(jnp.concatenate([jnp.concatenate([tl,tr],1),jnp.concatenate([bl,br],1)],0))


def sum_z(v):
    x, y, z, c = place()
    got = [pz(v, s) for s in (1, 2, 3)]
    a = order_z(v, got, z)
    return (a[0] + a[1]) + (a[2] + a[3])


def total_fsdp(v):
    return sum_z(v + pc(v))


def total_all(v):
    v = v + pc(v)
    v = v + px(v)
    v = v + py(v)
    return sum_z(v)


def gather_vector(shard):
    x, y, z, c = place()
    row = shard.reshape(1, -1)
    rows = jnp.stack(order_z(row, [pz(row, s) for s in (1, 2, 3)], z))
    other = pc(rows)
    return jnp.stack([pick(c, rows, other), pick(c, other, rows)], 1).reshape(-1)


def reduce_vector(v):
    x, y, z, c = place()
    v = v.reshape(4, 2, -1)
    v = v + pc(v)
    v = v + px(v)
    v = v + py(v)
    v = pick(c, v[:, 0], v[:, 1])
    send = lambda s: lax.dynamic_index_in_dim(v, (z + s) % 4, 0, keepdims=True)
    got = [pz(send(s), s) for s in (1, 2, 3)]
    return (send(0) + got[0] + got[1] + got[2]).reshape(-1)


def body(
    mesh_fast,
    tokens,
    cotangent,
    image_ids,
    patch_grid,
    qkv_weight,
    out_weight,
    up_weight,
    down_weight,
    vectors,
    qkv_first,
    out_first,
    up_first,
    down_first,
    vector_first,
    qkv_second,
    out_second,
    up_second,
    down_second,
    vector_second,
):
    rows = tokens.shape[0]
    width = tokens.shape[1]
    hidden_width = up_weight.shape[1]
    scale = HD ** (-0.5)
    masters = (qkv_weight, out_weight, up_weight, down_weight)
    low_qkv = qkv_weight.astype(jnp.bfloat16)
    low_out = out_weight.astype(jnp.bfloat16)
    low_up = up_weight.astype(jnp.bfloat16)
    low_down = down_weight.astype(jnp.bfloat16)
    low_vectors = vectors.astype(jnp.bfloat16)
    if mesh_fast:
        get, get_vector, give, give_vector = gather, gather_vector, reduce, reduce_vector
        over_fsdp, over_all = total_fsdp, total_all
    else:
        get = get_vector = lambda v: lax.all_gather(v, "fsdp", axis=0, tiled=True)
        give = lambda v: lax.psum(
            lax.psum_scatter(up(v), "fsdp", scatter_dimension=0, tiled=True), "dp"
        )
        give_vector = give
        over_fsdp = lambda v: lax.psum(v, "fsdp")
        over_all = lambda v: lax.psum(v, ("dp", "fsdp"))
    full_vectors = get_vector(low_vectors)
    full_qkv, full_out, full_up, full_down = get(low_qkv), get(low_out), get(low_up), get(low_down)
    gain_one, shift_one, gain_two, shift_two, bias_qkv, bias_out, bias_up, bias_down, freq_flat = (
        split_vector(full_vectors.astype(jnp.float32), width, hidden_width)
    )
    freqs = freq_flat.reshape(2, H, HD // 2)
    given = cotangent.astype(jnp.float32) * (image_ids >= 0).astype(jnp.float32)[:, None]
    grid_rows = patch_grid[0].astype(jnp.float32)
    grid_cols = patch_grid[1].astype(jnp.float32)

    def rotary(query_part, key_part, freq_table):
        angles = (
            grid_rows[:, None, None] * freq_table[0][None]
            + grid_cols[:, None, None] * freq_table[1][None]
        )
        return (rotate(query_part, angles), rotate(key_part, angles))

    inputs = tokens.astype(jnp.float32)
    normed_one = layer_norm(inputs, gain_one, shift_one).astype(jnp.bfloat16)
    projected = jnp.dot(normed_one, full_qkv, preferred_element_type=jnp.float32) + bias_qkv
    queries = projected[:, :width].reshape(rows, H, HD)
    keys = projected[:, width : 2 * width].reshape(rows, H, HD)
    values = projected[:, 2 * width :].reshape(rows, H, HD).astype(jnp.bfloat16)
    queries_rot, keys_rot = rotary(queries, keys, freqs)
    query_heads = queries_rot.astype(jnp.bfloat16).transpose(1, 0, 2)
    key_heads = keys_rot.astype(jnp.bfloat16).transpose(1, 0, 2)
    value_heads = values.transpose(1, 0, 2)
    same_image = image_ids[:, None] == image_ids[None, :]
    mixed_heads, log_total = lax.map(
        partial(attend_forward, same_image=same_image, scale=scale),
        (query_heads, key_heads, value_heads),
    )
    mixed = mixed_heads.transpose(1, 0, 2).reshape(rows, width)
    resid = inputs + jnp.dot(mixed, full_out, preferred_element_type=jnp.float32) + bias_out
    normed_two = layer_norm(resid, gain_two, shift_two).astype(jnp.bfloat16)
    hidden = jnp.dot(normed_two, full_up, preferred_element_type=jnp.float32) + bias_up
    active = exact_gelu(hidden).astype(jnp.bfloat16)
    output = (
        resid + jnp.dot(active, full_down, preferred_element_type=jnp.float32) + bias_down
    ).astype(jnp.bfloat16)
    back_qkv, back_out, back_up, back_down = full_qkv, full_out, full_up, full_down
    given_low = given.astype(jnp.bfloat16)
    down_grad = across_rows(active, given_low)
    grad_bias_down = jnp.sum(given, axis=0)
    down_bias_grad = over_all(grad_bias_down.reshape(1, -1)).reshape(-1)
    grad_active = against_columns(given_low, back_down)
    unused_gelu, gelu_pull = jax.vjp(exact_gelu, hidden)
    grad_hidden = gelu_pull(grad_active)[0].astype(jnp.bfloat16)
    up_grad = across_rows(normed_two, grad_hidden)
    grad_bias_up = jnp.sum(grad_hidden.astype(jnp.float32), axis=0)
    grad_normed_two = against_columns(grad_hidden, back_up)
    unused_two, norm_pull_two = jax.vjp(layer_norm, resid, gain_two, shift_two)
    grad_resid_part, grad_gain_two, grad_shift_two = norm_pull_two(grad_normed_two)
    grad_resid = given + grad_resid_part
    grad_branch = grad_resid.astype(jnp.bfloat16)
    out_grad = across_rows(mixed, grad_branch)
    grad_bias_out = jnp.sum(grad_branch.astype(jnp.float32), axis=0)
    grad_mixed = against_columns(grad_branch, back_out).astype(jnp.bfloat16)
    grad_mixed_heads = grad_mixed.reshape(rows, H, HD).transpose(1, 0, 2)
    grad_query_heads, grad_key_heads, grad_value_heads = lax.map(
        partial(attend_backward, same_image=same_image, scale=scale),
        (query_heads, key_heads, value_heads, grad_mixed_heads, log_total),
    )
    unused_rot, rotary_pull = jax.vjp(rotary, queries, keys, freqs)
    grad_queries, grad_keys, grad_freqs = rotary_pull(
        (grad_query_heads.transpose(1, 0, 2), grad_key_heads.transpose(1, 0, 2))
    )
    grad_values = grad_value_heads.transpose(1, 0, 2)
    grad_projected = jnp.concatenate(
        [
            grad_queries.reshape(rows, width),
            grad_keys.reshape(rows, width),
            grad_values.reshape(rows, width),
        ],
        axis=1,
    ).astype(jnp.bfloat16)
    qkv_grad = across_rows(normed_one, grad_projected)
    grad_bias_qkv = jnp.sum(grad_projected.astype(jnp.float32), axis=0)
    grad_normed_one = against_columns(grad_projected, back_qkv)
    unused_one, norm_pull_one = jax.vjp(layer_norm, inputs, gain_one, shift_one)
    grad_tokens_part, grad_gain_one, grad_shift_one = norm_pull_one(grad_normed_one)
    tokens_grad = (grad_resid + grad_tokens_part).astype(jnp.bfloat16)
    vector_grad = jnp.concatenate(
        [
            grad_gain_one,
            grad_shift_one,
            grad_gain_two,
            grad_shift_two,
            grad_bias_qkv,
            grad_bias_out,
            grad_bias_up,
            grad_bias_down,
            grad_freqs.reshape(-1),
        ]
    )
    reduced = (
        give(rnd(qkv_grad)),
        give(rnd(out_grad)),
        give(rnd(up_grad)),
        give(rnd(down_grad)),
        give_vector(vector_grad),
    )
    firsts = (qkv_first, out_first, up_first, down_first)
    seconds = (qkv_second, out_second, up_second, down_second)
    first_list = []
    second_list = []
    update_list = []
    for index in range(4):
        first_new, second_new, update = adam_terms(
            reduced[index], firsts[index], seconds[index], masters[index], 0.01
        )
        first_list.append(first_new)
        second_list.append(second_new)
        update_list.append(update)
    update_local = jnp.stack([jnp.sum(update * update) for update in update_list])
    weight_local = jnp.stack([jnp.sum(matrix * matrix) for matrix in masters])
    weight_squares = over_fsdp(weight_local.reshape(1, -1)).reshape(-1)
    update_squares = over_fsdp(update_local.reshape(1, -1)).reshape(-1)
    weight_norms = jnp.sqrt(weight_squares)
    update_norms = jnp.sqrt(update_squares)
    new_list = []
    for index in range(4):
        ratio = weight_norms[index] / (update_norms[index] + 1e-06)
        new_list.append(masters[index] - 0.3 * ratio * update_list[index])
    vector_first_new, vector_second_new, vector_update = adam_terms(
        reduced[4], vector_first, vector_second, vectors, 0.0
    )
    vectors_new = vectors - 0.2 * vector_update
    return (
        output,
        tokens_grad,
        reduced[0],
        reduced[1],
        reduced[2],
        reduced[3],
        reduced[4],
        down_bias_grad,
        first_list[0],
        first_list[1],
        first_list[2],
        first_list[3],
        vector_first_new,
        second_list[0],
        second_list[1],
        second_list[2],
        second_list[3],
        vector_second_new,
        new_list[0],
        new_list[1],
        new_list[2],
        new_list[3],
        vectors_new,
        weight_norms,
        update_norms,
    )


def solution(mesh):
    in_specs = (
        P(("dp", "fsdp"), None),
        P(("dp", "fsdp"), None),
        P(("dp", "fsdp")),
        P(None, ("dp", "fsdp")),
        P("fsdp", None),
        P("fsdp", None),
        P("fsdp", None),
        P("fsdp", None),
        P("fsdp"),
        P("fsdp", None),
        P("fsdp", None),
        P("fsdp", None),
        P("fsdp", None),
        P("fsdp"),
        P("fsdp", None),
        P("fsdp", None),
        P("fsdp", None),
        P("fsdp", None),
        P("fsdp"),
    )
    out_specs = (
        P(("dp", "fsdp"), None),
        P(("dp", "fsdp"), None),
        P("fsdp", None),
        P("fsdp", None),
        P("fsdp", None),
        P("fsdp", None),
        P("fsdp"),
        P(),
        P("fsdp", None),
        P("fsdp", None),
        P("fsdp", None),
        P("fsdp", None),
        P("fsdp"),
        P("fsdp", None),
        P("fsdp", None),
        P("fsdp", None),
        P("fsdp", None),
        P("fsdp"),
        P("fsdp", None),
        P("fsdp", None),
        P("fsdp", None),
        P("fsdp", None),
        P("fsdp"),
        P(),
        P(),
    )
    fast = mesh.shape["dp"] == 4 and mesh.shape["fsdp"] == 8
    return jax.shard_map(partial(body, fast), mesh=mesh, in_specs=in_specs, out_specs=out_specs, check_vma=False)
```

```python
from functools import partial

import jax
import jax.numpy as jnp
from jax import lax
from jax.experimental import pallas as pl
from jax.experimental.pallas import tpu as pltpu
from jax.sharding import PartitionSpec as P

H = 12
HD = 64
STEP = 10
QT = 256
KT = 128
PAIRS = 3
VARIANTS = (2, 3, 4, 5, 7, 8)
norm_eps = 1e-06
bf = jnp.bfloat16
f32 = jnp.float32


def nt(a, b):
    return lax.dot_general(a, b, (((1,), (1,)), ((), ())), preferred_element_type=f32)


def nn(a, b):
    return lax.dot_general(a, b, (((1,), (0,)), ((), ())), preferred_element_type=f32)


def rnd(v):
    return v.astype(bf)


def up(v):
    return v.astype(f32)


def params(mib=48):
    return pltpu.CompilerParams(vmem_limit_bytes=mib << 20)


def cost(flops, moved):
    return pl.CostEstimate(flops=int(flops), bytes_accessed=int(moved), transcendentals=0)


def shaped(shape, kind):
    return jax.ShapeDtypeStruct(shape, kind)


def row_norm(v):
    centre = jnp.mean(v, axis=-1, keepdims=True)
    centred = v - centre
    spread = jnp.mean(centred * centred, axis=-1, keepdims=True)
    scale = lax.rsqrt(spread + norm_eps)
    return centred * scale, scale


def first_kernel(tok_ref, vec_ref, freq_ref, grid_ref, n_ref, nt_ref, cos_ref, sin_ref):
    w = tok_ref.shape[1]
    hat, scale = row_norm(up(tok_ref[...]))
    normed = hat * vec_ref[:, :w] + vec_ref[:, w : 2 * w]
    n_ref[...] = rnd(normed)
    nt_ref[...] = rnd(normed.T)
    g = grid_ref[...]
    angle = g[:, 0:1] * freq_ref[0:1, :] + g[:, 1:2] * freq_ref[1:2, :]
    lane = lax.broadcasted_iota(jnp.int32, (1, w), 1)
    cos_ref[...] = jnp.cos(angle)
    s = jnp.sin(angle)
    sin_ref[...] = jnp.where(lane & 63 < 32, -s, s)


def first(tokens, vec, freq, grid_t):
    n, w = tokens.shape
    rows = lambda: pl.BlockSpec((QT, w), lambda i: (i, 0))
    whole = lambda a: pl.BlockSpec(a.shape, lambda i: (0, 0))
    return pl.pallas_call(
        first_kernel,
        name="first",
        grid=(n // QT,),
        in_specs=[rows(), whole(vec), whole(freq), pl.BlockSpec((QT, 2), lambda i: (i, 0))],
        out_specs=[rows(), pl.BlockSpec((w, QT), lambda i: (0, i)), rows(), rows()],
        out_shape=[shaped((n, w), bf), shaped((w, n), bf), shaped((n, w), f32), shaped((n, w), f32)],
        compiler_params=params(),
        cost_estimate=cost(1e10, 1e7),
    )(tokens, vec, freq, grid_t)


def swap(v):
    w = v.shape[1]
    lane = lax.broadcasted_iota(jnp.int32, (1, w), 1)
    return jnp.where(lane & 63 < 32, pltpu.roll(v, w - 32, 1), pltpu.roll(v, 32, 1))


def project_kernel(n_ref, w_ref, b_ref, cos_ref, sin_ref, o_ref):
    j = pl.program_id(0)
    u = nn(n_ref[...], w_ref[...]) + b_ref[...]

    @pl.when(j < 6)
    def _():
        turned = u * cos_ref[...] + swap(u) * sin_ref[...]
        o_ref[...] = rnd(turned * jnp.where(j < 3, 0.125, 1.0))

    @pl.when(j >= 6)
    def _():
        o_ref[...] = rnd(u)


def project(normed, weight, vec, cos, sin):
    n, w = normed.shape
    return pl.pallas_call(
        project_kernel,
        name="project",
        grid=(9,),
        in_specs=[
            pl.BlockSpec((n, w), lambda j: (0, 0)),
            pl.BlockSpec((w, 256), lambda j: (0, j)),
            pl.BlockSpec((1, 256), lambda j: (0, 12 + j)),
            pl.BlockSpec((n, 256), lambda j: (0, jnp.where(j < 6, j % 3, 2))),
            pl.BlockSpec((n, 256), lambda j: (0, jnp.where(j < 6, j % 3, 2))),
        ],
        out_specs=pl.BlockSpec((n, 256), lambda j: (0, j)),
        out_shape=shaped((n, 3 * w), bf),
        compiler_params=params(),
        cost_estimate=cost(8e9, 1e7),
    )(normed, weight, vec, cos, sin)


def tables(ids):
    n = ids.shape[0]
    lane = jnp.arange(128) & 63
    one = (ids[:, None] + 1 == lane[None]).astype(f32)
    small = (lane < 8)[None]
    aug_q = rnd(jnp.where(small, one, 0.0))
    aug_k = rnd(jnp.where(small, (one - 1.0) * 1e30, jnp.where((lane < 11)[None], 1.0, 0.0)))
    tiles = n // QT
    hit = (ids.reshape(tiles, QT, 1) == ids[None, None, :]).any(1)
    pos = jnp.arange(n)[None]
    lo = jnp.min(jnp.where(hit, pos, n), 1) // KT
    hi = jnp.max(jnp.where(hit, pos, -1), 1) // KT + 1
    need = hi - lo
    width = jnp.full_like(need, VARIANTS[-1])
    for v in VARIANTS[::-1]:
        width = jnp.where(need <= v, v, width)
    start = jnp.minimum(lo, n // KT - width)
    return aug_q, aug_k, jnp.stack([start, width]).astype(jnp.int32)


def low_lanes():
    return lax.broadcasted_iota(jnp.int32, (1, 128), 1) < 64


def attend_kernel(rng, q_ref, k_ref, v_ref, aq_ref, ak_ref, mix_ref, mixt_ref, lb_ref, vt):
    i = pl.program_id(1)
    n = k_ref.shape[0]
    start = rng[0, i]
    width = rng[1, i]
    low = low_lanes()

    @pl.when(i == 0)
    def _():
        one = jnp.ones((16, n), bf)
        for p in range(PAIRS):
            t = v_ref[:, 128 * p : 128 * p + 128].T
            for h in (0, 1):
                vt[2 * p + h, :64, :] = t[64 * h : 64 * h + 64]
                vt[2 * p + h, 64:, :] = one

    aq = aq_ref[...]
    for W in VARIANTS:

        @pl.when(width == W)
        def _():
            at = pl.ds(pl.multiple_of(start * KT, KT), W * KT)
            ak = ak_ref[at, :]
            scores = []
            for p in range(PAIRS):
                c = slice(128 * p, 128 * p + 128)
                q = q_ref[:, c]
                k = k_ref[at, c]
                scores.append(nt(jnp.where(low, k, ak), jnp.where(low, q, aq)))
                scores.append(nt(jnp.where(low, ak, k), jnp.where(low, aq, q)))
            for p in range(PAIRS):
                c = slice(128 * p, 128 * p + 128)
                outs = []
                for h in (0, 1):
                    s = scores[2 * p + h]
                    m = jnp.max(s, axis=0, keepdims=True)
                    e = rnd(jnp.exp(s - m))
                    o = nn(vt[2 * p + h, :, at], e)
                    t = o[64:65]
                    outs.append(o[:64] * (1.0 / t))
                    lb_ref[p, h : h + 1, :] = m + jnp.log(t)
                both = jnp.concatenate(outs, 0)
                mix_ref[:, c] = rnd(both.T)
                mixt_ref[c, :] = rnd(both)


def attend(qkv, aug_q, aug_k, rng):
    n, w3 = qkv.shape
    w = w3 // 3
    L = 128 * PAIRS
    g = w // L
    spec = pltpu.PrefetchScalarGridSpec(
        num_scalar_prefetch=1,
        grid=(g, n // QT),
        in_specs=[
            pl.BlockSpec((QT, L), lambda p, i, r: (i, p)),
            pl.BlockSpec((n, L), lambda p, i, r: (0, g + p)),
            pl.BlockSpec((n, L), lambda p, i, r: (0, 2 * g + p)),
            pl.BlockSpec((QT, 128), lambda p, i, r: (i, 0)),
            pl.BlockSpec((n, 128), lambda p, i, r: (0, 0)),
        ],
        out_specs=[
            pl.BlockSpec((QT, L), lambda p, i, r: (i, p)),
            pl.BlockSpec((L, QT), lambda p, i, r: (p, i)),
            pl.BlockSpec((PAIRS, 8, QT), lambda p, i, r: (p, 0, i)),
        ],
        scratch_shapes=[pltpu.VMEM((2 * PAIRS, 80, n), bf)],
    )
    return pl.pallas_call(
        attend_kernel,
        name="attend",
        grid_spec=spec,
        out_shape=[shaped((n, w), bf), shaped((w, n), bf), shaped((w // 128, 8, n), f32)],
        compiler_params=params(),
        cost_estimate=cost(2.3e10, 1e7),
    )(rng, qkv, qkv, qkv, aug_q, aug_k)


def fill(aug, x):
    lane = lax.broadcasted_iota(jnp.int32, (1, 128), 1) & 63
    a = rnd(x)
    r = x - up(a)
    b = rnd(r)
    c = rnd(r - up(b))
    return jnp.where(lane == 8, a, jnp.where(lane == 9, b, jnp.where(lane == 10, c, aug)))


def attend_back_kernel(
    rng, q_ref, k_ref, v_ref, g_ref, mix_ref, lb_ref, aq_ref, ak_ref,
    dq_ref, dk_ref, dv_ref, dk_acc, dv_acc,
):
    i = pl.program_id(0)
    start = rng[0, i]
    width = rng[1, i]

    @pl.when(i == 0)
    def _():
        dk_acc[...] = jnp.zeros_like(dk_acc)
        dv_acc[...] = jnp.zeros_like(dv_acc)

    low = low_lanes()
    aq0 = aq_ref[...]
    zero = jnp.zeros((1, 128), bf)
    held = []
    for p in range(PAIRS):
        c = slice(128 * p, 128 * p + 128)
        q = q_ref[:, c]
        g = g_ref[:, c]
        prod = up(g) * up(mix_ref[:, c])
        even = jnp.sum(jnp.where(low, prod, 0.0), axis=1, keepdims=True)
        odd = jnp.sum(jnp.where(low, 0.0, prod), axis=1, keepdims=True)
        lt = lb_ref[p].T
        aq = fill(aq0, -jnp.where(low, lt[:, 1:2], lt[:, 0:1]))
        ag = fill(zero, -jnp.where(low, odd, even))
        held.append(
            (
                (jnp.where(low, q, aq), jnp.where(low, aq, q)),
                (jnp.where(low, g, ag), jnp.where(low, ag, g)),
                q.T,
                g.T,
            )
        )
    for W in VARIANTS:

        @pl.when(width == W)
        def _():
            at = pl.ds(pl.multiple_of(start * KT, KT), W * KT)
            ak = ak_ref[at, :]
            for p in range(PAIRS):
                c = slice(128 * p, 128 * p + 128)
                qs, gs, qt, gt = held[p]
                k = k_ref[at, c]
                v = v_ref[at, c]
                one = jnp.ones_like(v)
                ks = (jnp.where(low, k, ak), jnp.where(low, ak, k))
                vs = (jnp.where(low, v, one), jnp.where(low, one, v))
                dqs = []
                for h in (0, 1):
                    e = jnp.exp(nt(qs[h], ks[h]))
                    ds = rnd(e * nt(gs[h], vs[h]))
                    e = rnd(e)
                    half = slice(64 * h, 64 * h + 64)
                    to = slice(128 * p + 64 * h, 128 * p + 64 * h + 64)
                    dqs.append(nn(ds, k))
                    dk_acc[to, at] += nn(qt[half], ds)
                    dv_acc[to, at] += nn(gt[half], e)
                dq_ref[:, c] = jnp.where(low, dqs[0], dqs[1]) * 0.125

    @pl.when(i == pl.num_programs(0) - 1)
    def _():
        dk_ref[...] = dk_acc[...].T
        dv_ref[...] = rnd(dv_acc[...].T)


def attend_back(part, qkv, g_mix, mix, lb, aug_q, aug_k, rng):
    n, w3 = qkv.shape
    L = 128 * PAIRS
    g = w3 // 3 // L
    spec = pltpu.PrefetchScalarGridSpec(
        num_scalar_prefetch=1,
        grid=(n // QT,),
        in_specs=[
            pl.BlockSpec((QT, L), lambda i, r: (i, part)),
            pl.BlockSpec((n, L), lambda i, r: (0, g + part)),
            pl.BlockSpec((n, L), lambda i, r: (0, 2 * g + part)),
            pl.BlockSpec((QT, L), lambda i, r: (i, part)),
            pl.BlockSpec((QT, L), lambda i, r: (i, part)),
            pl.BlockSpec((PAIRS, 8, QT), lambda i, r: (part, 0, i)),
            pl.BlockSpec((QT, 128), lambda i, r: (i, 0)),
            pl.BlockSpec((n, 128), lambda i, r: (0, 0)),
        ],
        out_specs=[
            pl.BlockSpec((QT, L), lambda i, r: (i, 0)),
            pl.BlockSpec((n, L), lambda i, r: (0, 0)),
            pl.BlockSpec((n, L), lambda i, r: (0, 0)),
        ],
        scratch_shapes=[pltpu.VMEM((L, n), f32), pltpu.VMEM((L, n), f32)],
    )
    return pl.pallas_call(
        attend_back_kernel,
        name="attend_back",
        grid_spec=spec,
        out_shape=[shaped((n, L), f32), shaped((n, L), f32), shaped((n, L), bf)],
        compiler_params=params(),
        cost_estimate=cost(2.2e10, 1e7),
    )(rng, qkv, qkv, qkv, g_mix, mix, lb, aug_q, aug_k)


def branch_kernel(tok_ref, mix_ref, w_ref, vec_ref, res_ref, n_ref, nt_ref):
    w = tok_ref.shape[1]
    resid = up(tok_ref[...]) + nn(mix_ref[...], w_ref[...]) + vec_ref[:, 7 * w : 8 * w]
    res_ref[...] = resid
    hat, scale = row_norm(resid)
    normed = hat * vec_ref[:, 2 * w : 3 * w] + vec_ref[:, 3 * w : 4 * w]
    n_ref[...] = rnd(normed)
    nt_ref[...] = rnd(normed.T)


def branch(tokens, mix, weight, vec):
    n, w = tokens.shape
    rows = lambda: pl.BlockSpec((QT, w), lambda i: (i, 0))
    whole = lambda a: pl.BlockSpec(a.shape, lambda i: (0, 0))
    return pl.pallas_call(
        branch_kernel,
        name="branch",
        grid=(n // QT,),
        in_specs=[rows(), rows(), whole(weight), whole(vec)],
        out_specs=[rows(), rows(), pl.BlockSpec((w, QT), lambda i: (0, i))],
        out_shape=[shaped((n, w), f32), shaped((n, w), bf), shaped((w, n), bf)],
        compiler_params=params(),
        cost_estimate=cost(4e9, 1e7),
    )(tokens, mix, weight, vec)


def gelu_parts(x):
    z = jnp.abs(x)
    e = jnp.exp(x * x * -0.5)
    t = 1.0 / (1.0 + (0.3275911 * 0.7071067811865476) * z)
    poly = t * (
        0.5 * 0.254829592
        + t
        * (
            0.5 * -0.284496736
            + t * (0.5 * 1.421413741 + t * (0.5 * -1.453152027 + t * (0.5 * 1.061405429)))
        )
    )
    tail = poly * e
    cdf = jnp.where(x < 0.0, tail, 1.0 - tail)
    return x * cdf, cdf + x * (e * 0.3989422804014327)


def hidden_kernel(n_ref, w_ref, b_ref, a_ref, at_ref, d_ref):
    x = nn(n_ref[...], w_ref[...]) + b_ref[...]
    active, slope = gelu_parts(x)
    active = rnd(active)
    a_ref[...] = active
    at_ref[...] = active.T
    d_ref[...] = rnd(slope)


def hidden_units(normed, weight, vec):
    n, w = normed.shape
    ff = weight.shape[1]
    B = 256
    off = 8 * w // B
    return pl.pallas_call(
        hidden_kernel,
        name="hidden",
        grid=(ff // B,),
        in_specs=[
            pl.BlockSpec((n, w), lambda j: (0, 0)),
            pl.BlockSpec((w, B), lambda j: (0, j)),
            pl.BlockSpec((1, B), lambda j: (0, off + j)),
        ],
        out_specs=[
            pl.BlockSpec((n, B), lambda j: (0, j)),
            pl.BlockSpec((B, n), lambda j: (j, 0)),
            pl.BlockSpec((n, B), lambda j: (0, j)),
        ],
        out_shape=[shaped((n, ff), bf), shaped((ff, n), bf), shaped((n, ff), bf)],
        compiler_params=params(),
        cost_estimate=cost(1.5e10, 1e7),
    )(normed, weight, vec)


def last_kernel(a_ref, w_ref, res_ref, b_ref, o_ref):
    o_ref[...] = rnd(res_ref[...] + nn(a_ref[...], w_ref[...]) + b_ref[...])


def last(active, weight, resid, vec):
    n, ff = active.shape
    w = resid.shape[1]
    off = (8 * w + ff) // w
    return pl.pallas_call(
        last_kernel,
        name="last",
        grid=(n // QT,),
        in_specs=[
            pl.BlockSpec((QT, ff), lambda i: (i, 0)),
            pl.BlockSpec((ff, w), lambda i: (0, 0)),
            pl.BlockSpec((QT, w), lambda i: (i, 0)),
            pl.BlockSpec((1, w), lambda i: (0, off)),
        ],
        out_specs=pl.BlockSpec((QT, w), lambda i: (i, 0)),
        out_shape=shaped((n, w), bf),
        compiler_params=params(),
        cost_estimate=cost(6e9, 1e7),
    )(active, weight, resid, vec)


def hidden_back_kernel(g_ref, w_ref, d_ref, gh_ref, sum_ref):
    gh = rnd(nt(g_ref[...], w_ref[...]) * up(d_ref[...]))
    gh_ref[...] = gh
    sum_ref[...] = jnp.sum(up(gh), axis=0, keepdims=True)


def hidden_back(given, weight, slope):
    n, w = given.shape
    ff = weight.shape[0]
    B = 512
    return pl.pallas_call(
        hidden_back_kernel,
        name="hidden_back",
        grid=(ff // B,),
        in_specs=[
            pl.BlockSpec((n, w), lambda j: (0, 0)),
            pl.BlockSpec((B, w), lambda j: (j, 0)),
            pl.BlockSpec((n, B), lambda j: (0, j)),
        ],
        out_specs=[pl.BlockSpec((n, B), lambda j: (0, j)), pl.BlockSpec((1, B), lambda j: (0, j))],
        out_shape=[shaped((n, ff), bf), shaped((1, ff), f32)],
        compiler_params=params(),
        cost_estimate=cost(8e9, 1e7),
    )(given, weight, slope)


def norm_back(grad, hat, scale, gain):
    d = grad * gain
    a = jnp.mean(d, axis=-1, keepdims=True)
    b = jnp.mean(d * hat, axis=-1, keepdims=True)
    return (d - a - hat * b) * scale


def second_back_kernel(gh_ref, w_ref, res_ref, cot_ref, vec_ref, wo_ref, gr_ref, gb_ref, gm_ref, sum_ref):
    i = pl.program_id(0)
    w = res_ref.shape[1]
    grad = nt(gh_ref[...], w_ref[...])
    hat, scale = row_norm(res_ref[...])
    total = up(cot_ref[...]) + norm_back(grad, hat, scale, vec_ref[:, 2 * w : 3 * w])
    gr_ref[...] = total
    low = rnd(total)
    gb_ref[...] = low
    gm_ref[...] = rnd(nt(low, wo_ref[...]))
    sums = jnp.concatenate(
        [
            jnp.sum(grad * hat, axis=0, keepdims=True),
            jnp.sum(grad, axis=0, keepdims=True),
            jnp.sum(up(low), axis=0, keepdims=True),
        ],
        axis=0,
    )

    @pl.when(i == 0)
    def _():
        sum_ref[...] = jnp.zeros_like(sum_ref)

    sum_ref[0:3, :] += sums


def second_back(gh, weight, resid, given, vec, out_w):
    n, ff = gh.shape
    w = resid.shape[1]
    rows = lambda c: pl.BlockSpec((QT, c), lambda i: (i, 0))
    whole = lambda a: pl.BlockSpec(a.shape, lambda i: (0, 0))
    return pl.pallas_call(
        second_back_kernel,
        name="second_back",
        grid=(n // QT,),
        in_specs=[rows(ff), whole(weight), rows(w), rows(w), whole(vec), whole(out_w)],
        out_specs=[rows(w), rows(w), rows(w), pl.BlockSpec((8, w), lambda i: (0, 0))],
        out_shape=[shaped((n, w), f32), shaped((n, w), bf), shaped((n, w), bf), shaped((8, w), f32)],
        compiler_params=params(),
        cost_estimate=cost(9e9, 1e7),
    )(gh, weight, resid, given, vec, out_w)


def outer_kernel(sel, x_ref, y_ref, o_ref):
    z, one, r, n = x_ref.shape
    got = nn(x_ref[...].reshape(z * r, n), y_ref[...])
    o_ref[...] = rnd(got).reshape(o_ref.shape)


def outer(x_t, y, sel, groups, share):
    rows, n = x_t.shape
    c = y.shape[1]
    r = rows // (groups * share)
    B = 256 if rows > 2 * c else 512 if c % 512 == 0 else 384 if c % 384 == 0 else 256
    spec = pltpu.PrefetchScalarGridSpec(
        num_scalar_prefetch=1,
        grid=(c // B,),
        in_specs=[
            pl.BlockSpec((groups, 1, r, n), lambda j, s: (0, s[0], 0, 0)),
            pl.BlockSpec((n, B), lambda j, s: (0, j)),
        ],
        out_specs=pl.BlockSpec((groups, r, B), lambda j, s: (0, 0, j)),
    )
    return pl.pallas_call(
        outer_kernel,
        name="outer",
        grid_spec=spec,
        out_shape=shaped((groups, r, c), bf),
        compiler_params=params(),
        cost_estimate=cost(4 * groups * r * c * n, 1e7),
    )(sel, x_t.reshape(groups, share, r, n), y)


def turn_back_kernel(
    dq_ref, dk_ref, dv_ref, q_ref, k_ref, cos_ref, sin_ref, grid_ref, gp_ref, b_ref, f_ref
):
    i = pl.program_id(0)
    w = cos_ref.shape[1]
    cos = cos_ref[...]
    sin = sin_ref[...]
    dq = dq_ref[...]
    dk = dk_ref[...]
    gv = dv_ref[...]
    sq = swap(dq)
    sk = swap(dk)
    t = sq * (up(q_ref[...]) * 8.0) + sk * up(k_ref[...])
    g = grid_ref[...]
    gq = rnd(dq * cos - sq * sin)
    gk = rnd(dk * cos - sk * sin)
    gp_ref[:, :w] = gq
    gp_ref[:, w : 2 * w] = gk
    gp_ref[:, 2 * w :] = gv
    add = lambda v: jnp.sum(v, axis=0, keepdims=True)

    @pl.when(i == 0)
    def _():
        b_ref[...] = jnp.zeros_like(b_ref)
        f_ref[...] = jnp.zeros_like(f_ref)

    b_ref[0:3, :] += jnp.concatenate([add(up(gq)), add(up(gk)), add(up(gv))], axis=0)
    f_ref[0:2, :] += jnp.concatenate([add(t * g[:, 0:1]), add(t * g[:, 1:2])], axis=0)


def turn_back(part, dq, dk, dv, qkv, cos, sin, grid_t):
    n, L = dq.shape
    g = qkv.shape[1] // 3 // L
    rows = lambda c, j=0: pl.BlockSpec((QT, c), lambda i: (i, j))
    fixed = lambda: pl.BlockSpec((8, L), lambda i: (0, 0))
    return pl.pallas_call(
        turn_back_kernel,
        name="turn_back",
        grid=(n // QT,),
        in_specs=[rows(L), rows(L), rows(L), rows(L, part), rows(L, g + part)]
        + [rows(L, part), rows(L, part), pl.BlockSpec((QT, 2), lambda i: (i, 0))],
        out_specs=[rows(3 * L), fixed(), fixed()],
        out_shape=[shaped((n, 3 * L), bf), shaped((8, L), f32), shaped((8, L), f32)],
        compiler_params=params(),
        cost_estimate=cost(4e9, 1e7),
    )(dq, dk, dv, qkv, qkv, cos, sin, grid_t)


def first_back_kernel(*refs):
    gp_refs = refs[:-6]
    w_ref, tok_ref, gr_ref, vec_ref, o_ref, sum_ref = refs[-6:]
    i = pl.program_id(0)
    w = tok_ref.shape[1]
    L = w // len(gp_refs)
    gp = [r[:, s * L : (s + 1) * L] for s in range(3) for r in gp_refs]
    grad = nt(jnp.concatenate(gp, axis=1), w_ref[...])
    hat, scale = row_norm(up(tok_ref[...]))
    o_ref[...] = rnd(gr_ref[...] + norm_back(grad, hat, scale, vec_ref[:, :w]))
    sums = jnp.concatenate(
        [jnp.sum(grad * hat, axis=0, keepdims=True), jnp.sum(grad, axis=0, keepdims=True)], axis=0
    )

    @pl.when(i == 0)
    def _():
        sum_ref[...] = jnp.zeros_like(sum_ref)

    sum_ref[0:2, :] += sums


def first_back(gps, weight, tokens, grad_resid, vec):
    n, w = tokens.shape
    rows = lambda c: pl.BlockSpec((QT, c), lambda i: (i, 0))
    whole = lambda a: pl.BlockSpec(a.shape, lambda i: (0, 0))
    return pl.pallas_call(
        first_back_kernel,
        name="first_back",
        grid=(n // QT,),
        in_specs=[rows(g.shape[1]) for g in gps] + [whole(weight), rows(w), rows(w), whole(vec)],
        out_specs=[rows(w), pl.BlockSpec((8, w), lambda i: (0, 0))],
        out_shape=[shaped((n, w), bf), shaped((8, w), f32)],
        compiler_params=params(),
        cost_estimate=cost(7e9, 1e7),
    )(*gps, weight, tokens, grad_resid, vec)


def over_dp(v, k):
    return lax.ppermute(v, "dp", [(i, i ^ k) for i in range(4)])


def over_core(v):
    return lax.ppermute(v, "fsdp", [(i, i ^ 1) for i in range(8)])


def over_z(v, k):
    return lax.ppermute(v, "fsdp", [(i, i ^ (2 * k)) for i in range(8)])


def along_z(v, s):
    return lax.ppermute(v, "fsdp", [(i, (i + 2 * s) % 8) for i in range(8)])


def tie(*values):
    return lax.optimization_barrier(values)


def place():
    d = lax.axis_index("dp")
    f = lax.axis_index("fsdp")
    return d, f // 2, f % 2


def quarter(shard):
    d, z, c = place()
    r, cols = shard.shape
    return lax.dynamic_slice(shard, (d * (r // 4), 0), (r // 4, cols))


def spread_z(part):
    return jnp.stack([part] + [along_z(part, s) for s in (1, 2, 3)])


def spread_dp(column):
    return [column] + [over_dp(column, k) for k in (1, 2, 3)]


def arrange_kernel(at, *refs):
    out = refs[-1]
    for side in (0, 1):
        for k in range(4):
            for s in range(4):
                to = ((lax.rem(at[1] + 4 - s, 4) * 2 + lax.bitwise_xor(at[2], side)) * 4) + lax.bitwise_xor(at[0], k)
                out[to] = refs[side * 4 + k][s]


def arrange(own, other):
    d, z, c = place()
    at = jnp.stack([d, z, c]).astype(jnp.int32)
    r, cols = own[0].shape[1:]
    B = cols // 3
    spec = pltpu.PrefetchScalarGridSpec(
        num_scalar_prefetch=1,
        grid=(3,),
        in_specs=[pl.BlockSpec((4, r, B), lambda j, a: (0, 0, j))] * 8,
        out_specs=pl.BlockSpec((32, r, B), lambda j, a: (0, 0, j)),
    )
    out = pl.pallas_call(
        arrange_kernel,
        name="arrange",
        grid_spec=spec,
        out_shape=shaped((32, r, cols), bf),
        compiler_params=params(),
        cost_estimate=cost(1e6, 4 * 32 * r * cols),
    )(at, *own, *other)
    return out.reshape(32 * r, cols)


def at_index(v, axis, k):
    return lax.dynamic_index_in_dim(v, k, axis, keepdims=False)


def fold_core(mine, other):
    d, z, c = place()
    groups, r, cols = mine.shape
    both = rnd(up(mine) + up(other)).reshape(groups, 4, r // 4, cols)
    return [at_index(both, 1, lax.bitwise_xor(d, k)) for k in range(4)]


def fold_dp(pieces):
    own, got = pieces
    d, z, c = place()
    total = up(own)
    for g in got:
        total = total + up(g)
    total = rnd(total)
    return [at_index(total, 0, lax.rem(z + s, 4)) for s in range(4)]


def fold_z(own, got):
    total = up(own)
    for g in got:
        total = total + up(g)
    return rnd(total)


def share(own, got):
    d, z, c = place()
    all_of = [own] + got
    rows = []
    for j in range(4):
        rel = lax.bitwise_xor(d, j)
        v = all_of[3]
        for k in (2, 1, 0):
            v = jnp.where(rel == k, all_of[k], v)
        rows.append(v)
    return up(jnp.concatenate(rows, 0))


def doubled(v, other, bit):
    return jnp.concatenate([jnp.where(bit == 0, v, other), jnp.where(bit == 0, other, v)], 0)


def gather_vector(shard):
    d, z, c = place()
    v = shard.reshape(1, -1)
    v = doubled(v, over_core(v), c)
    v = doubled(v, over_z(v, 1), z % 2)
    v = doubled(v, over_z(v, 2), z // 2)
    return v.reshape(-1)


def sum_dp(v):
    v = v + over_dp(v, 1)
    return v + over_dp(v, 2)


def sum_fsdp(v):
    v = v + over_core(v)
    v = v + over_z(v, 1)
    return v + over_z(v, 2)


def sum_dp_low(v):
    v = rnd(up(v) + up(over_dp(v, 1)))
    return rnd(up(v) + up(over_dp(v, 2)))


def adam_terms(grad, first, second, master, decay):
    first_new = 0.9 * first + 0.1 * grad
    second_new = 0.999 * second + 0.001 * grad * grad
    first_hat = first_new / (1.0 - 0.9**STEP)
    second_hat = second_new / (1.0 - 0.999**STEP)
    update = first_hat / (jnp.sqrt(second_hat) + 1e-06) + decay * master
    return (first_new, second_new, update)


def body(fast, tokens, cotangent, image_ids, patch_grid, *state):
    masters, vectors = state[:4], state[4]
    firsts, vector_first = state[5:9], state[9]
    seconds, vector_second = state[10:14], state[14]
    n, w = tokens.shape
    heads = w // HD
    count = w // 128 // PAIRS
    low = [rnd(m) for m in masters]
    gather = lambda v: lax.all_gather(v, "fsdp", axis=0, tiled=True)
    scatter = lambda v: lax.psum_scatter(v, "fsdp", scatter_dimension=0, tiled=True)
    whole = jnp.zeros((1,), jnp.int32)
    d, z, c = place()
    mine = jnp.stack([c]).astype(jnp.int32)

    if fast:
        qkv_column = spread_z(quarter(low[0]))
        packed = gather_vector(rnd(vectors))
        full_out = gather(low[1])
        up_part, _ = tie(quarter(low[2]), qkv_column)
        up_column = spread_z(up_part)
        down_part, _ = tie(low[3], full_out)
        full_down = gather(down_part)
        qkv_own = spread_dp(qkv_column)
    else:
        packed = gather(rnd(vectors))
        full_qkv, full_out, full_up, full_down = [gather(v) for v in low]
    vec = up(packed).reshape(1, -1)
    freq = vec[0, -w:].reshape(2, heads, 1, HD // 2)
    freq = jnp.broadcast_to(freq, (2, heads, 2, HD // 2)).reshape(2, w)
    grid_t = up(patch_grid.T)
    given = jnp.where((image_ids >= 0)[:, None], cotangent, jnp.zeros_like(cotangent))
    grad_bias_down = jnp.sum(up(given), axis=0)
    weight_local = jnp.stack([jnp.sum(m * m) for m in masters])
    aug_q, aug_k, rng = tables(image_ids)

    normed, normed_t, cos, sin = first(tokens, vec, freq, grid_t)
    if fast:
        normed, *qkv_own = tie(normed, *qkv_own)
        qkv_other = [over_core(v) for v in qkv_own]
        full_qkv = arrange(qkv_own, qkv_other)
        up_column, full_qkv = tie(up_column, full_qkv)
        up_own = spread_dp(up_column)
    qkv = project(normed, full_qkv, vec, cos, sin)
    mix, mix_t, lb = attend(qkv, aug_q, aug_k, rng)
    if fast:
        mix, *up_own = tie(mix, *up_own)
        up_other = [over_core(v) for v in up_own]
    resid, normed_two, normed_two_t = branch(tokens, mix, full_out, vec)
    if fast:
        full_up = arrange(up_own, up_other)
        normed_two, full_down = tie(normed_two, full_down)
    active, active_t, slope = hidden_units(normed_two, full_up, vec)
    if fast:
        theirs = outer(active_t, given, 1 - mine, 4, 2)
        down_sent = over_core(theirs)
        down_mine = outer(active_t, given, mine, 4, 2)
        down_pieces = fold_core(down_mine, down_sent)
        active, slope, *down_pieces = tie(active, slope, *down_pieces)
        down_got = [over_dp(v, k) for k, v in zip((1, 2, 3), down_pieces[1:])]
    else:
        down_full = outer(active_t, given, whole, 1, 1)[0]
    output = last(active, full_down, resid, vec)
    grad_hidden, grad_bias_up = hidden_back(given, full_down, slope)
    if fast:
        output, grad_hidden, *down_got = tie(output, grad_hidden, *down_got)
        down_z = fold_dp((down_pieces[0], down_got))
        grad_hidden, *down_z = tie(grad_hidden, *down_z)
        down_zgot = [along_z(v, s) for s, v in zip((1, 2, 3), down_z[1:])]
        theirs = outer(normed_two_t, grad_hidden, 1 - mine, 4, 2)
        up_sent = over_core(theirs)
        up_mine = outer(normed_two_t, grad_hidden, mine, 4, 2)
        up_pieces = fold_core(up_mine, up_sent)
        up_mine, *down_zgot = tie(up_mine, *down_zgot)
        down_f = fold_z(down_z[0], down_zgot)
        grad_hidden, down_f, *up_pieces = tie(grad_hidden, down_f, *up_pieces)
        down_quarters = [over_dp(down_f, k) for k in (1, 2, 3)]
        up_got = [over_dp(v, k) for k, v in zip((1, 2, 3), up_pieces[1:])]
    else:
        up_full = outer(normed_two_t, grad_hidden, whole, 1, 1)[0]
    grad_resid, grad_branch, grad_mix, sums_two = second_back(
        grad_hidden, full_up, resid, given, vec, full_out
    )
    out_full = outer(mix_t, grad_branch, whole, 1, 1)[0]
    if fast:
        out_rows = scatter(out_full)
        grad_mix, down_f, *down_quarters = tie(grad_mix, down_f, *down_quarters)
        down_grad = share(down_f, down_quarters)
    projs = []
    sums_proj = []
    sums_freq = []
    qkv_parts = []
    chains = []
    for part in range(count):
        dq, dk, dv = attend_back(part, qkv, grad_mix, mix, lb, aug_q, aug_k, rng)
        if fast and part == 0:
            dq, *up_got = tie(dq, *up_got)
            up_z = fold_dp((up_pieces[0], up_got))
            dq, *up_z = tie(dq, *up_z)
            up_zgot = [along_z(v, s) for s, v in zip((1, 2, 3), up_z[1:])]
        gp, bs, fs = turn_back(part, dq, dk, dv, qkv, cos, sin, grid_t)
        projs.append(gp)
        sums_proj.append(bs)
        sums_freq.append(fs)
        if not fast:
            qkv_parts.append(outer(normed_t, gp, whole, 1, 1)[0])
            continue
        theirs = outer(normed_t, gp, 1 - mine, 4, 2)
        sent = over_core(theirs)
        own = outer(normed_t, gp, mine, 4, 2)
        pieces = fold_core(own, sent)
        if part < count - 1:
            own, *up_zgot = tie(own, *up_zgot)
            up_f = fold_z(up_z[0], up_zgot)
            grad_mix, up_f, *pieces = tie(grad_mix, up_f, *pieces)
            up_quarters = [over_dp(up_f, k) for k in (1, 2, 3)]
            got = [over_dp(v, k) for k, v in zip((1, 2, 3), pieces[1:])]
            chains.append((pieces, got))
        else:
            theirs, up_f, out_rows, *up_quarters = tie(theirs, up_f, out_rows, *up_quarters)
            projs[-1], *pieces = tie(projs[-1], *pieces)
            got = [over_dp(v, k) for k, v in zip((1, 2, 3), pieces[1:])]
            chains.append((pieces, got))
    tokens_grad, sums_one = first_back(projs, full_qkv, tokens, grad_resid, vec)
    join = lambda rows: jnp.concatenate(rows, axis=-1)
    freq_sums = join([s[:2] for s in sums_freq]).reshape(2, heads, 2, HD // 2)
    vector_full = jnp.concatenate(
        [
            sums_one[0],
            sums_one[1],
            sums_two[0],
            sums_two[1],
            join([s[:3] for s in sums_proj]).reshape(-1),
            sums_two[2],
            grad_bias_up.reshape(-1),
            grad_bias_down,
            (freq_sums[:, :, 0] - freq_sums[:, :, 1]).reshape(-1),
        ]
    )
    size = vectors.shape[0]
    if fast:
        up_grad = share(up_f, up_quarters)
        out_grad = up(sum_dp_low(out_rows))
        done = []
        for pieces, got in chains:
            zs = fold_dp((pieces[0], got))
            f = fold_z(zs[0], [along_z(v, s) for s, v in zip((1, 2, 3), zs[1:])])
            done.append(share(f, [over_dp(f, k) for k in (1, 2, 3)]))
        both = jnp.concatenate([vector_full, weight_local * 0.25]).reshape(1, -1)
        both = sum_fsdp(sum_dp(both)).reshape(-1)
        vector_total, weight_squares = both[:-4], both[-4:]
        vector_grad = lax.dynamic_slice(vector_total, (lax.axis_index("fsdp") * size,), (size,))
        off = vector_total.shape[0] - 2 * w
        down_bias_grad = vector_total[off : off + w]
        total = lambda v: sum_fsdp(v.reshape(1, -1)).reshape(-1)
    else:
        give = lambda v: lax.psum(scatter(up(v)), "dp")
        up_grad, down_grad, out_grad = give(up_full), give(down_full), give(out_full)
        done = [give(v) for v in qkv_parts]
        vector_grad = give(vector_full)
        down_bias_grad = lax.psum(grad_bias_down, ("dp", "fsdp"))
        total = lambda v: lax.psum(v, "fsdp")
        weight_squares = total(weight_local)
    L = 128 * PAIRS
    qkv_grad = join([g[:, s * L : (s + 1) * L] for s in range(3) for g in done])
    weight_norms = jnp.sqrt(weight_squares)
    reduced = (qkv_grad, out_grad, up_grad, down_grad)
    steps = [
        adam_terms(reduced[k], firsts[k], seconds[k], masters[k], 0.01) for k in range(4)
    ]
    update_norms = jnp.sqrt(total(jnp.stack([jnp.sum(s[2] * s[2]) for s in steps])))
    new_list = [
        masters[k] - 0.3 * (weight_norms[k] / (update_norms[k] + 1e-06)) * steps[k][2]
        for k in range(4)
    ]
    vector_step = adam_terms(vector_grad, vector_first, vector_second, vectors, 0.0)
    return (
        output,
        tokens_grad,
        *reduced,
        vector_grad,
        down_bias_grad,
        *[s[0] for s in steps],
        vector_step[0],
        *[s[1] for s in steps],
        vector_step[1],
        *new_list,
        vectors - 0.2 * vector_step[2],
        weight_norms,
        update_norms,
    )


def solution(mesh):
    both = P(("dp", "fsdp"), None)
    mat = [P("fsdp", None)] * 4 + [P("fsdp")]
    in_specs = (both, both, P(("dp", "fsdp")), P(None, ("dp", "fsdp")), *mat, *mat, *mat)
    out_specs = (both, both, *mat, P(), *mat, *mat, *mat, P(), P())
    fast = mesh.shape["dp"] == 4 and mesh.shape["fsdp"] == 8
    return jax.shard_map(
        partial(body, fast), mesh=mesh, in_specs=in_specs, out_specs=out_specs, check_vma=False
    )
```

```python
from functools import partial

import jax
import jax.numpy as jnp
from jax import lax
from jax.experimental import pallas as pl
from jax.experimental.pallas import tpu as pltpu
from jax.sharding import PartitionSpec as P

H = 12
HD = 64
STEP = 10
QT = 256
KT = 128
PAIRS = 3
VARIANTS = (2, 3, 4, 5, 7, 8)
norm_eps = 1e-06
bf = jnp.bfloat16
f32 = jnp.float32


def nt(a, b):
    return lax.dot_general(a, b, (((1,), (1,)), ((), ())), preferred_element_type=f32)


def nn(a, b):
    return lax.dot_general(a, b, (((1,), (0,)), ((), ())), preferred_element_type=f32)


def rnd(v):
    return v.astype(bf)


def up(v):
    return v.astype(f32)


def params(mib=22):
    return pltpu.CompilerParams(vmem_limit_bytes=mib << 20)


def cost(flops, moved):
    return pl.CostEstimate(flops=int(flops), bytes_accessed=int(moved), transcendentals=0)


def shaped(shape, kind):
    return jax.ShapeDtypeStruct(shape, kind)


def row_norm(v):
    centre = jnp.mean(v, axis=-1, keepdims=True)
    centred = v - centre
    spread = jnp.mean(centred * centred, axis=-1, keepdims=True)
    scale = lax.rsqrt(spread + norm_eps)
    return centred * scale, scale


def first_kernel(tok_ref, vec_ref, freq_ref, grid_ref, n_ref, nt_ref, cos_ref, sin_ref):
    w = tok_ref.shape[1]
    hat, scale = row_norm(up(tok_ref[...]))
    normed = hat * vec_ref[:, :w] + vec_ref[:, w : 2 * w]
    n_ref[...] = rnd(normed)
    nt_ref[...] = rnd(normed.T)
    g = grid_ref[...]
    angle = g[:, 0:1] * freq_ref[0:1, :] + g[:, 1:2] * freq_ref[1:2, :]
    lane = lax.broadcasted_iota(jnp.int32, (1, w), 1)
    cos_ref[...] = jnp.cos(angle)
    s = jnp.sin(angle)
    sin_ref[...] = jnp.where(lane & 63 < 32, -s, s)


def first(tokens, vec, freq, grid_t):
    n, w = tokens.shape
    rows = lambda: pl.BlockSpec((QT, w), lambda i: (i, 0))
    whole = lambda a: pl.BlockSpec(a.shape, lambda i: (0, 0))
    return pl.pallas_call(
        first_kernel,
        name="first",
        grid=(n // QT,),
        in_specs=[rows(), whole(vec), whole(freq), pl.BlockSpec((QT, 2), lambda i: (i, 0))],
        out_specs=[rows(), pl.BlockSpec((w, QT), lambda i: (0, i)), rows(), rows()],
        out_shape=[shaped((n, w), bf), shaped((w, n), bf), shaped((n, w), f32), shaped((n, w), f32)],
        compiler_params=params(),
        cost_estimate=cost(1e10, 1e7),
    )(tokens, vec, freq, grid_t)


def swap(v):
    w = v.shape[1]
    lane = lax.broadcasted_iota(jnp.int32, (1, w), 1)
    return jnp.where(lane & 63 < 32, pltpu.roll(v, w - 32, 1), pltpu.roll(v, 32, 1))


def project_kernel(n_ref, w_ref, b_ref, cos_ref, sin_ref, o_ref):
    j = pl.program_id(0)
    u = nn(n_ref[...], w_ref[...]) + b_ref[...]

    @pl.when(j < 2)
    def _():
        turned = u * cos_ref[...] + swap(u) * sin_ref[...]
        o_ref[...] = rnd(turned * jnp.where(j < 1, 0.125, 1.0))

    @pl.when(j >= 2)
    def _():
        o_ref[...] = rnd(u)


def project(normed, weight, vec, cos, sin):
    n, w = normed.shape
    whole = lambda: pl.BlockSpec((n, w), lambda j: (0, 0))
    return pl.pallas_call(
        project_kernel,
        name="project",
        grid=(3,),
        in_specs=[
            whole(),
            pl.BlockSpec((w, w), lambda j: (0, j)),
            pl.BlockSpec((1, w), lambda j: (0, 4 + j)),
            whole(),
            whole(),
        ],
        out_specs=pl.BlockSpec((n, w), lambda j: (0, j)),
        out_shape=shaped((n, 3 * w), bf),
        compiler_params=params(40),
        cost_estimate=cost(8e9, 1e7),
    )(normed, weight, vec, cos, sin)


def tables(ids):
    n = ids.shape[0]
    lane = jnp.arange(128) & 63
    one = (ids[:, None] + 1 == lane[None]).astype(f32)
    small = (lane < 8)[None]
    aug_q = rnd(jnp.where(small, one, 0.0))
    aug_k = rnd(jnp.where(small, (one - 1.0) * 1e30, jnp.where((lane < 11)[None], 1.0, 0.0)))
    tiles = n // QT
    hit = (ids.reshape(tiles, QT, 1) == ids[None, None, :]).any(1)
    pos = jnp.arange(n)[None]
    lo = jnp.min(jnp.where(hit, pos, n), 1) // KT
    hi = jnp.max(jnp.where(hit, pos, -1), 1) // KT + 1
    need = hi - lo
    width = jnp.full_like(need, VARIANTS[-1])
    for v in VARIANTS[::-1]:
        width = jnp.where(need <= v, v, width)
    start = jnp.minimum(lo, n // KT - width)
    return aug_q, aug_k, jnp.stack([start, width]).astype(jnp.int32)


def low_lanes():
    return lax.broadcasted_iota(jnp.int32, (1, 128), 1) < 64


def attend_kernel(rng, q_ref, k_ref, v_ref, aq_ref, ak_ref, mix_ref, mixt_ref, lb_ref, vt):
    i = pl.program_id(1)
    n = k_ref.shape[0]
    start = rng[0, i]
    width = rng[1, i]
    low = low_lanes()

    @pl.when(i == 0)
    def _():
        one = jnp.ones((16, n), bf)
        for p in range(PAIRS):
            t = v_ref[:, 128 * p : 128 * p + 128].T
            for h in (0, 1):
                vt[2 * p + h, :64, :] = t[64 * h : 64 * h + 64]
                vt[2 * p + h, 64:, :] = one

    aq = aq_ref[...]
    for W in VARIANTS:

        @pl.when(width == W)
        def _():
            at = pl.ds(pl.multiple_of(start * KT, KT), W * KT)
            ak = ak_ref[at, :]
            scores = []
            for p in range(PAIRS):
                c = slice(128 * p, 128 * p + 128)
                q = q_ref[:, c]
                k = k_ref[at, c]
                scores.append(nt(jnp.where(low, k, ak), jnp.where(low, q, aq)))
                scores.append(nt(jnp.where(low, ak, k), jnp.where(low, aq, q)))
            for p in range(PAIRS):
                c = slice(128 * p, 128 * p + 128)
                outs = []
                for h in (0, 1):
                    s = scores[2 * p + h]
                    m = jnp.max(s, axis=0, keepdims=True)
                    e = rnd(jnp.exp(s - m))
                    o = nn(vt[2 * p + h, :, at], e)
                    t = o[64:65]
                    outs.append(o[:64] * (1.0 / t))
                    lb_ref[p, h : h + 1, :] = m + jnp.log(t)
                both = jnp.concatenate(outs, 0)
                mix_ref[:, c] = rnd(both.T)
                mixt_ref[c, :] = rnd(both)


def attend(qkv, aug_q, aug_k, rng):
    n, w3 = qkv.shape
    w = w3 // 3
    L = 128 * PAIRS
    g = w // L
    spec = pltpu.PrefetchScalarGridSpec(
        num_scalar_prefetch=1,
        grid=(g, n // QT),
        in_specs=[
            pl.BlockSpec((QT, L), lambda p, i, r: (i, p)),
            pl.BlockSpec((n, L), lambda p, i, r: (0, g + p)),
            pl.BlockSpec((n, L), lambda p, i, r: (0, 2 * g + p)),
            pl.BlockSpec((QT, 128), lambda p, i, r: (i, 0)),
            pl.BlockSpec((n, 128), lambda p, i, r: (0, 0)),
        ],
        out_specs=[
            pl.BlockSpec((QT, L), lambda p, i, r: (i, p)),
            pl.BlockSpec((L, QT), lambda p, i, r: (p, i)),
            pl.BlockSpec((PAIRS, 8, QT), lambda p, i, r: (p, 0, i)),
        ],
        scratch_shapes=[pltpu.VMEM((2 * PAIRS, 80, n), bf)],
    )
    return pl.pallas_call(
        attend_kernel,
        name="attend",
        grid_spec=spec,
        out_shape=[shaped((n, w), bf), shaped((w, n), bf), shaped((w // 128, 8, n), f32)],
        compiler_params=params(),
        cost_estimate=cost(2.3e10, 1e7),
    )(rng, qkv, qkv, qkv, aug_q, aug_k)


def fill(aug, x):
    lane = lax.broadcasted_iota(jnp.int32, (1, 128), 1) & 63
    a = rnd(x)
    r = x - up(a)
    b = rnd(r)
    c = rnd(r - up(b))
    return jnp.where(lane == 8, a, jnp.where(lane == 9, b, jnp.where(lane == 10, c, aug)))


def attend_back_kernel(
    rng, q_ref, k_ref, v_ref, g_ref, mix_ref, lb_ref, aq_ref, ak_ref,
    dq_ref, dk_ref, dv_ref, dk_acc, dv_acc,
):
    i = pl.program_id(0)
    start = rng[0, i]
    width = rng[1, i]

    @pl.when(i == 0)
    def _():
        dk_acc[...] = jnp.zeros_like(dk_acc)
        dv_acc[...] = jnp.zeros_like(dv_acc)

    low = low_lanes()
    aq0 = aq_ref[...]
    zero = jnp.zeros((1, 128), bf)
    held = []
    for p in range(PAIRS):
        c = slice(128 * p, 128 * p + 128)
        q = q_ref[:, c]
        g = g_ref[:, c]
        prod = up(g) * up(mix_ref[:, c])
        even = jnp.sum(jnp.where(low, prod, 0.0), axis=1, keepdims=True)
        odd = jnp.sum(jnp.where(low, 0.0, prod), axis=1, keepdims=True)
        lt = lb_ref[p].T
        aq = fill(aq0, -jnp.where(low, lt[:, 1:2], lt[:, 0:1]))
        ag = fill(zero, -jnp.where(low, odd, even))
        held.append(
            (
                (jnp.where(low, q, aq), jnp.where(low, aq, q)),
                (jnp.where(low, g, ag), jnp.where(low, ag, g)),
                q.T,
                g.T,
            )
        )
    for W in VARIANTS:

        @pl.when(width == W)
        def _():
            at = pl.ds(pl.multiple_of(start * KT, KT), W * KT)
            ak = ak_ref[at, :]
            for p in range(PAIRS):
                c = slice(128 * p, 128 * p + 128)
                qs, gs, qt, gt = held[p]
                k = k_ref[at, c]
                v = v_ref[at, c]
                one = jnp.ones_like(v)
                ks = (jnp.where(low, k, ak), jnp.where(low, ak, k))
                vs = (jnp.where(low, v, one), jnp.where(low, one, v))
                dqs = []
                for h in (0, 1):
                    e = jnp.exp(nt(qs[h], ks[h]))
                    ds = rnd(e * nt(gs[h], vs[h]))
                    e = rnd(e)
                    half = slice(64 * h, 64 * h + 64)
                    to = slice(128 * p + 64 * h, 128 * p + 64 * h + 64)
                    dqs.append(nn(ds, k))
                    dk_acc[to, at] += nn(qt[half], ds)
                    dv_acc[to, at] += nn(gt[half], e)
                dq_ref[:, c] = jnp.where(low, dqs[0], dqs[1]) * 0.125

    @pl.when(i == pl.num_programs(0) - 1)
    def _():
        dk_ref[...] = dk_acc[...].T
        dv_ref[...] = rnd(dv_acc[...].T)


def attend_back(part, qkv, g_mix, mix, lb, aug_q, aug_k, rng):
    n, w3 = qkv.shape
    L = 128 * PAIRS
    g = w3 // 3 // L
    spec = pltpu.PrefetchScalarGridSpec(
        num_scalar_prefetch=1,
        grid=(n // QT,),
        in_specs=[
            pl.BlockSpec((QT, L), lambda i, r: (i, part)),
            pl.BlockSpec((n, L), lambda i, r: (0, g + part)),
            pl.BlockSpec((n, L), lambda i, r: (0, 2 * g + part)),
            pl.BlockSpec((QT, L), lambda i, r: (i, part)),
            pl.BlockSpec((QT, L), lambda i, r: (i, part)),
            pl.BlockSpec((PAIRS, 8, QT), lambda i, r: (part, 0, i)),
            pl.BlockSpec((QT, 128), lambda i, r: (i, 0)),
            pl.BlockSpec((n, 128), lambda i, r: (0, 0)),
        ],
        out_specs=[
            pl.BlockSpec((QT, L), lambda i, r: (i, 0)),
            pl.BlockSpec((n, L), lambda i, r: (0, 0)),
            pl.BlockSpec((n, L), lambda i, r: (0, 0)),
        ],
        scratch_shapes=[pltpu.VMEM((L, n), f32), pltpu.VMEM((L, n), f32)],
    )
    return pl.pallas_call(
        attend_back_kernel,
        name="attend_back",
        grid_spec=spec,
        out_shape=[shaped((n, L), f32), shaped((n, L), f32), shaped((n, L), bf)],
        compiler_params=params(),
        cost_estimate=cost(2.2e10, 1e7),
    )(rng, qkv, qkv, qkv, g_mix, mix, lb, aug_q, aug_k)


def branch_kernel(tok_ref, mix_ref, w_ref, vec_ref, res_ref, n_ref, nt_ref):
    w = tok_ref.shape[1]
    resid = up(tok_ref[...]) + nn(mix_ref[...], w_ref[...]) + vec_ref[:, 7 * w : 8 * w]
    res_ref[...] = resid
    hat, scale = row_norm(resid)
    normed = hat * vec_ref[:, 2 * w : 3 * w] + vec_ref[:, 3 * w : 4 * w]
    n_ref[...] = rnd(normed)
    nt_ref[...] = rnd(normed.T)


def branch(tokens, mix, weight, vec):
    n, w = tokens.shape
    rows = lambda: pl.BlockSpec((QT, w), lambda i: (i, 0))
    whole = lambda a: pl.BlockSpec(a.shape, lambda i: (0, 0))
    return pl.pallas_call(
        branch_kernel,
        name="branch",
        grid=(n // QT,),
        in_specs=[rows(), rows(), whole(weight), whole(vec)],
        out_specs=[rows(), rows(), pl.BlockSpec((w, QT), lambda i: (0, i))],
        out_shape=[shaped((n, w), f32), shaped((n, w), bf), shaped((w, n), bf)],
        compiler_params=params(),
        cost_estimate=cost(4e9, 1e7),
    )(tokens, mix, weight, vec)


def gelu_parts(x):
    z = jnp.abs(x)
    e = jnp.exp(x * x * -0.5)
    t = 1.0 / (1.0 + (0.3275911 * 0.7071067811865476) * z)
    poly = t * (
        0.5 * 0.254829592
        + t
        * (
            0.5 * -0.284496736
            + t * (0.5 * 1.421413741 + t * (0.5 * -1.453152027 + t * (0.5 * 1.061405429)))
        )
    )
    tail = poly * e
    cdf = jnp.where(x < 0.0, tail, 1.0 - tail)
    return x * cdf, cdf + x * (e * 0.3989422804014327)


def hidden_kernel(n_ref, w_ref, b_ref, a_ref, at_ref, d_ref):
    x = nn(n_ref[...], w_ref[...]) + b_ref[...]
    active, slope = gelu_parts(x)
    active = rnd(active)
    a_ref[...] = active
    at_ref[...] = active.T
    d_ref[...] = rnd(slope)


def hidden_units(normed, weight, vec):
    n, w = normed.shape
    ff = weight.shape[1]
    B = 256
    off = 8 * w // B
    return pl.pallas_call(
        hidden_kernel,
        name="hidden",
        grid=(ff // B,),
        in_specs=[
            pl.BlockSpec((n, w), lambda j: (0, 0)),
            pl.BlockSpec((w, B), lambda j: (0, j)),
            pl.BlockSpec((1, B), lambda j: (0, off + j)),
        ],
        out_specs=[
            pl.BlockSpec((n, B), lambda j: (0, j)),
            pl.BlockSpec((B, n), lambda j: (j, 0)),
            pl.BlockSpec((n, B), lambda j: (0, j)),
        ],
        out_shape=[shaped((n, ff), bf), shaped((ff, n), bf), shaped((n, ff), bf)],
        compiler_params=params(48),
        cost_estimate=cost(1.5e10, 1e7),
    )(normed, weight, vec)


def last_kernel(a_ref, w_ref, res_ref, b_ref, o_ref):
    o_ref[...] = rnd(res_ref[...] + nn(a_ref[...], w_ref[...]) + b_ref[...])


def last(active, weight, resid, vec):
    n, ff = active.shape
    w = resid.shape[1]
    off = (8 * w + ff) // w
    return pl.pallas_call(
        last_kernel,
        name="last",
        grid=(n // QT,),
        in_specs=[
            pl.BlockSpec((QT, ff), lambda i: (i, 0)),
            pl.BlockSpec((ff, w), lambda i: (0, 0)),
            pl.BlockSpec((QT, w), lambda i: (i, 0)),
            pl.BlockSpec((1, w), lambda i: (0, off)),
        ],
        out_specs=pl.BlockSpec((QT, w), lambda i: (i, 0)),
        out_shape=shaped((n, w), bf),
        compiler_params=params(),
        cost_estimate=cost(6e9, 1e7),
    )(active, weight, resid, vec)


def hidden_back_kernel(g_ref, w_ref, d_ref, gh_ref, sum_ref):
    gh = rnd(nt(g_ref[...], w_ref[...]) * up(d_ref[...]))
    gh_ref[...] = gh
    sum_ref[...] = jnp.sum(up(gh), axis=0, keepdims=True)


def hidden_back(given, weight, slope):
    n, w = given.shape
    ff = weight.shape[0]
    B = 768
    return pl.pallas_call(
        hidden_back_kernel,
        name="hidden_back",
        grid=(ff // B,),
        in_specs=[
            pl.BlockSpec((n, w), lambda j: (0, 0)),
            pl.BlockSpec((B, w), lambda j: (j, 0)),
            pl.BlockSpec((n, B), lambda j: (0, j)),
        ],
        out_specs=[pl.BlockSpec((n, B), lambda j: (0, j)), pl.BlockSpec((1, B), lambda j: (0, j))],
        out_shape=[shaped((n, ff), bf), shaped((1, ff), f32)],
        compiler_params=params(),
        cost_estimate=cost(8e9, 1e7),
    )(given, weight, slope)


def norm_back(grad, hat, scale, gain):
    d = grad * gain
    a = jnp.mean(d, axis=-1, keepdims=True)
    b = jnp.mean(d * hat, axis=-1, keepdims=True)
    return (d - a - hat * b) * scale


def second_back_kernel(gh_ref, w_ref, res_ref, cot_ref, vec_ref, wo_ref, gr_ref, gb_ref, gm_ref, sum_ref):
    i = pl.program_id(0)
    w = res_ref.shape[1]
    grad = nt(gh_ref[...], w_ref[...])
    hat, scale = row_norm(res_ref[...])
    total = up(cot_ref[...]) + norm_back(grad, hat, scale, vec_ref[:, 2 * w : 3 * w])
    gr_ref[...] = total
    low = rnd(total)
    gb_ref[...] = low
    gm_ref[...] = rnd(nt(low, wo_ref[...]))
    sums = jnp.concatenate(
        [
            jnp.sum(grad * hat, axis=0, keepdims=True),
            jnp.sum(grad, axis=0, keepdims=True),
            jnp.sum(up(low), axis=0, keepdims=True),
        ],
        axis=0,
    )

    @pl.when(i == 0)
    def _():
        sum_ref[...] = jnp.zeros_like(sum_ref)

    sum_ref[0:3, :] += sums


def second_back(gh, weight, resid, given, vec, out_w):
    n, ff = gh.shape
    w = resid.shape[1]
    rows = lambda c: pl.BlockSpec((QT, c), lambda i: (i, 0))
    whole = lambda a: pl.BlockSpec(a.shape, lambda i: (0, 0))
    return pl.pallas_call(
        second_back_kernel,
        name="second_back",
        grid=(n // QT,),
        in_specs=[rows(ff), whole(weight), rows(w), rows(w), whole(vec), whole(out_w)],
        out_specs=[rows(w), rows(w), rows(w), pl.BlockSpec((8, w), lambda i: (0, 0))],
        out_shape=[shaped((n, w), f32), shaped((n, w), bf), shaped((n, w), bf), shaped((8, w), f32)],
        compiler_params=params(),
        cost_estimate=cost(9e9, 1e7),
    )(gh, weight, resid, given, vec, out_w)


def outer_kernel(sel, x_ref, y_ref, o_ref):
    z, one, r, n = x_ref.shape
    got = nn(x_ref[...].reshape(z * r, n), y_ref[...])
    o_ref[...] = rnd(got).reshape(o_ref.shape)


def outer(x_t, y, sel, groups, share):
    rows, n = x_t.shape
    c = y.shape[1]
    r = rows // (groups * share)
    B = 768 if c % 768 == 0 else 384 if c % 384 == 0 else 256
    spec = pltpu.PrefetchScalarGridSpec(
        num_scalar_prefetch=1,
        grid=(c // B,),
        in_specs=[
            pl.BlockSpec((groups, 1, r, n), lambda j, s: (0, s[0], 0, 0)),
            pl.BlockSpec((n, B), lambda j, s: (0, j)),
        ],
        out_specs=pl.BlockSpec((groups, r, B), lambda j, s: (0, 0, j)),
    )
    return pl.pallas_call(
        outer_kernel,
        name="outer",
        grid_spec=spec,
        out_shape=shaped((groups, r, c), bf),
        compiler_params=params(),
        cost_estimate=cost(4 * groups * r * c * n, 1e7),
    )(sel, x_t.reshape(groups, share, r, n), y)


def turn_back_kernel(
    dq_ref, dk_ref, dv_ref, q_ref, k_ref, cos_ref, sin_ref, grid_ref, gp_ref, b_ref, f_ref
):
    i = pl.program_id(0)
    w = cos_ref.shape[1]
    cos = cos_ref[...]
    sin = sin_ref[...]
    dq = dq_ref[...]
    dk = dk_ref[...]
    gv = dv_ref[...]
    sq = swap(dq)
    sk = swap(dk)
    t = sq * (up(q_ref[...]) * 8.0) + sk * up(k_ref[...])
    g = grid_ref[...]
    gq = rnd(dq * cos - sq * sin)
    gk = rnd(dk * cos - sk * sin)
    gp_ref[:, :w] = gq
    gp_ref[:, w : 2 * w] = gk
    gp_ref[:, 2 * w :] = gv
    add = lambda v: jnp.sum(v, axis=0, keepdims=True)

    @pl.when(i == 0)
    def _():
        b_ref[...] = jnp.zeros_like(b_ref)
        f_ref[...] = jnp.zeros_like(f_ref)

    b_ref[0:3, :] += jnp.concatenate([add(up(gq)), add(up(gk)), add(up(gv))], axis=0)
    f_ref[0:2, :] += jnp.concatenate([add(t * g[:, 0:1]), add(t * g[:, 1:2])], axis=0)


def turn_back(part, dq, dk, dv, qkv, cos, sin, grid_t):
    n, L = dq.shape
    g = qkv.shape[1] // 3 // L
    rows = lambda c, j=0: pl.BlockSpec((QT, c), lambda i: (i, j))
    fixed = lambda: pl.BlockSpec((8, L), lambda i: (0, 0))
    return pl.pallas_call(
        turn_back_kernel,
        name="turn_back",
        grid=(n // QT,),
        in_specs=[rows(L), rows(L), rows(L), rows(L, part), rows(L, g + part)]
        + [rows(L, part), rows(L, part), pl.BlockSpec((QT, 2), lambda i: (i, 0))],
        out_specs=[rows(3 * L), fixed(), fixed()],
        out_shape=[shaped((n, 3 * L), bf), shaped((8, L), f32), shaped((8, L), f32)],
        compiler_params=params(),
        cost_estimate=cost(4e9, 1e7),
    )(dq, dk, dv, qkv, qkv, cos, sin, grid_t)


def first_back_kernel(*refs):
    gp_refs = refs[:-6]
    w_ref, tok_ref, gr_ref, vec_ref, o_ref, sum_ref = refs[-6:]
    i = pl.program_id(0)
    w = tok_ref.shape[1]
    L = w // len(gp_refs)
    gp = [r[:, s * L : (s + 1) * L] for s in range(3) for r in gp_refs]
    grad = nt(jnp.concatenate(gp, axis=1), w_ref[...])
    hat, scale = row_norm(up(tok_ref[...]))
    o_ref[...] = rnd(gr_ref[...] + norm_back(grad, hat, scale, vec_ref[:, :w]))
    sums = jnp.concatenate(
        [jnp.sum(grad * hat, axis=0, keepdims=True), jnp.sum(grad, axis=0, keepdims=True)], axis=0
    )

    @pl.when(i == 0)
    def _():
        sum_ref[...] = jnp.zeros_like(sum_ref)

    sum_ref[0:2, :] += sums


def first_back(gps, weight, tokens, grad_resid, vec):
    n, w = tokens.shape
    rows = lambda c: pl.BlockSpec((QT, c), lambda i: (i, 0))
    whole = lambda a: pl.BlockSpec(a.shape, lambda i: (0, 0))
    return pl.pallas_call(
        first_back_kernel,
        name="first_back",
        grid=(n // QT,),
        in_specs=[rows(g.shape[1]) for g in gps] + [whole(weight), rows(w), rows(w), whole(vec)],
        out_specs=[rows(w), pl.BlockSpec((8, w), lambda i: (0, 0))],
        out_shape=[shaped((n, w), bf), shaped((8, w), f32)],
        compiler_params=params(),
        cost_estimate=cost(7e9, 1e7),
    )(*gps, weight, tokens, grad_resid, vec)


def over_dp(v, k):
    return lax.ppermute(v, "dp", [(i, i ^ k) for i in range(4)])


def over_core(v):
    return lax.ppermute(v, "fsdp", [(i, i ^ 1) for i in range(8)])


def over_z(v, k):
    return lax.ppermute(v, "fsdp", [(i, i ^ (2 * k)) for i in range(8)])


def spread_dp(v):
    return [v] + [over_dp(v, k) for k in (1, 2, 3)]


def spread_z(v):
    return [v] + [over_z(v, k) for k in (1, 2, 3)]


def pairs(v):
    return (v[0] + v[1]) + (v[2] + v[3])


def tie(*values):
    return lax.optimization_barrier(values)


def place():
    d = lax.axis_index("dp")
    f = lax.axis_index("fsdp")
    return d, f // 2, f % 2


def here():
    return jnp.stack(place()).astype(jnp.int32)


def by_index(got, at):
    rows = []
    for j in range(4):
        rel = lax.bitwise_xor(at, j)
        v = got[3]
        for k in (2, 1, 0):
            v = jnp.where(rel == k, got[k], v)
        rows.append(v)
    return rows


def quarter(shard, j):
    r, cols = shard.shape
    return lax.dynamic_slice(shard, (j * (r // 4), 0), (r // 4, cols))


def arrange_kernel(at, *refs):
    out = refs[-1]
    for side in (0, 1):
        for k in range(4):
            for s in range(4):
                column = lax.bitwise_xor(at[1], s) * 2 + lax.bitwise_xor(at[2], side)
                out[column * 4 + lax.bitwise_xor(at[0], k)] = refs[side * 4 + k][s]


def arrange(own, other):
    r, cols = own[0].shape[1:]
    B = cols // 3
    spec = pltpu.PrefetchScalarGridSpec(
        num_scalar_prefetch=1,
        grid=(3,),
        in_specs=[pl.BlockSpec((4, r, B), lambda j, a: (0, 0, j))] * 8,
        out_specs=pl.BlockSpec((32, r, B), lambda j, a: (0, 0, j)),
    )
    out = pl.pallas_call(
        arrange_kernel,
        name="arrange",
        grid_spec=spec,
        out_shape=shaped((32, r, cols), bf),
        compiler_params=params(),
        cost_estimate=cost(1e6, 4 * 32 * r * cols),
    )(here(), *own, *other)
    return out.reshape(32 * r, cols)


def fold_core_kernel(parts, extra, at, *refs):
    outs = refs[-4:]
    for k in range(4):
        col = 0
        for p in range(parts):
            a = refs[(k * parts + p) * 2][0, 0]
            b = refs[(k * parts + p) * 2 + 1][0, 0]
            w = a.shape[1]
            outs[k][0, :, col : col + w] = rnd(up(a) + up(b))
            col += w
        if extra and k:
            e = refs[8 * parts]
            v = e[0] if len(e.shape) == 3 else e[...]
            outs[k][0, :, col:] = v


def fold_core(mines, others, extra=None):
    r = mines[0].shape[1] // 4
    wide = sum(m.shape[2] for m in mines)
    more = 0
    args, specs = [], []
    for k in range(4):
        for m, o in zip(mines, others):
            for v in (m, o):
                w = v.shape[2]
                args.append(v.reshape(4, 4, r, w))
                specs.append(
                    pl.BlockSpec((1, 1, r, w), lambda j, a, k=k: (j, lax.bitwise_xor(a[0], k), 0, 0))
                )
    if extra is not None:
        args.append(extra)
        if extra.ndim == 3:
            more = extra.shape[2]
            specs.append(pl.BlockSpec((1, r, more), lambda j, a: (j, 0, 0)))
        else:
            more = extra.shape[1] // 4
            specs.append(pl.BlockSpec((r, more), lambda j, a: (0, j)))
    widths = [wide] + [wide + more] * 3
    spec = pltpu.PrefetchScalarGridSpec(
        num_scalar_prefetch=1,
        grid=(4,),
        in_specs=specs,
        out_specs=[pl.BlockSpec((1, r, w), lambda j, a: (j, 0, 0)) for w in widths],
    )
    return pl.pallas_call(
        partial(fold_core_kernel, len(mines), extra is not None),
        name="fold_core",
        grid_spec=spec,
        out_shape=[shaped((4, r, w), bf) for w in widths],
        compiler_params=params(),
        cost_estimate=cost(1e6, 48 * r * wide),
    )(here(), *args)


def fold_dp_kernel(at, *refs):
    ins, outs = refs[:-4], refs[-4:]
    w = outs[0].shape[1]
    for k in range(4):
        to = lax.bitwise_xor(at[1], k)
        total = up(ins[0][to])
        for g in ins[1:]:
            total = total + up(g[to][:, :w])
        outs[k][...] = rnd(total)


def fold_dp(own, got):
    whole = lambda v: pl.BlockSpec(v.shape, lambda j, a: (0, 0, 0))
    r, w = own.shape[1:]
    spec = pltpu.PrefetchScalarGridSpec(
        num_scalar_prefetch=1,
        grid=(1,),
        in_specs=[whole(v) for v in [own] + got],
        out_specs=[pl.BlockSpec((r, w), lambda j, a: (0, 0))] * 4,
    )
    return pl.pallas_call(
        fold_dp_kernel,
        name="fold_dp",
        grid_spec=spec,
        out_shape=[shaped((r, w), bf)] * 4,
        compiler_params=params(),
        cost_estimate=cost(1e6, 40 * r * w),
    )(here(), own, *got)


def fold_z(got):
    return rnd(pairs([up(g) for g in got]))


def share(got):
    return up(jnp.concatenate(by_index(got, place()[0]), 0))


def adam_terms(grad, first, second, master, decay):
    first_new = 0.9 * first + 0.1 * grad
    second_new = 0.999 * second + 0.001 * grad * grad
    first_hat = first_new / (1.0 - 0.9**STEP)
    second_hat = second_new / (1.0 - 0.999**STEP)
    update = first_hat / (jnp.sqrt(second_hat) + 1e-06) + decay * master
    return (first_new, second_new, update)


def body(fast, tokens, cotangent, image_ids, patch_grid, *state):
    masters, vectors = state[:4], state[4]
    firsts, vector_first = state[5:9], state[9]
    seconds, vector_second = state[10:14], state[14]
    n, w = tokens.shape
    size = vectors.shape[0]
    heads = w // HD
    count = w // 128 // PAIRS
    L = 128 * PAIRS
    low = [rnd(m) for m in masters]
    gather = lambda v: lax.all_gather(v, "fsdp", axis=0, tiled=True)
    scatter = lambda v: lax.psum_scatter(v, "fsdp", scatter_dimension=0, tiled=True)
    whole = jnp.zeros((1,), jnp.int32)
    d, z, c = place()
    mine = jnp.stack([c]).astype(jnp.int32)
    halves = lambda x_t, y: (outer(x_t, y, 1 - mine, 4, 2), outer(x_t, y, mine, 4, 2))
    join = lambda rows: jnp.concatenate(rows, axis=-1)

    if fast:
        q_rows = low[0].shape[0] // 4
        row = jnp.pad(rnd(vectors), (0, low[0].shape[1] - size)).reshape(1, -1)
        got = spread_z(jnp.concatenate([quarter(low[0], d), row], 0))
        qkv_column = jnp.stack([g[:q_rows] for g in got])
        packed = jnp.concatenate(by_index([g[q_rows:, :size] for g in got], z), 0)
        other = over_core(packed)
        packed = jnp.stack([jnp.where(c == 0, packed, other), jnp.where(c == 0, other, packed)], 1)
        packed = packed.reshape(-1)
        up_part, out_part, down_part, qkv_column = tie(
            quarter(low[2], d), low[1], low[3], qkv_column
        )
        full_out = gather(out_part)
        qkv_own = spread_dp(qkv_column)
        up_column = jnp.stack(spread_z(up_part))
        full_down = gather(down_part)
    else:
        packed = gather(rnd(vectors))
        full_qkv, full_out, full_up, full_down = [gather(v) for v in low]
    vec = up(packed).reshape(1, -1)
    freq = vec[0, -w:].reshape(2, heads, 1, HD // 2)
    freq = jnp.broadcast_to(freq, (2, heads, 2, HD // 2)).reshape(2, w)
    grid_t = up(patch_grid.T)
    given = jnp.where((image_ids >= 0)[:, None], cotangent, jnp.zeros_like(cotangent))
    grad_bias_down = jnp.sum(up(given), axis=0)
    weight_local = jnp.stack([jnp.sum(m * m) for m in masters])
    aug_q, aug_k, rng = tables(image_ids)

    normed, normed_t, cos, sin = first(tokens, vec, freq, grid_t)
    if fast:
        normed, *qkv_own = tie(normed, *qkv_own)
        full_qkv = arrange(qkv_own, [over_core(v) for v in qkv_own])
        up_column, full_qkv = tie(up_column, full_qkv)
        up_own = spread_dp(up_column)
    qkv = project(normed, full_qkv, vec, cos, sin)
    mix, mix_t, lb = attend(qkv, aug_q, aug_k, rng)
    if fast:
        mix, *up_own = tie(mix, *up_own)
        up_other = [over_core(v) for v in up_own]
    resid, normed_two, normed_two_t = branch(tokens, mix, full_out, vec)
    if fast:
        full_up = arrange(up_own, up_other)
    active, active_t, slope = hidden_units(normed_two, full_up, vec)
    if fast:
        theirs, own = halves(active_t, given)
        pieces = fold_core([own], [over_core(theirs)])
        active, slope, full_down = tie(active, slope, full_down)
        active, slope, *pieces = tie(active, slope, *pieces)
        got = [over_dp(v, k) for k, v in zip((1, 2, 3), pieces[1:])]
    else:
        down_full = outer(active_t, given, whole, 1, 1)[0]
    output = last(active, full_down, resid, vec)
    grad_hidden, grad_bias_up = hidden_back(given, full_down, slope)
    if fast:
        output, grad_hidden, *got = tie(output, grad_hidden, *got)
        down_z = fold_dp(pieces[0], got)
        grad_hidden, *down_z = tie(grad_hidden, *down_z)
        got = [down_z[0]] + [over_z(v, k) for k, v in zip((1, 2, 3), down_z[1:])]
        theirs, own = halves(normed_two_t, grad_hidden)
        own, *got = tie(own, *got)
        down_f = fold_z(got)
        more = down_f.reshape(4, -1, w)
        pieces = fold_core([own], [over_core(theirs)], more)
        grad_hidden, down_f, *pieces = tie(grad_hidden, down_f, *pieces)
        got = [over_dp(v, k) for k, v in zip((1, 2, 3), pieces[1:])]
    else:
        up_full = outer(normed_two_t, grad_hidden, whole, 1, 1)[0]
    grad_resid, grad_branch, grad_mix, sums_two = second_back(
        grad_hidden, full_up, resid, given, vec, full_out
    )
    if fast:
        out_theirs, out_own = halves(mix_t, grad_branch)
        out_sent = over_core(out_theirs)
    else:
        out_full = outer(mix_t, grad_branch, whole, 1, 1)[0]
    projs, sums_proj, sums_freq, qkv_parts = [], [], [], []
    for part in range(count):
        dq, dk, dv = attend_back(part, qkv, grad_mix, mix, lb, aug_q, aug_k, rng)
        if fast and part == 0:
            dq, *got = tie(dq, *got)
            up_width = pieces[0].shape[2]
            down_grad = share([down_f] + [g[:, :, up_width:].reshape(down_f.shape) for g in got])
            up_z = fold_dp(pieces[0], got)
            dq, *up_z = tie(dq, *up_z)
            got = [up_z[0]] + [over_z(v, k) for k, v in zip((1, 2, 3), up_z[1:])]
        if fast and part > 0:
            dq, *got = tie(dq, *got)
        gp, bs, fs = turn_back(part, dq, dk, dv, qkv, cos, sin, grid_t)
        projs.append(gp)
        sums_proj.append(bs)
        sums_freq.append(fs)
        if not fast:
            qkv_parts.append(outer(normed_t, gp, whole, 1, 1)[0])
        elif part == 0:
            theirs, own = halves(normed_t, gp)
            own, *got = tie(own, *got)
            up_f = fold_z(got)
            pieces = fold_core([own, out_own], [over_core(theirs), out_sent], up_f)
            grad_mix, up_f, *pieces = tie(grad_mix, up_f, *pieces)
            got = [over_dp(v, k) for k, v in zip((1, 2, 3), pieces[1:])]
        else:
            a_width = pieces[0].shape[2]
            back = lambda g: join([g[i, :, a_width:] for i in range(4)])
            up_grad = share([up_f] + [back(g) for g in got])
            theirs, own = halves(normed_t, gp)
            a_z = fold_dp(pieces[0], got)
            pieces = fold_core([own], [over_core(theirs)])
            projs[-1], *pieces = tie(gp, *pieces)
            got = [over_dp(v, k) for k, v in zip((1, 2, 3), pieces[1:])]
    tokens_grad, sums_one = first_back(projs, full_qkv, tokens, grad_resid, vec)
    if fast:
        sums_one, *got = tie(sums_one, *got)
    freq_sums = join([s[:2] for s in sums_freq]).reshape(2, heads, 2, HD // 2)
    vector_full = jnp.concatenate(
        [
            sums_one[0],
            sums_one[1],
            sums_two[0],
            sums_two[1],
            join([s[:3] for s in sums_proj]).reshape(-1),
            sums_two[2],
            grad_bias_up.reshape(-1),
            grad_bias_down,
            (freq_sums[:, :, 0] - freq_sums[:, :, 1]).reshape(-1),
        ]
    )
    off = vector_full.shape[0] - 2 * w
    if fast:
        v = vector_full.reshape(1, -1)
        v = v + over_core(v)
        bias_down = v[:, off : off + w]
        v = v.reshape(4, 2, size)
        v = jnp.where(c == 0, v[:, 0], v[:, 1])
        v = jnp.concatenate([v, jnp.broadcast_to(bias_down, (4, w))], 1)
        v = jnp.pad(v, ((0, 0), (0, 128 * q_rows - v.shape[1]))).reshape(4, q_rows, 128)
        v = rnd(v)
        b_z = fold_dp(pieces[0], got)
        sends = []
        for k in range(4):
            mine_v = lax.dynamic_index_in_dim(v, lax.bitwise_xor(z, k), 0, keepdims=False)
            sends.append(join([a_z[k], b_z[k], mine_v]))
        got = [sends[0]] + [over_z(s, k) for k, s in zip((1, 2, 3), sends[1:])]
        total = pairs([up(g) for g in got])
        got = spread_dp(rnd(total))
        tail = pairs([up(g[:, -128:]) for g in got]).reshape(-1)
        vector_grad = tail[:size]
        down_bias_grad = tail[size : size + w]
        grads = share([g[:, :-128] for g in got])
        done = [grads[:, : 3 * L], grads[:, 3 * L + w :]]
        out_grad = grads[:, 3 * L : 3 * L + w]
        total_fsdp = lambda v: pairs(spread_z(v + over_core(v)))
    else:
        give = lambda v: lax.psum(scatter(up(v)), "dp")
        up_grad, down_grad, out_grad = give(up_full), give(down_full), give(out_full)
        done = [give(v) for v in qkv_parts]
        vector_grad = give(vector_full)
        down_bias_grad = lax.psum(grad_bias_down, ("dp", "fsdp"))
        total_fsdp = lambda v: lax.psum(v, "fsdp")
    qkv_grad = join([g[:, s * L : (s + 1) * L] for s in range(3) for g in done])
    reduced = (qkv_grad, out_grad, up_grad, down_grad)
    steps = [
        adam_terms(reduced[k], firsts[k], seconds[k], masters[k], 0.01) for k in range(4)
    ]
    update_local = jnp.stack([jnp.sum(s[2] * s[2]) for s in steps])
    norms = jnp.sqrt(total_fsdp(jnp.concatenate([weight_local, update_local]).reshape(1, -1)))
    weight_norms, update_norms = norms[0, :4], norms[0, 4:]
    new_list = [
        masters[k] - 0.3 * (weight_norms[k] / (update_norms[k] + 1e-06)) * steps[k][2]
        for k in range(4)
    ]
    vector_step = adam_terms(vector_grad, vector_first, vector_second, vectors, 0.0)
    return (
        output,
        tokens_grad,
        *reduced,
        vector_grad,
        down_bias_grad,
        *[s[0] for s in steps],
        vector_step[0],
        *[s[1] for s in steps],
        vector_step[1],
        *new_list,
        vectors - 0.2 * vector_step[2],
        weight_norms,
        update_norms,
    )


def solution(mesh):
    both = P(("dp", "fsdp"), None)
    mat = [P("fsdp", None)] * 4 + [P("fsdp")]
    in_specs = (both, both, P(("dp", "fsdp")), P(None, ("dp", "fsdp")), *mat, *mat, *mat)
    out_specs = (both, both, *mat, P(), *mat, *mat, *mat, P(), P())
    fast = mesh.shape["dp"] == 4 and mesh.shape["fsdp"] == 8
    return jax.shard_map(
        partial(body, fast), mesh=mesh, in_specs=in_specs, out_specs=out_specs, check_vma=False
    )
```

```python
from functools import partial

import jax
import jax.numpy as jnp
from jax import lax
from jax.experimental import pallas as pl
from jax.experimental.pallas import tpu as pltpu
from jax.sharding import PartitionSpec as P

H = 12
HD = 64
STEP = 10
QT = 256
KT = 128
PAIRS = 3
VARIANTS = (2, 3, 4, 5, 7, 8)
norm_eps = 1e-06
bf = jnp.bfloat16
f32 = jnp.float32


def nt(a, b):
    return lax.dot_general(a, b, (((1,), (1,)), ((), ())), preferred_element_type=f32)


def nn(a, b):
    return lax.dot_general(a, b, (((1,), (0,)), ((), ())), preferred_element_type=f32)


def rnd(v):
    return v.astype(bf)


def up(v):
    return v.astype(f32)


def params(mib=22):
    return pltpu.CompilerParams(vmem_limit_bytes=mib << 20)


def cost(flops, moved):
    return pl.CostEstimate(flops=int(flops), bytes_accessed=int(moved), transcendentals=0)


def shaped(shape, kind):
    return jax.ShapeDtypeStruct(shape, kind)


def row_norm(v):
    centre = jnp.mean(v, axis=-1, keepdims=True)
    centred = v - centre
    spread = jnp.mean(centred * centred, axis=-1, keepdims=True)
    scale = lax.rsqrt(spread + norm_eps)
    return centred * scale, scale


def first_kernel(tok_ref, vec_ref, freq_ref, grid_ref, n_ref, nt_ref, cos_ref, sin_ref):
    w = tok_ref.shape[1]
    hat, scale = row_norm(up(tok_ref[...]))
    normed = hat * vec_ref[:, :w] + vec_ref[:, w : 2 * w]
    n_ref[...] = rnd(normed)
    nt_ref[...] = rnd(normed.T)
    g = grid_ref[...]
    angle = g[:, 0:1] * freq_ref[0:1, :] + g[:, 1:2] * freq_ref[1:2, :]
    lane = lax.broadcasted_iota(jnp.int32, (1, w), 1)
    cos_ref[...] = jnp.cos(angle)
    s = jnp.sin(angle)
    sin_ref[...] = jnp.where(lane & 63 < 32, -s, s)


def first(tokens, vec, freq, grid_t):
    n, w = tokens.shape
    rows = lambda: pl.BlockSpec((QT, w), lambda i: (i, 0))
    whole = lambda a: pl.BlockSpec(a.shape, lambda i: (0, 0))
    return pl.pallas_call(
        first_kernel,
        name="first",
        grid=(n // QT,),
        in_specs=[rows(), whole(vec), whole(freq), pl.BlockSpec((QT, 2), lambda i: (i, 0))],
        out_specs=[rows(), pl.BlockSpec((w, QT), lambda i: (0, i)), rows(), rows()],
        out_shape=[shaped((n, w), bf), shaped((w, n), bf), shaped((n, w), f32), shaped((n, w), f32)],
        compiler_params=params(),
        cost_estimate=cost(1e10, 1e7),
    )(tokens, vec, freq, grid_t)


def swap(v):
    w = v.shape[1]
    lane = lax.broadcasted_iota(jnp.int32, (1, w), 1)
    return jnp.where(lane & 63 < 32, pltpu.roll(v, w - 32, 1), pltpu.roll(v, 32, 1))


def project_kernel(n_ref, w_ref, b_ref, cos_ref, sin_ref, o_ref):
    j = pl.program_id(0)
    u = nn(n_ref[...], w_ref[...]) + b_ref[...]

    @pl.when(j < 2)
    def _():
        turned = u * cos_ref[...] + swap(u) * sin_ref[...]
        o_ref[...] = rnd(turned * jnp.where(j < 1, 0.125, 1.0))

    @pl.when(j >= 2)
    def _():
        o_ref[...] = rnd(u)


def project(normed, weight, vec, cos, sin):
    n, w = normed.shape
    whole = lambda: pl.BlockSpec((n, w), lambda j: (0, 0))
    return pl.pallas_call(
        project_kernel,
        name="project",
        grid=(3,),
        in_specs=[
            whole(),
            pl.BlockSpec((w, w), lambda j: (0, j)),
            pl.BlockSpec((1, w), lambda j: (0, 4 + j)),
            whole(),
            whole(),
        ],
        out_specs=pl.BlockSpec((n, w), lambda j: (0, j)),
        out_shape=shaped((n, 3 * w), bf),
        compiler_params=params(22),
        cost_estimate=cost(8e9, 1e7),
    )(normed, weight, vec, cos, sin)


def tables(ids):
    n = ids.shape[0]
    lane = jnp.arange(128) & 63
    one = (ids[:, None] + 1 == lane[None]).astype(f32)
    small = (lane < 8)[None]
    aug_q = rnd(jnp.where(small, one, 0.0))
    aug_k = rnd(jnp.where(small, (one - 1.0) * 1e30, jnp.where((lane < 11)[None], 1.0, 0.0)))
    tiles = n // QT
    hit = (ids.reshape(tiles, QT, 1) == ids[None, None, :]).any(1)
    pos = jnp.arange(n)[None]
    lo = jnp.min(jnp.where(hit, pos, n), 1) // KT
    hi = jnp.max(jnp.where(hit, pos, -1), 1) // KT + 1
    need = hi - lo
    width = jnp.full_like(need, VARIANTS[-1])
    for v in VARIANTS[::-1]:
        width = jnp.where(need <= v, v, width)
    start = jnp.minimum(lo, n // KT - width)
    return aug_q, aug_k, jnp.stack([start, width]).astype(jnp.int32)


def low_lanes():
    return lax.broadcasted_iota(jnp.int32, (1, 128), 1) < 64


def attend_kernel(rng, q_ref, k_ref, v_ref, aq_ref, ak_ref, mix_ref, mixt_ref, lb_ref, vt):
    i = pl.program_id(1)
    n = k_ref.shape[0]
    start = rng[0, i]
    width = rng[1, i]
    low = low_lanes()

    @pl.when(i == 0)
    def _():
        one = jnp.ones((16, n), bf)
        for p in range(PAIRS):
            t = v_ref[:, 128 * p : 128 * p + 128].T
            for h in (0, 1):
                vt[2 * p + h, :64, :] = t[64 * h : 64 * h + 64]
                vt[2 * p + h, 64:, :] = one

    aq = aq_ref[...]
    for W in VARIANTS:

        @pl.when(width == W)
        def _():
            at = pl.ds(pl.multiple_of(start * KT, KT), W * KT)
            ak = ak_ref[at, :]
            scores = []
            for p in range(PAIRS):
                c = slice(128 * p, 128 * p + 128)
                q = q_ref[:, c]
                k = k_ref[at, c]
                scores.append(nt(jnp.where(low, k, ak), jnp.where(low, q, aq)))
                scores.append(nt(jnp.where(low, ak, k), jnp.where(low, aq, q)))
            for p in range(PAIRS):
                c = slice(128 * p, 128 * p + 128)
                outs = []
                for h in (0, 1):
                    s = scores[2 * p + h]
                    m = jnp.max(s, axis=0, keepdims=True)
                    e = rnd(jnp.exp(s - m))
                    o = nn(vt[2 * p + h, :, at], e)
                    t = o[64:65]
                    outs.append(o[:64] * (1.0 / t))
                    lb_ref[p, h : h + 1, :] = m + jnp.log(t)
                both = jnp.concatenate(outs, 0)
                mix_ref[:, c] = rnd(both.T)
                mixt_ref[c, :] = rnd(both)


def attend(qkv, aug_q, aug_k, rng):
    n, w3 = qkv.shape
    w = w3 // 3
    L = 128 * PAIRS
    g = w // L
    spec = pltpu.PrefetchScalarGridSpec(
        num_scalar_prefetch=1,
        grid=(g, n // QT),
        in_specs=[
            pl.BlockSpec((QT, L), lambda p, i, r: (i, p)),
            pl.BlockSpec((n, L), lambda p, i, r: (0, g + p)),
            pl.BlockSpec((n, L), lambda p, i, r: (0, 2 * g + p)),
            pl.BlockSpec((QT, 128), lambda p, i, r: (i, 0)),
            pl.BlockSpec((n, 128), lambda p, i, r: (0, 0)),
        ],
        out_specs=[
            pl.BlockSpec((QT, L), lambda p, i, r: (i, p)),
            pl.BlockSpec((L, QT), lambda p, i, r: (p, i)),
            pl.BlockSpec((PAIRS, 8, QT), lambda p, i, r: (p, 0, i)),
        ],
        scratch_shapes=[pltpu.VMEM((2 * PAIRS, 80, n), bf)],
    )
    return pl.pallas_call(
        attend_kernel,
        name="attend",
        grid_spec=spec,
        out_shape=[shaped((n, w), bf), shaped((w, n), bf), shaped((w // 128, 8, n), f32)],
        compiler_params=params(),
        cost_estimate=cost(2.3e10, 1e7),
    )(rng, qkv, qkv, qkv, aug_q, aug_k)


def fill(aug, x):
    lane = lax.broadcasted_iota(jnp.int32, (1, 128), 1) & 63
    a = rnd(x)
    r = x - up(a)
    b = rnd(r)
    c = rnd(r - up(b))
    return jnp.where(lane == 8, a, jnp.where(lane == 9, b, jnp.where(lane == 10, c, aug)))


def attend_back_kernel(
    rng, q_ref, k_ref, v_ref, g_ref, mix_ref, lb_ref, aq_ref, ak_ref,
    dq_ref, dk_ref, dv_ref, dk_acc, dv_acc,
):
    i = pl.program_id(0)
    start = rng[0, i]
    width = rng[1, i]

    @pl.when(i == 0)
    def _():
        dk_acc[...] = jnp.zeros_like(dk_acc)
        dv_acc[...] = jnp.zeros_like(dv_acc)

    low = low_lanes()
    aq0 = aq_ref[...]
    zero = jnp.zeros((1, 128), bf)
    held = []
    for p in range(PAIRS):
        c = slice(128 * p, 128 * p + 128)
        q = q_ref[:, c]
        g = g_ref[:, c]
        prod = up(g) * up(mix_ref[:, c])
        even = jnp.sum(jnp.where(low, prod, 0.0), axis=1, keepdims=True)
        odd = jnp.sum(jnp.where(low, 0.0, prod), axis=1, keepdims=True)
        lt = lb_ref[p].T
        aq = fill(aq0, -jnp.where(low, lt[:, 1:2], lt[:, 0:1]))
        ag = fill(zero, -jnp.where(low, odd, even))
        held.append(
            (
                (jnp.where(low, q, aq), jnp.where(low, aq, q)),
                (jnp.where(low, g, ag), jnp.where(low, ag, g)),
                q.T,
                g.T,
            )
        )
    for W in VARIANTS:

        @pl.when(width == W)
        def _():
            at = pl.ds(pl.multiple_of(start * KT, KT), W * KT)
            ak = ak_ref[at, :]
            for p in range(PAIRS):
                c = slice(128 * p, 128 * p + 128)
                qs, gs, qt, gt = held[p]
                k = k_ref[at, c]
                v = v_ref[at, c]
                one = jnp.ones_like(v)
                ks = (jnp.where(low, k, ak), jnp.where(low, ak, k))
                vs = (jnp.where(low, v, one), jnp.where(low, one, v))
                dqs = []
                for h in (0, 1):
                    e = jnp.exp(nt(qs[h], ks[h]))
                    ds = rnd(e * nt(gs[h], vs[h]))
                    e = rnd(e)
                    half = slice(64 * h, 64 * h + 64)
                    to = slice(128 * p + 64 * h, 128 * p + 64 * h + 64)
                    dqs.append(nn(ds, k))
                    dk_acc[to, at] += nn(qt[half], ds)
                    dv_acc[to, at] += nn(gt[half], e)
                dq_ref[:, c] = jnp.where(low, dqs[0], dqs[1]) * 0.125

    @pl.when(i == pl.num_programs(0) - 1)
    def _():
        dk_ref[...] = dk_acc[...].T
        dv_ref[...] = rnd(dv_acc[...].T)


def attend_back(part, qkv, g_mix, mix, lb, aug_q, aug_k, rng):
    n, w3 = qkv.shape
    L = 128 * PAIRS
    g = w3 // 3 // L
    spec = pltpu.PrefetchScalarGridSpec(
        num_scalar_prefetch=1,
        grid=(n // QT,),
        in_specs=[
            pl.BlockSpec((QT, L), lambda i, r: (i, part)),
            pl.BlockSpec((n, L), lambda i, r: (0, g + part)),
            pl.BlockSpec((n, L), lambda i, r: (0, 2 * g + part)),
            pl.BlockSpec((QT, L), lambda i, r: (i, part)),
            pl.BlockSpec((QT, L), lambda i, r: (i, part)),
            pl.BlockSpec((PAIRS, 8, QT), lambda i, r: (part, 0, i)),
            pl.BlockSpec((QT, 128), lambda i, r: (i, 0)),
            pl.BlockSpec((n, 128), lambda i, r: (0, 0)),
        ],
        out_specs=[
            pl.BlockSpec((QT, L), lambda i, r: (i, 0)),
            pl.BlockSpec((n, L), lambda i, r: (0, 0)),
            pl.BlockSpec((n, L), lambda i, r: (0, 0)),
        ],
        scratch_shapes=[pltpu.VMEM((L, n), f32), pltpu.VMEM((L, n), f32)],
    )
    return pl.pallas_call(
        attend_back_kernel,
        name="attend_back",
        grid_spec=spec,
        out_shape=[shaped((n, L), f32), shaped((n, L), f32), shaped((n, L), bf)],
        compiler_params=params(),
        cost_estimate=cost(2.2e10, 1e7),
    )(rng, qkv, qkv, qkv, g_mix, mix, lb, aug_q, aug_k)


def branch_kernel(tok_ref, mix_ref, w_ref, vec_ref, res_ref, n_ref, nt_ref):
    w = tok_ref.shape[1]
    resid = up(tok_ref[...]) + nn(mix_ref[...], w_ref[...]) + vec_ref[:, 7 * w : 8 * w]
    res_ref[...] = resid
    hat, scale = row_norm(resid)
    normed = hat * vec_ref[:, 2 * w : 3 * w] + vec_ref[:, 3 * w : 4 * w]
    n_ref[...] = rnd(normed)
    nt_ref[...] = rnd(normed.T)


def branch(tokens, mix, weight, vec):
    n, w = tokens.shape
    rows = lambda: pl.BlockSpec((QT, w), lambda i: (i, 0))
    whole = lambda a: pl.BlockSpec(a.shape, lambda i: (0, 0))
    return pl.pallas_call(
        branch_kernel,
        name="branch",
        grid=(n // QT,),
        in_specs=[rows(), rows(), whole(weight), whole(vec)],
        out_specs=[rows(), rows(), pl.BlockSpec((w, QT), lambda i: (0, i))],
        out_shape=[shaped((n, w), f32), shaped((n, w), bf), shaped((w, n), bf)],
        compiler_params=params(48),
        cost_estimate=cost(4e9, 1e7),
    )(tokens, mix, weight, vec)


def gelu_parts(x):
    cdf = 0.5 + 0.5 * lax.erf(x * 0.7071067811865476)
    return x * cdf, cdf + x * (jnp.exp(x * x * -0.5) * 0.3989422804014327)


def hidden_kernel(n_ref, w_ref, b_ref, a_ref, at_ref, d_ref):
    x = nn(n_ref[...], w_ref[...]) + b_ref[...]
    active, slope = gelu_parts(x)
    active = rnd(active)
    a_ref[...] = active
    at_ref[...] = active.T
    d_ref[...] = rnd(slope)


def hidden_units(normed, weight, vec):
    n, w = normed.shape
    ff = weight.shape[1]
    B = 768
    off = 8 * w // B
    return pl.pallas_call(
        hidden_kernel,
        name="hidden",
        grid=(ff // B,),
        in_specs=[
            pl.BlockSpec((n, w), lambda j: (0, 0)),
            pl.BlockSpec((w, B), lambda j: (0, j)),
            pl.BlockSpec((1, B), lambda j: (0, off + j)),
        ],
        out_specs=[
            pl.BlockSpec((n, B), lambda j: (0, j)),
            pl.BlockSpec((B, n), lambda j: (j, 0)),
            pl.BlockSpec((n, B), lambda j: (0, j)),
        ],
        out_shape=[shaped((n, ff), bf), shaped((ff, n), bf), shaped((n, ff), bf)],
        compiler_params=params(48),
        cost_estimate=cost(1.5e10, 1e7),
    )(normed, weight, vec)


def last_kernel(a_ref, w_ref, res_ref, b_ref, o_ref):
    o_ref[...] = rnd(res_ref[...] + nn(a_ref[...], w_ref[...]) + b_ref[...])


def last(active, weight, resid, vec):
    n, ff = active.shape
    w = resid.shape[1]
    off = (8 * w + ff) // w
    return pl.pallas_call(
        last_kernel,
        name="last",
        grid=(n // QT,),
        in_specs=[
            pl.BlockSpec((QT, ff), lambda i: (i, 0)),
            pl.BlockSpec((ff, w), lambda i: (0, 0)),
            pl.BlockSpec((QT, w), lambda i: (i, 0)),
            pl.BlockSpec((1, w), lambda i: (0, off)),
        ],
        out_specs=pl.BlockSpec((QT, w), lambda i: (i, 0)),
        out_shape=shaped((n, w), bf),
        compiler_params=params(),
        cost_estimate=cost(6e9, 1e7),
    )(active, weight, resid, vec)


def hidden_back_kernel(g_ref, w_ref, d_ref, gh_ref, sum_ref):
    gh = rnd(nt(g_ref[...], w_ref[...]) * up(d_ref[...]))
    gh_ref[...] = gh
    sum_ref[...] = jnp.sum(up(gh), axis=0, keepdims=True)


def hidden_back(given, weight, slope):
    n, w = given.shape
    ff = weight.shape[0]
    B = 768
    return pl.pallas_call(
        hidden_back_kernel,
        name="hidden_back",
        grid=(ff // B,),
        in_specs=[
            pl.BlockSpec((n, w), lambda j: (0, 0)),
            pl.BlockSpec((B, w), lambda j: (j, 0)),
            pl.BlockSpec((n, B), lambda j: (0, j)),
        ],
        out_specs=[pl.BlockSpec((n, B), lambda j: (0, j)), pl.BlockSpec((1, B), lambda j: (0, j))],
        out_shape=[shaped((n, ff), bf), shaped((1, ff), f32)],
        compiler_params=params(),
        cost_estimate=cost(8e9, 1e7),
    )(given, weight, slope)


def norm_back(grad, hat, scale, gain):
    d = grad * gain
    a = jnp.mean(d, axis=-1, keepdims=True)
    b = jnp.mean(d * hat, axis=-1, keepdims=True)
    return (d - a - hat * b) * scale


def second_back_kernel(gh_ref, w_ref, res_ref, cot_ref, vec_ref, wo_ref, gr_ref, gb_ref, gm_ref, sum_ref):
    i = pl.program_id(0)
    w = res_ref.shape[1]
    grad = nt(gh_ref[...], w_ref[...])
    hat, scale = row_norm(res_ref[...])
    total = up(cot_ref[...]) + norm_back(grad, hat, scale, vec_ref[:, 2 * w : 3 * w])
    gr_ref[...] = total
    low = rnd(total)
    gb_ref[...] = low
    gm_ref[...] = rnd(nt(low, wo_ref[...]))
    sums = jnp.concatenate(
        [
            jnp.sum(grad * hat, axis=0, keepdims=True),
            jnp.sum(grad, axis=0, keepdims=True),
            jnp.sum(up(low), axis=0, keepdims=True),
        ],
        axis=0,
    )

    @pl.when(i == 0)
    def _():
        sum_ref[...] = jnp.zeros_like(sum_ref)

    sum_ref[0:3, :] += sums


def second_back(gh, weight, resid, given, vec, out_w):
    n, ff = gh.shape
    w = resid.shape[1]
    rows = lambda c: pl.BlockSpec((QT, c), lambda i: (i, 0))
    whole = lambda a: pl.BlockSpec(a.shape, lambda i: (0, 0))
    return pl.pallas_call(
        second_back_kernel,
        name="second_back",
        grid=(n // QT,),
        in_specs=[rows(ff), whole(weight), rows(w), rows(w), whole(vec), whole(out_w)],
        out_specs=[rows(w), rows(w), rows(w), pl.BlockSpec((8, w), lambda i: (0, 0))],
        out_shape=[shaped((n, w), f32), shaped((n, w), bf), shaped((n, w), bf), shaped((8, w), f32)],
        compiler_params=params(),
        cost_estimate=cost(9e9, 1e7),
    )(gh, weight, resid, given, vec, out_w)


def outer_kernel(sel, x_ref, y_ref, o_ref):
    z, one, r, n = x_ref.shape
    got = nn(x_ref[...].reshape(z * r, n), y_ref[...])
    o_ref[...] = rnd(got).reshape(o_ref.shape)


def outer(x_t, y, sel, groups, share):
    rows, n = x_t.shape
    c = y.shape[1]
    r = rows // (groups * share)
    B = 768 if c % 768 == 0 else 384 if c % 384 == 0 else 256
    spec = pltpu.PrefetchScalarGridSpec(
        num_scalar_prefetch=1,
        grid=(c // B,),
        in_specs=[
            pl.BlockSpec((groups, 1, r, n), lambda j, s: (0, s[0], 0, 0)),
            pl.BlockSpec((n, B), lambda j, s: (0, j)),
        ],
        out_specs=pl.BlockSpec((groups, r, B), lambda j, s: (0, 0, j)),
    )
    return pl.pallas_call(
        outer_kernel,
        name="outer",
        grid_spec=spec,
        out_shape=shaped((groups, r, c), bf),
        compiler_params=params(),
        cost_estimate=cost(4 * groups * r * c * n, 1e7),
    )(sel, x_t.reshape(groups, share, r, n), y)


def turn_back_kernel(
    dq_ref, dk_ref, dv_ref, q_ref, k_ref, cos_ref, sin_ref, grid_ref, gp_ref, b_ref, f_ref
):
    i = pl.program_id(0)
    w = cos_ref.shape[1]
    cos = cos_ref[...]
    sin = sin_ref[...]
    dq = dq_ref[...]
    dk = dk_ref[...]
    gv = dv_ref[...]
    sq = swap(dq)
    sk = swap(dk)
    t = sq * (up(q_ref[...]) * 8.0) + sk * up(k_ref[...])
    g = grid_ref[...]
    gq = rnd(dq * cos - sq * sin)
    gk = rnd(dk * cos - sk * sin)
    gp_ref[:, :w] = gq
    gp_ref[:, w : 2 * w] = gk
    gp_ref[:, 2 * w :] = gv
    add = lambda v: jnp.sum(v, axis=0, keepdims=True)

    @pl.when(i == 0)
    def _():
        b_ref[...] = jnp.zeros_like(b_ref)
        f_ref[...] = jnp.zeros_like(f_ref)

    b_ref[0:3, :] += jnp.concatenate([add(up(gq)), add(up(gk)), add(up(gv))], axis=0)
    f_ref[0:2, :] += jnp.concatenate([add(t * g[:, 0:1]), add(t * g[:, 1:2])], axis=0)


def turn_back(part, dq, dk, dv, qkv, cos, sin, grid_t):
    n, L = dq.shape
    g = qkv.shape[1] // 3 // L
    rows = lambda c, j=0: pl.BlockSpec((QT, c), lambda i: (i, j))
    fixed = lambda: pl.BlockSpec((8, L), lambda i: (0, 0))
    return pl.pallas_call(
        turn_back_kernel,
        name="turn_back",
        grid=(n // QT,),
        in_specs=[rows(L), rows(L), rows(L), rows(L, part), rows(L, g + part)]
        + [rows(L, part), rows(L, part), pl.BlockSpec((QT, 2), lambda i: (i, 0))],
        out_specs=[rows(3 * L), fixed(), fixed()],
        out_shape=[shaped((n, 3 * L), bf), shaped((8, L), f32), shaped((8, L), f32)],
        compiler_params=params(),
        cost_estimate=cost(4e9, 1e7),
    )(dq, dk, dv, qkv, qkv, cos, sin, grid_t)


def first_back_kernel(*refs):
    gp_refs = refs[:-6]
    w_ref, tok_ref, gr_ref, vec_ref, o_ref, sum_ref = refs[-6:]
    i = pl.program_id(0)
    w = tok_ref.shape[1]
    L = w // len(gp_refs)
    gp = [r[:, s * L : (s + 1) * L] for s in range(3) for r in gp_refs]
    grad = nt(jnp.concatenate(gp, axis=1), w_ref[...])
    hat, scale = row_norm(up(tok_ref[...]))
    o_ref[...] = rnd(gr_ref[...] + norm_back(grad, hat, scale, vec_ref[:, :w]))
    sums = jnp.concatenate(
        [jnp.sum(grad * hat, axis=0, keepdims=True), jnp.sum(grad, axis=0, keepdims=True)], axis=0
    )

    @pl.when(i == 0)
    def _():
        sum_ref[...] = jnp.zeros_like(sum_ref)

    sum_ref[0:2, :] += sums


def first_back(gps, weight, tokens, grad_resid, vec):
    n, w = tokens.shape
    rows = lambda c: pl.BlockSpec((QT, c), lambda i: (i, 0))
    whole = lambda a: pl.BlockSpec(a.shape, lambda i: (0, 0))
    return pl.pallas_call(
        first_back_kernel,
        name="first_back",
        grid=(n // QT,),
        in_specs=[rows(g.shape[1]) for g in gps] + [whole(weight), rows(w), rows(w), whole(vec)],
        out_specs=[rows(w), pl.BlockSpec((8, w), lambda i: (0, 0))],
        out_shape=[shaped((n, w), bf), shaped((8, w), f32)],
        compiler_params=params(),
        cost_estimate=cost(7e9, 1e7),
    )(*gps, weight, tokens, grad_resid, vec)


def over_dp(v, k):
    return lax.ppermute(v, "dp", [(i, i ^ k) for i in range(4)])


def over_core(v):
    return lax.ppermute(v, "fsdp", [(i, i ^ 1) for i in range(8)])


def over_z(v, k):
    return lax.ppermute(v, "fsdp", [(i, i ^ (2 * k)) for i in range(8)])


def spread_dp(v):
    return [v] + [over_dp(v, k) for k in (1, 2, 3)]


def spread_z(v):
    return [v] + [over_z(v, k) for k in (1, 2, 3)]


def pairs(v):
    return (v[0] + v[1]) + (v[2] + v[3])


def tie(*values):
    return lax.optimization_barrier(values)


def place():
    d = lax.axis_index("dp")
    f = lax.axis_index("fsdp")
    return d, f // 2, f % 2


def here():
    return jnp.stack(place()).astype(jnp.int32)


def by_index(got, at):
    rows = []
    for j in range(4):
        rel = lax.bitwise_xor(at, j)
        v = got[3]
        for k in (2, 1, 0):
            v = jnp.where(rel == k, got[k], v)
        rows.append(v)
    return rows


def quarter(shard, j):
    r, cols = shard.shape
    return lax.dynamic_slice(shard, (j * (r // 4), 0), (r // 4, cols))


def arrange_kernel(at, *refs):
    out = refs[-1]
    for side in (0, 1):
        for k in range(4):
            for s in range(4):
                column = lax.bitwise_xor(at[1], s) * 2 + lax.bitwise_xor(at[2], side)
                out[column * 4 + lax.bitwise_xor(at[0], k)] = refs[side * 4 + k][s]


def arrange(own, other):
    r, cols = own[0].shape[1:]
    B = cols // 3
    spec = pltpu.PrefetchScalarGridSpec(
        num_scalar_prefetch=1,
        grid=(3,),
        in_specs=[pl.BlockSpec((4, r, B), lambda j, a: (0, 0, j))] * 8,
        out_specs=pl.BlockSpec((32, r, B), lambda j, a: (0, 0, j)),
    )
    out = pl.pallas_call(
        arrange_kernel,
        name="arrange",
        grid_spec=spec,
        out_shape=shaped((32, r, cols), bf),
        compiler_params=params(),
        cost_estimate=cost(1e6, 4 * 32 * r * cols),
    )(here(), *own, *other)
    return out.reshape(32 * r, cols)


def fold_core_kernel(parts, extra, at, *refs):
    outs = refs[-4:]
    for k in range(4):
        col = 0
        for p in range(parts):
            a = refs[(k * parts + p) * 2][0, 0]
            b = refs[(k * parts + p) * 2 + 1][0, 0]
            w = a.shape[1]
            outs[k][0, :, col : col + w] = rnd(up(a) + up(b))
            col += w
        if extra and k:
            e = refs[8 * parts]
            v = e[0] if len(e.shape) == 3 else e[...]
            outs[k][0, :, col:] = v


def fold_core(mines, others, extra=None):
    r = mines[0].shape[1] // 4
    wide = sum(m.shape[2] for m in mines)
    more = 0
    args, specs = [], []
    for k in range(4):
        for m, o in zip(mines, others):
            for v in (m, o):
                w = v.shape[2]
                args.append(v.reshape(4, 4, r, w))
                specs.append(
                    pl.BlockSpec((1, 1, r, w), lambda j, a, k=k: (j, lax.bitwise_xor(a[0], k), 0, 0))
                )
    if extra is not None:
        args.append(extra)
        if extra.ndim == 3:
            more = extra.shape[2]
            specs.append(pl.BlockSpec((1, r, more), lambda j, a: (j, 0, 0)))
        else:
            more = extra.shape[1] // 4
            specs.append(pl.BlockSpec((r, more), lambda j, a: (0, j)))
    widths = [wide] + [wide + more] * 3
    spec = pltpu.PrefetchScalarGridSpec(
        num_scalar_prefetch=1,
        grid=(4,),
        in_specs=specs,
        out_specs=[pl.BlockSpec((1, r, w), lambda j, a: (j, 0, 0)) for w in widths],
    )
    return pl.pallas_call(
        partial(fold_core_kernel, len(mines), extra is not None),
        name="fold_core",
        grid_spec=spec,
        out_shape=[shaped((4, r, w), bf) for w in widths],
        compiler_params=params(),
        cost_estimate=cost(1e6, 48 * r * wide),
    )(here(), *args)


def fold_dp_kernel(at, *refs):
    ins, outs = refs[:-4], refs[-4:]
    w = outs[0].shape[1]
    for k in range(4):
        to = lax.bitwise_xor(at[1], k)
        total = up(ins[0][to])
        for g in ins[1:]:
            total = total + up(g[to][:, :w])
        outs[k][...] = rnd(total)


def fold_dp(own, got):
    whole = lambda v: pl.BlockSpec(v.shape, lambda j, a: (0, 0, 0))
    r, w = own.shape[1:]
    spec = pltpu.PrefetchScalarGridSpec(
        num_scalar_prefetch=1,
        grid=(1,),
        in_specs=[whole(v) for v in [own] + got],
        out_specs=[pl.BlockSpec((r, w), lambda j, a: (0, 0))] * 4,
    )
    return pl.pallas_call(
        fold_dp_kernel,
        name="fold_dp",
        grid_spec=spec,
        out_shape=[shaped((r, w), bf)] * 4,
        compiler_params=params(),
        cost_estimate=cost(1e6, 40 * r * w),
    )(here(), own, *got)


def pack_kernel(size, off, w, at, flat_ref, half_ref, *refs):
    ins, left, outs = refs[:4], refs[4:8], refs[8:]
    rows, wide = left[0].shape
    room = -(-size // 128) * 128
    for k in range(4):
        to = lax.bitwise_xor(at[1], k)
        outs[k][:rows, :wide] = left[k][...]
        outs[k][:rows, wide:] = rnd(pairs([up(g[to]) for g in ins]))
        outs[k][rows:, :] = jnp.zeros((1, outs[k].shape[1]), bf)
        mine = half_ref[:, pl.ds(pl.multiple_of(to * (2 * size), 128), size)]
        outs[k][rows:, :size] = rnd(mine)
        outs[k][rows:, room : room + w] = rnd(flat_ref[:, off : off + w])


def pack(flat, size, off, w, got, left):
    c = place()[2]
    half = lax.dynamic_slice(flat, (0, c * size), (1, 7 * size))
    r, cols = got[0].shape[1:]
    wide = left[0].shape[1] + cols
    whole = lambda v: pl.BlockSpec(v.shape, lambda j, a, n=v.ndim: (0,) * n)
    args = [flat, half, *got, *left]
    spec = pltpu.PrefetchScalarGridSpec(
        num_scalar_prefetch=1,
        grid=(1,),
        in_specs=[whole(v) for v in args],
        out_specs=[pl.BlockSpec((r + 1, wide), lambda j, a: (0, 0))] * 4,
    )
    return pl.pallas_call(
        partial(pack_kernel, size, off, w),
        name="pack",
        grid_spec=spec,
        out_shape=[shaped((r + 1, wide), bf)] * 4,
        compiler_params=params(),
        cost_estimate=cost(1e6, 40 * r * wide),
    )(here(), *args)


def fold_z(got):
    return rnd(pairs([up(g) for g in got]))


def adam_terms(grad, first, second, master, decay):
    first_new = 0.9 * first + 0.1 * grad
    second_new = 0.999 * second + 0.001 * grad * grad
    first_hat = first_new / (1.0 - 0.9**STEP)
    second_hat = second_new / (1.0 - 0.999**STEP)
    update = first_hat / (jnp.sqrt(second_hat) + 1e-06) + decay * master
    return (first_new, second_new, update)


def step_kernel(plan, base, at, *refs):
    j = pl.program_id(0)
    sources, refs = refs[:4], refs[4:]
    count = len(plan)
    states, outs, sum_ref = refs[: 3 * count], refs[3 * count : 7 * count], refs[7 * count]
    rel = lax.bitwise_xor(at[0], j)

    @pl.when(j == 0)
    def _():
        sum_ref[...] = jnp.zeros_like(sum_ref)

    for t, chunks in enumerate(plan):
        w_ref, m_ref, v_ref = states[3 * t : 3 * t + 3]
        g_out, m_out, v_out, u_out = outs[4 * t : 4 * t + 4]
        total = jnp.zeros((1, 1), f32)
        size = jnp.sum(w_ref[...] * w_ref[...], keepdims=True)
        for row, rows, col, cols, read in chunks:
            g = read(sources[3], 3)
            for k in (2, 1, 0):
                g = jnp.where(rel == k, read(sources[k], k), g)
            g = up(g)
            to = (slice(row, row + rows), slice(col, col + cols))
            first_new, second_new, update = adam_terms(g, m_ref[to], v_ref[to], w_ref[to], 0.01)
            g_out[to] = g
            m_out[to] = first_new
            v_out[to] = second_new
            u_out[to] = update
            total = total + jnp.sum(update * update, keepdims=True)
        sum_ref[base + t : base + t + 1, :] += jnp.broadcast_to(total, (1, 128))
        sum_ref[base + t + 4 : base + t + 5, :] += jnp.broadcast_to(size, (1, 128))


def step(plan, base, sources, states):
    whole = lambda v: pl.BlockSpec(v.shape, lambda j, a, n=v.ndim: (0,) * n)
    rows = lambda v: pl.BlockSpec((v.shape[0] // 4, v.shape[1]), lambda j, a: (j, 0))
    flat = [v for s in states for v in s]
    spec = pltpu.PrefetchScalarGridSpec(
        num_scalar_prefetch=1,
        grid=(4,),
        in_specs=[whole(v) for v in sources] + [rows(v) for v in flat],
        out_specs=[rows(s[0]) for s in states for _ in range(4)]
        + [pl.BlockSpec((8, 128), lambda j, a: (0, 0))],
    )
    out = pl.pallas_call(
        partial(step_kernel, plan, base),
        name="step",
        grid_spec=spec,
        out_shape=[shaped(s[0].shape, f32) for s in states for _ in range(4)]
        + [shaped((8, 128), f32)],
        compiler_params=params(),
        cost_estimate=cost(1e6, 28 * sum(s[0].size for s in states)),
    )(here(), *sources, *flat)
    return [out[4 * t : 4 * t + 4] for t in range(len(states))], out[-1]


def finish_kernel(*refs):
    parts = [r[...] for r in refs[:4]]
    refs = refs[4:]
    norms = jnp.sqrt(pairs(parts))
    refs[12][...] = norms
    for t in range(4):
        factor = 0.3 * (norms[t + 4 : t + 5, 0:1] / (norms[t : t + 1, 0:1] + 1e-06))
        refs[8 + t][...] = refs[t][...] - factor * refs[4 + t][...]


def finish(masters, updates, parts):
    rows = lambda v: pl.BlockSpec((v.shape[0] // 4, v.shape[1]), lambda j: (j, 0))
    whole = lambda: pl.BlockSpec((8, 128), lambda j: (0, 0))
    out = pl.pallas_call(
        finish_kernel,
        name="finish",
        grid=(4,),
        in_specs=[whole() for _ in parts] + [rows(v) for v in masters + updates],
        out_specs=[rows(v) for v in masters] + [whole()],
        out_shape=[shaped(v.shape, f32) for v in masters] + [shaped((8, 128), f32)],
        compiler_params=params(),
        cost_estimate=cost(1e6, 12 * sum(v.size for v in masters)),
    )(*parts, *masters, *updates)
    return out[:4], out[4]


def body(fast, tokens, cotangent, image_ids, patch_grid, *state):
    masters, vectors = state[:4], state[4]
    firsts, vector_first = state[5:9], state[9]
    seconds, vector_second = state[10:14], state[14]
    n, w = tokens.shape
    size = vectors.shape[0]
    heads = w // HD
    count = w // 128 // PAIRS
    L = 128 * PAIRS
    low = [rnd(m) for m in masters]
    gather = lambda v: lax.all_gather(v, "fsdp", axis=0, tiled=True)
    scatter = lambda v: lax.psum_scatter(v, "fsdp", scatter_dimension=0, tiled=True)
    whole = jnp.zeros((1,), jnp.int32)
    d, z, c = place()
    mine = jnp.stack([c]).astype(jnp.int32)
    halves = lambda x_t, y: (outer(x_t, y, 1 - mine, 4, 2), outer(x_t, y, mine, 4, 2))
    join = lambda rows: jnp.concatenate(rows, axis=-1)

    if fast:
        q_rows = low[0].shape[0] // 4
        row = jnp.pad(rnd(vectors), (0, low[0].shape[1] - size)).reshape(1, -1)
        got = spread_z(jnp.concatenate([quarter(low[0], d), row], 0))
        qkv_column = jnp.stack([g[:q_rows] for g in got])
        packed = jnp.concatenate(by_index([g[q_rows:, :size] for g in got], z), 0)
        other = over_core(packed)
        packed = jnp.stack([jnp.where(c == 0, packed, other), jnp.where(c == 0, other, packed)], 1)
        packed = packed.reshape(-1)
        up_part, out_part, down_part, qkv_column = tie(
            quarter(low[2], d), low[1], low[3], qkv_column
        )
        full_out = gather(out_part)
        qkv_own = spread_dp(qkv_column)
        up_column = jnp.stack(spread_z(up_part))
        full_down = gather(down_part)
    else:
        packed = gather(rnd(vectors))
        full_qkv, full_out, full_up, full_down = [gather(v) for v in low]
    vec = up(packed).reshape(1, -1)
    freq = vec[0, -w:].reshape(2, heads, 1, HD // 2)
    freq = jnp.broadcast_to(freq, (2, heads, 2, HD // 2)).reshape(2, w)
    grid_t = up(patch_grid.T)
    given = jnp.where((image_ids >= 0)[:, None], cotangent, jnp.zeros_like(cotangent))
    grad_bias_down = jnp.sum(up(given), axis=0, keepdims=True)
    aug_q, aug_k, rng = tables(image_ids)

    normed, normed_t, cos, sin = first(tokens, vec, freq, grid_t)
    if fast:
        normed, *qkv_own = tie(normed, *qkv_own)
        full_qkv = arrange(qkv_own, [over_core(v) for v in qkv_own])
        up_column, full_qkv = tie(up_column, full_qkv)
        up_own = spread_dp(up_column)
    qkv = project(normed, full_qkv, vec, cos, sin)
    mix, mix_t, lb = attend(qkv, aug_q, aug_k, rng)
    if fast:
        mix, *up_own = tie(mix, *up_own)
        up_other = [over_core(v) for v in up_own]
    resid, normed_two, normed_two_t = branch(tokens, mix, full_out, vec)
    if fast:
        full_up = arrange(up_own, up_other)
    active, active_t, slope = hidden_units(normed_two, full_up, vec)
    if fast:
        theirs, own = halves(active_t, given)
        pieces = fold_core([own], [over_core(theirs)])
        active, slope, full_down = tie(active, slope, full_down)
        active, slope, *pieces = tie(active, slope, *pieces)
        got = [over_dp(v, k) for k, v in zip((1, 2, 3), pieces[1:])]
    else:
        down_full = outer(active_t, given, whole, 1, 1)[0]
    output = last(active, full_down, resid, vec)
    grad_hidden, grad_bias_up = hidden_back(given, full_down, slope)
    if fast:
        output, grad_hidden, *got = tie(output, grad_hidden, *got)
        down_z = fold_dp(pieces[0], got)
        grad_hidden, *down_z = tie(grad_hidden, *down_z)
        got = [down_z[0]] + [over_z(v, k) for k, v in zip((1, 2, 3), down_z[1:])]
        theirs, own = halves(normed_two_t, grad_hidden)
        own, *got = tie(own, *got)
        down_f = fold_z(got)
        more = down_f.reshape(4, -1, w)
        pieces = fold_core([own], [over_core(theirs)], more)
        grad_hidden, down_f, *pieces = tie(grad_hidden, down_f, *pieces)
        got = [over_dp(v, k) for k, v in zip((1, 2, 3), pieces[1:])]
    else:
        up_full = outer(normed_two_t, grad_hidden, whole, 1, 1)[0]
    grad_resid, grad_branch, grad_mix, sums_two = second_back(
        grad_hidden, full_up, resid, given, vec, full_out
    )
    if fast:
        out_theirs, out_own = halves(mix_t, grad_branch)
        out_sent = over_core(out_theirs)
    else:
        out_full = outer(mix_t, grad_branch, whole, 1, 1)[0]
    projs, sums_proj, sums_freq, qkv_parts = [], [], [], []
    for part in range(count):
        dq, dk, dv = attend_back(part, qkv, grad_mix, mix, lb, aug_q, aug_k, rng)
        if fast and part == 0:
            dq, *got = tie(dq, *got)
            up_width = pieces[0].shape[2]
            q = down_f.shape[0] // 4

            def read_down(i, q, skip, ref, k):
                return ref[i, :, skip:] if k else ref[q * i : q * i + q]

            plan = [[(q * i, q, 0, w, partial(read_down, i, q, up_width)) for i in range(4)]]
            later = [(plan, [down_f] + got, (masters[3], firsts[3], seconds[3]))]
            up_z = fold_dp(pieces[0], got)
            dq, *up_z = tie(dq, *up_z)
            got = [up_z[0]] + [over_z(v, k) for k, v in zip((1, 2, 3), up_z[1:])]
        if fast and part > 0:
            dq, *got = tie(dq, *got)
        gp, bs, fs = turn_back(part, dq, dk, dv, qkv, cos, sin, grid_t)
        projs.append(gp)
        sums_proj.append(bs)
        sums_freq.append(fs)
        if not fast:
            qkv_parts.append(outer(normed_t, gp, whole, 1, 1)[0])
        elif part == 0:
            theirs, own = halves(normed_t, gp)
            own, *got = tie(own, *got)
            up_f = fold_z(got)
            pieces = fold_core([own, out_own], [over_core(theirs), out_sent], up_f)
            grad_mix, up_f, *pieces = tie(grad_mix, up_f, *pieces)
            got = [over_dp(v, k) for k, v in zip((1, 2, 3), pieces[1:])]
        else:
            a_width = pieces[0].shape[2]
            q, wide = up_f.shape[0], up_f.shape[1] // 4

            def read_up(i, wide, skip, ref, k):
                return ref[i, :, skip:] if k else ref[:, wide * i : wide * i + wide]

            plan = [
                [(0, q, wide * i, wide, partial(read_up, i, wide, a_width)) for i in range(4)]
            ]
            later.append((plan, [up_f] + got, (masters[2], firsts[2], seconds[2])))
            theirs, own = halves(normed_t, gp)
            a_z = fold_dp(pieces[0], got)
            pieces = fold_core([own], [over_core(theirs)])
            projs[-1], *pieces = tie(gp, *pieces)
            got = [over_dp(v, k) for k, v in zip((1, 2, 3), pieces[1:])]
    tokens_grad, sums_one = first_back(projs, full_qkv, tokens, grad_resid, vec)
    if fast:
        sums_one, *got = tie(sums_one, *got)
    freq_sums = join([s[:2] for s in sums_freq]).reshape(2, heads, 2, HD // 2)
    vector_full = join(
        [
            sums_one[0:1],
            sums_one[1:2],
            sums_two[0:1],
            sums_two[1:2],
            *[s[i : i + 1] for i in range(3) for s in sums_proj],
            sums_two[2:3],
            grad_bias_up,
            grad_bias_down,
            (freq_sums[:, :, 0] - freq_sums[:, :, 1]).reshape(1, -1),
        ]
    )
    off = vector_full.shape[1] - 2 * w
    if fast:
        flat = vector_full + over_core(vector_full)
        sends = pack(flat, size, off, w, [pieces[0]] + got, a_z)
        got = [sends[0]] + [over_z(s, k) for k, s in zip((1, 2, 3), sends[1:])]
        held = tie(*[v for entry in later for v in entry[1]], *sends)
        (down_step, down_square), (up_step, up_square) = [
            step(entry[0], 3 - i, list(held[4 * i : 4 * i + 4]), [entry[2]])
            for i, entry in enumerate(later)
        ]
        up_square, down_square, *got = tie(up_square, down_square, *got)
        got = spread_dp(rnd(pairs([up(g) for g in got])))
        tail = pairs([up(g[q_rows:]) for g in got])[0]
        room = -(-size // 128) * 128
        vector_grad = tail[:size]
        down_bias_grad = tail[room : room + w]

        def read(col, ref, k):
            return ref[:q_rows, col : col + L]

        plan = [
            [
                (0, q_rows, (s * count + p) * L, L, partial(read, p * (3 * L + w) + s * L))
                for p in range(count)
                for s in range(3)
            ],
            [(0, q_rows, i * L, L, partial(read, 3 * L + i * L)) for i in range(w // L)],
        ]
        states = [(masters[k], firsts[k], seconds[k]) for k in (0, 1)]
        last_steps, last_squares = step(plan, 0, got, states)
        steps = last_steps + up_step + down_step
        squares = last_squares + up_square + down_square
        squares = spread_z(squares + over_core(squares))
        new_list, norms = finish(list(masters), [s[3] for s in steps], squares)
        update_norms, weight_norms = norms[:4, 0], norms[4:, 0]
    else:
        give = lambda v: lax.psum(scatter(up(v)), "dp")
        up_grad, down_grad, out_grad = give(up_full), give(down_full), give(out_full)
        done = [give(v) for v in qkv_parts]
        vector_grad = give(vector_full[0])
        down_bias_grad = lax.psum(grad_bias_down[0], ("dp", "fsdp"))
        qkv_grad = join([g[:, s * L : (s + 1) * L] for s in range(3) for g in done])
        steps = [
            (g, *adam_terms(g, firsts[k], seconds[k], masters[k], 0.01))
            for k, g in enumerate((qkv_grad, out_grad, up_grad, down_grad))
        ]
        weight_local = jnp.stack([jnp.sum(m * m) for m in masters])
        update_local = jnp.stack([jnp.sum(s[3] * s[3]) for s in steps])
        both = jnp.sqrt(lax.psum(jnp.stack([weight_local, update_local]), "fsdp"))
        weight_norms, update_norms = both[0], both[1]
        factor = 0.3 * (weight_norms / (update_norms + 1e-06))
        new_list = [masters[k] - factor[k] * steps[k][3] for k in range(4)]
    vector_step = adam_terms(vector_grad, vector_first, vector_second, vectors, 0.0)
    return (
        output,
        tokens_grad,
        *[s[0] for s in steps],
        vector_grad,
        down_bias_grad,
        *[s[1] for s in steps],
        vector_step[0],
        *[s[2] for s in steps],
        vector_step[1],
        *new_list,
        vectors - 0.2 * vector_step[2],
        weight_norms,
        update_norms,
    )


def solution(mesh):
    both = P(("dp", "fsdp"), None)
    mat = [P("fsdp", None)] * 4 + [P("fsdp")]
    in_specs = (both, both, P(("dp", "fsdp")), P(None, ("dp", "fsdp")), *mat, *mat, *mat)
    out_specs = (both, both, *mat, P(), *mat, *mat, *mat, P(), P())
    fast = mesh.shape["dp"] == 4 and mesh.shape["fsdp"] == 8
    return jax.shard_map(
        partial(body, fast), mesh=mesh, in_specs=in_specs, out_specs=out_specs, check_vma=False
    )
```

```python
from functools import partial

import jax
import jax.numpy as jnp
from jax import lax
from jax.experimental import pallas as pl
from jax.experimental.pallas import tpu as pltpu
from jax.sharding import PartitionSpec as P

H = 12
HD = 64
STEP = 10
QT = 256
KT = 128
PAIRS = 3
VARIANTS = (2, 3, 4, 5, 7, 8)
norm_eps = 1e-06
bf = jnp.bfloat16
f32 = jnp.float32


def nt(a, b):
    return lax.dot_general(a, b, (((1,), (1,)), ((), ())), preferred_element_type=f32)


def nn(a, b):
    return lax.dot_general(a, b, (((1,), (0,)), ((), ())), preferred_element_type=f32)


def rnd(v):
    return v.astype(bf)


def up(v):
    return v.astype(f32)


def params(mib=22):
    return pltpu.CompilerParams(vmem_limit_bytes=mib << 20)


def cost(flops, moved):
    return pl.CostEstimate(flops=int(flops), bytes_accessed=int(moved), transcendentals=0)


def shaped(shape, kind):
    return jax.ShapeDtypeStruct(shape, kind)


def row_norm(v):
    centre = jnp.mean(v, axis=-1, keepdims=True)
    centred = v - centre
    spread = jnp.mean(centred * centred, axis=-1, keepdims=True)
    scale = lax.rsqrt(spread + norm_eps)
    return centred * scale, scale


def split3(x):
    a = rnd(x)
    r = x - up(a)
    b = rnd(r)
    return jnp.concatenate([a, b, rnd(r - up(b))], axis=0)


def first_kernel(tok_ref, vec_ref, freq_ref, grid_ref, n_ref, nt_ref, cos_ref, sin_ref, table):
    w = tok_ref.shape[1]

    @pl.when(pl.program_id(0) == 0)
    def _():
        place_of = lax.broadcasted_iota(jnp.int32, (32, w), 0).astype(f32)
        for axis in (0, 1):
            angle = place_of * freq_ref[axis : axis + 1, :]
            table[2 * axis] = split3(jnp.cos(angle))
            table[2 * axis + 1] = split3(jnp.sin(angle))

    hat, scale = row_norm(up(tok_ref[...]))
    normed = hat * vec_ref[:, :w] + vec_ref[:, w : 2 * w]
    n_ref[...] = rnd(normed)
    nt_ref[...] = rnd(normed.T)
    g = grid_ref[...]
    index = lax.broadcasted_iota(jnp.int32, (1, 96), 1) & 31
    hot = [rnd(jnp.where(g[:, axis : axis + 1] == index, 1.0, 0.0)) for axis in (0, 1)]
    cos_row, sin_row = nn(hot[0], table[0]), nn(hot[0], table[1])
    cos_col, sin_col = nn(hot[1], table[2]), nn(hot[1], table[3])
    lane = lax.broadcasted_iota(jnp.int32, (1, w), 1)
    cos_ref[...] = cos_row * cos_col - sin_row * sin_col
    s = sin_row * cos_col + cos_row * sin_col
    sin_ref[...] = jnp.where(lane & 63 < 32, -s, s)


def first(tokens, vec, freq, grid_t):
    n, w = tokens.shape
    rows = lambda: pl.BlockSpec((QT, w), lambda i: (i, 0))
    whole = lambda a: pl.BlockSpec(a.shape, lambda i: (0, 0))
    return pl.pallas_call(
        first_kernel,
        name="first",
        grid=(n // QT,),
        in_specs=[rows(), whole(vec), whole(freq), pl.BlockSpec((QT, 2), lambda i: (i, 0))],
        out_specs=[rows(), pl.BlockSpec((w, QT), lambda i: (0, i)), rows(), rows()],
        out_shape=[shaped((n, w), bf), shaped((w, n), bf), shaped((n, w), f32), shaped((n, w), f32)],
        scratch_shapes=[pltpu.VMEM((4, 96, w), bf)],
        compiler_params=params(),
        cost_estimate=cost(5e9, 1e7),
    )(tokens, vec, freq, grid_t)


def swap(v):
    w = v.shape[1]
    lane = lax.broadcasted_iota(jnp.int32, (1, w), 1)
    return jnp.where(lane & 63 < 32, pltpu.roll(v, w - 32, 1), pltpu.roll(v, 32, 1))


def project_kernel(n_ref, w_ref, b_ref, cos_ref, sin_ref, o_ref):
    j = pl.program_id(0)
    u = nn(n_ref[...], w_ref[...]) + b_ref[...]

    @pl.when(j < 2)
    def _():
        turned = u * cos_ref[...] + swap(u) * sin_ref[...]
        o_ref[...] = rnd(turned * jnp.where(j < 1, 0.125, 1.0))

    @pl.when(j >= 2)
    def _():
        o_ref[...] = rnd(u)


def project(normed, weight, vec, cos, sin):
    n, w = normed.shape
    whole = lambda: pl.BlockSpec((n, w), lambda j: (0, 0))
    return pl.pallas_call(
        project_kernel,
        name="project",
        grid=(3,),
        in_specs=[
            whole(),
            pl.BlockSpec((w, w), lambda j: (0, j)),
            pl.BlockSpec((1, w), lambda j: (0, 4 + j)),
            whole(),
            whole(),
        ],
        out_specs=pl.BlockSpec((n, w), lambda j: (0, j)),
        out_shape=shaped((n, 3 * w), bf),
        compiler_params=params(22),
        cost_estimate=cost(8e9, 1e7),
    )(normed, weight, vec, cos, sin)


def tables(ids):
    n = ids.shape[0]
    lane = jnp.arange(128) & 63
    one = (ids[:, None] + 1 == lane[None]).astype(f32)
    small = (lane < 8)[None]
    aug_q = rnd(jnp.where(small, one, 0.0))
    aug_k = rnd(jnp.where(small, (one - 1.0) * 1e30, jnp.where((lane < 11)[None], 1.0, 0.0)))
    tiles = n // QT
    hit = (ids.reshape(tiles, QT, 1) == ids[None, None, :]).any(1)
    pos = jnp.arange(n)[None]
    lo = jnp.min(jnp.where(hit, pos, n), 1) // KT
    hi = jnp.max(jnp.where(hit, pos, -1), 1) // KT + 1
    need = hi - lo
    width = jnp.full_like(need, VARIANTS[-1])
    for v in VARIANTS[::-1]:
        width = jnp.where(need <= v, v, width)
    start = jnp.minimum(lo, n // KT - width)
    return aug_q, aug_k, jnp.stack([start, width]).astype(jnp.int32)


def low_lanes():
    return lax.broadcasted_iota(jnp.int32, (1, 128), 1) < 64


def attend_kernel(rng, q_ref, k_ref, v_ref, aq_ref, ak_ref, mix_ref, mixt_ref, lb_ref, vt):
    i = pl.program_id(1)
    n = k_ref.shape[0]
    start = rng[0, i]
    width = rng[1, i]
    low = low_lanes()

    @pl.when(i == 0)
    def _():
        one = jnp.ones((16, n), bf)
        for p in range(PAIRS):
            t = v_ref[:, 128 * p : 128 * p + 128].T
            for h in (0, 1):
                vt[2 * p + h, :64, :] = t[64 * h : 64 * h + 64]
                vt[2 * p + h, 64:, :] = one

    aq = aq_ref[...]
    for W in VARIANTS:

        @pl.when(width == W)
        def _():
            at = pl.ds(pl.multiple_of(start * KT, KT), W * KT)
            ak = ak_ref[at, :]
            scores = []
            for p in range(PAIRS):
                c = slice(128 * p, 128 * p + 128)
                q = q_ref[:, c]
                k = k_ref[at, c]
                scores.append(nt(jnp.where(low, k, ak), jnp.where(low, q, aq)))
                scores.append(nt(jnp.where(low, ak, k), jnp.where(low, aq, q)))
            for p in range(PAIRS):
                c = slice(128 * p, 128 * p + 128)
                outs = []
                for h in (0, 1):
                    s = scores[2 * p + h]
                    m = jnp.max(s, axis=0, keepdims=True)
                    e = rnd(jnp.exp(s - m))
                    o = nn(vt[2 * p + h, :, at], e)
                    t = o[64:65]
                    outs.append(o[:64] * (1.0 / t))
                    lb_ref[p, h : h + 1, :] = m + jnp.log(t)
                both = jnp.concatenate(outs, 0)
                mix_ref[:, c] = rnd(both.T)
                mixt_ref[c, :] = rnd(both)


def attend(qkv, aug_q, aug_k, rng):
    n, w3 = qkv.shape
    w = w3 // 3
    L = 128 * PAIRS
    g = w // L
    spec = pltpu.PrefetchScalarGridSpec(
        num_scalar_prefetch=1,
        grid=(g, n // QT),
        in_specs=[
            pl.BlockSpec((QT, L), lambda p, i, r: (i, p)),
            pl.BlockSpec((n, L), lambda p, i, r: (0, g + p)),
            pl.BlockSpec((n, L), lambda p, i, r: (0, 2 * g + p)),
            pl.BlockSpec((QT, 128), lambda p, i, r: (i, 0)),
            pl.BlockSpec((n, 128), lambda p, i, r: (0, 0)),
        ],
        out_specs=[
            pl.BlockSpec((QT, L), lambda p, i, r: (i, p)),
            pl.BlockSpec((L, QT), lambda p, i, r: (p, i)),
            pl.BlockSpec((PAIRS, 8, QT), lambda p, i, r: (p, 0, i)),
        ],
        scratch_shapes=[pltpu.VMEM((2 * PAIRS, 80, n), bf)],
    )
    return pl.pallas_call(
        attend_kernel,
        name="attend",
        grid_spec=spec,
        out_shape=[shaped((n, w), bf), shaped((w, n), bf), shaped((w // 128, 8, n), f32)],
        compiler_params=params(),
        cost_estimate=cost(2.3e10, 1e7),
    )(rng, qkv, qkv, qkv, aug_q, aug_k)


def fill(aug, x):
    lane = lax.broadcasted_iota(jnp.int32, (1, 128), 1) & 63
    a = rnd(x)
    r = x - up(a)
    b = rnd(r)
    c = rnd(r - up(b))
    return jnp.where(lane == 8, a, jnp.where(lane == 9, b, jnp.where(lane == 10, c, aug)))


def attend_back_kernel(
    rng, q_ref, k_ref, v_ref, g_ref, mix_ref, lb_ref, aq_ref, ak_ref,
    dq_ref, dk_ref, dv_ref, dk_acc, dv_acc,
):
    i = pl.program_id(0)
    start = rng[0, i]
    width = rng[1, i]

    @pl.when(i == 0)
    def _():
        dk_acc[...] = jnp.zeros_like(dk_acc)
        dv_acc[...] = jnp.zeros_like(dv_acc)

    low = low_lanes()
    aq0 = aq_ref[...]
    zero = jnp.zeros((1, 128), bf)
    held = []
    for p in range(PAIRS):
        c = slice(128 * p, 128 * p + 128)
        q = q_ref[:, c]
        g = g_ref[:, c]
        prod = up(g) * up(mix_ref[:, c])
        even = jnp.sum(jnp.where(low, prod, 0.0), axis=1, keepdims=True)
        odd = jnp.sum(jnp.where(low, 0.0, prod), axis=1, keepdims=True)
        lt = lb_ref[p].T
        aq = fill(aq0, -jnp.where(low, lt[:, 1:2], lt[:, 0:1]))
        ag = fill(zero, -jnp.where(low, odd, even))
        held.append(
            (
                (jnp.where(low, q, aq), jnp.where(low, aq, q)),
                (jnp.where(low, g, ag), jnp.where(low, ag, g)),
                q.T,
                g.T,
            )
        )
    for W in VARIANTS:

        @pl.when(width == W)
        def _():
            at = pl.ds(pl.multiple_of(start * KT, KT), W * KT)
            ak = ak_ref[at, :]
            for p in range(PAIRS):
                c = slice(128 * p, 128 * p + 128)
                qs, gs, qt, gt = held[p]
                k = k_ref[at, c]
                v = v_ref[at, c]
                one = jnp.ones_like(v)
                ks = (jnp.where(low, k, ak), jnp.where(low, ak, k))
                vs = (jnp.where(low, v, one), jnp.where(low, one, v))
                dqs = []
                for h in (0, 1):
                    e = jnp.exp(nt(qs[h], ks[h]))
                    ds = rnd(e * nt(gs[h], vs[h]))
                    e = rnd(e)
                    half = slice(64 * h, 64 * h + 64)
                    to = slice(128 * p + 64 * h, 128 * p + 64 * h + 64)
                    dqs.append(nn(ds, k))
                    dk_acc[to, at] += nn(qt[half], ds)
                    dv_acc[to, at] += nn(gt[half], e)
                dq_ref[:, c] = jnp.where(low, dqs[0], dqs[1]) * 0.125

    @pl.when(i == pl.num_programs(0) - 1)
    def _():
        dk_ref[...] = dk_acc[...].T
        dv_ref[...] = rnd(dv_acc[...].T)


def attend_back(part, qkv, g_mix, mix, lb, aug_q, aug_k, rng):
    n, w3 = qkv.shape
    L = 128 * PAIRS
    g = w3 // 3 // L
    spec = pltpu.PrefetchScalarGridSpec(
        num_scalar_prefetch=1,
        grid=(n // QT,),
        in_specs=[
            pl.BlockSpec((QT, L), lambda i, r: (i, part)),
            pl.BlockSpec((n, L), lambda i, r: (0, g + part)),
            pl.BlockSpec((n, L), lambda i, r: (0, 2 * g + part)),
            pl.BlockSpec((QT, L), lambda i, r: (i, part)),
            pl.BlockSpec((QT, L), lambda i, r: (i, part)),
            pl.BlockSpec((PAIRS, 8, QT), lambda i, r: (part, 0, i)),
            pl.BlockSpec((QT, 128), lambda i, r: (i, 0)),
            pl.BlockSpec((n, 128), lambda i, r: (0, 0)),
        ],
        out_specs=[
            pl.BlockSpec((QT, L), lambda i, r: (i, 0)),
            pl.BlockSpec((n, L), lambda i, r: (0, 0)),
            pl.BlockSpec((n, L), lambda i, r: (0, 0)),
        ],
        scratch_shapes=[pltpu.VMEM((L, n), f32), pltpu.VMEM((L, n), f32)],
    )
    return pl.pallas_call(
        attend_back_kernel,
        name="attend_back",
        grid_spec=spec,
        out_shape=[shaped((n, L), f32), shaped((n, L), f32), shaped((n, L), bf)],
        compiler_params=params(),
        cost_estimate=cost(2.2e10, 1e7),
    )(rng, qkv, qkv, qkv, g_mix, mix, lb, aug_q, aug_k)


def branch_kernel(tok_ref, mix_ref, w_ref, vec_ref, res_ref, n_ref, nt_ref):
    w = tok_ref.shape[1]
    resid = up(tok_ref[...]) + nn(mix_ref[...], w_ref[...]) + vec_ref[:, 7 * w : 8 * w]
    res_ref[...] = resid
    hat, scale = row_norm(resid)
    normed = hat * vec_ref[:, 2 * w : 3 * w] + vec_ref[:, 3 * w : 4 * w]
    n_ref[...] = rnd(normed)
    nt_ref[...] = rnd(normed.T)


def branch(tokens, mix, weight, vec):
    n, w = tokens.shape
    rows = lambda: pl.BlockSpec((QT, w), lambda i: (i, 0))
    whole = lambda a: pl.BlockSpec(a.shape, lambda i: (0, 0))
    return pl.pallas_call(
        branch_kernel,
        name="branch",
        grid=(n // QT,),
        in_specs=[rows(), rows(), whole(weight), whole(vec)],
        out_specs=[rows(), rows(), pl.BlockSpec((w, QT), lambda i: (0, i))],
        out_shape=[shaped((n, w), f32), shaped((n, w), bf), shaped((w, n), bf)],
        compiler_params=params(22),
        cost_estimate=cost(4e9, 1e7),
    )(tokens, mix, weight, vec)


def gelu_parts(x):
    cdf = 0.5 + 0.5 * lax.erf(x * 0.7071067811865476)
    return x * cdf, cdf + x * (jnp.exp(x * x * -0.5) * 0.3989422804014327)


def hidden_kernel(n_ref, w_ref, b_ref, a_ref, at_ref, d_ref):
    x = nn(n_ref[...], w_ref[...]) + b_ref[...]
    active, slope = gelu_parts(x)
    active = rnd(active)
    a_ref[...] = active
    at_ref[...] = active.T
    d_ref[...] = rnd(slope)


def hidden_units(normed, weight, vec):
    n, w = normed.shape
    ff = weight.shape[1]
    B = 768
    off = 8 * w // B
    return pl.pallas_call(
        hidden_kernel,
        name="hidden",
        grid=(ff // B,),
        in_specs=[
            pl.BlockSpec((n, w), lambda j: (0, 0)),
            pl.BlockSpec((w, B), lambda j: (0, j)),
            pl.BlockSpec((1, B), lambda j: (0, off + j)),
        ],
        out_specs=[
            pl.BlockSpec((n, B), lambda j: (0, j)),
            pl.BlockSpec((B, n), lambda j: (j, 0)),
            pl.BlockSpec((n, B), lambda j: (0, j)),
        ],
        out_shape=[shaped((n, ff), bf), shaped((ff, n), bf), shaped((n, ff), bf)],
        compiler_params=params(30),
        cost_estimate=cost(1.5e10, 1e7),
    )(normed, weight, vec)


def last_kernel(a_ref, w_ref, res_ref, b_ref, o_ref):
    o_ref[...] = rnd(res_ref[...] + nn(a_ref[...], w_ref[...]) + b_ref[...])


def last(active, weight, resid, vec):
    n, ff = active.shape
    w = resid.shape[1]
    off = (8 * w + ff) // w
    return pl.pallas_call(
        last_kernel,
        name="last",
        grid=(n // QT,),
        in_specs=[
            pl.BlockSpec((QT, ff), lambda i: (i, 0)),
            pl.BlockSpec((ff, w), lambda i: (0, 0)),
            pl.BlockSpec((QT, w), lambda i: (i, 0)),
            pl.BlockSpec((1, w), lambda i: (0, off)),
        ],
        out_specs=pl.BlockSpec((QT, w), lambda i: (i, 0)),
        out_shape=shaped((n, w), bf),
        compiler_params=params(),
        cost_estimate=cost(6e9, 1e7),
    )(active, weight, resid, vec)


def hidden_back_kernel(g_ref, w_ref, d_ref, gh_ref, sum_ref):
    gh = rnd(nt(g_ref[...], w_ref[...]) * up(d_ref[...]))
    gh_ref[...] = gh
    sum_ref[...] = jnp.sum(up(gh), axis=0, keepdims=True)


def hidden_back(given, weight, slope):
    n, w = given.shape
    ff = weight.shape[0]
    B = 768
    return pl.pallas_call(
        hidden_back_kernel,
        name="hidden_back",
        grid=(ff // B,),
        in_specs=[
            pl.BlockSpec((n, w), lambda j: (0, 0)),
            pl.BlockSpec((B, w), lambda j: (j, 0)),
            pl.BlockSpec((n, B), lambda j: (0, j)),
        ],
        out_specs=[pl.BlockSpec((n, B), lambda j: (0, j)), pl.BlockSpec((1, B), lambda j: (0, j))],
        out_shape=[shaped((n, ff), bf), shaped((1, ff), f32)],
        compiler_params=params(),
        cost_estimate=cost(8e9, 1e7),
    )(given, weight, slope)


def norm_back(grad, hat, scale, gain):
    d = grad * gain
    a = jnp.mean(d, axis=-1, keepdims=True)
    b = jnp.mean(d * hat, axis=-1, keepdims=True)
    return (d - a - hat * b) * scale


def second_back_kernel(gh_ref, w_ref, res_ref, cot_ref, vec_ref, wo_ref, gr_ref, gb_ref, gm_ref, sum_ref):
    i = pl.program_id(0)
    w = res_ref.shape[1]
    grad = nt(gh_ref[...], w_ref[...])
    hat, scale = row_norm(res_ref[...])
    total = up(cot_ref[...]) + norm_back(grad, hat, scale, vec_ref[:, 2 * w : 3 * w])
    gr_ref[...] = total
    low = rnd(total)
    gb_ref[...] = low
    gm_ref[...] = rnd(nt(low, wo_ref[...]))
    sums = jnp.concatenate(
        [
            jnp.sum(grad * hat, axis=0, keepdims=True),
            jnp.sum(grad, axis=0, keepdims=True),
            jnp.sum(up(low), axis=0, keepdims=True),
        ],
        axis=0,
    )

    @pl.when(i == 0)
    def _():
        sum_ref[...] = jnp.zeros_like(sum_ref)

    sum_ref[0:3, :] += sums


def second_back(gh, weight, resid, given, vec, out_w):
    n, ff = gh.shape
    w = resid.shape[1]
    rows = lambda c: pl.BlockSpec((QT, c), lambda i: (i, 0))
    whole = lambda a: pl.BlockSpec(a.shape, lambda i: (0, 0))
    return pl.pallas_call(
        second_back_kernel,
        name="second_back",
        grid=(n // QT,),
        in_specs=[rows(ff), whole(weight), rows(w), rows(w), whole(vec), whole(out_w)],
        out_specs=[rows(w), rows(w), rows(w), pl.BlockSpec((8, w), lambda i: (0, 0))],
        out_shape=[shaped((n, w), f32), shaped((n, w), bf), shaped((n, w), bf), shaped((8, w), f32)],
        compiler_params=params(),
        cost_estimate=cost(9e9, 1e7),
    )(gh, weight, resid, given, vec, out_w)


def outer_kernel(sel, x_ref, y_ref, o_ref):
    z, one, r, n = x_ref.shape
    got = nn(x_ref[...].reshape(z * r, n), y_ref[...])
    o_ref[...] = rnd(got).reshape(o_ref.shape)


def outer(x_t, y, sel, groups, share):
    rows, n = x_t.shape
    c = y.shape[1]
    r = rows // (groups * share)
    B = 768 if c % 768 == 0 else 384 if c % 384 == 0 else 256
    spec = pltpu.PrefetchScalarGridSpec(
        num_scalar_prefetch=1,
        grid=(c // B,),
        in_specs=[
            pl.BlockSpec((groups, 1, r, n), lambda j, s: (0, s[0], 0, 0)),
            pl.BlockSpec((n, B), lambda j, s: (0, j)),
        ],
        out_specs=pl.BlockSpec((groups, r, B), lambda j, s: (0, 0, j)),
    )
    return pl.pallas_call(
        outer_kernel,
        name="outer",
        grid_spec=spec,
        out_shape=shaped((groups, r, c), bf),
        compiler_params=params(),
        cost_estimate=cost(4 * groups * r * c * n, 1e7),
    )(sel, x_t.reshape(groups, share, r, n), y)


def turn_back_kernel(
    dq_ref, dk_ref, dv_ref, q_ref, k_ref, cos_ref, sin_ref, grid_ref, gp_ref, b_ref, f_ref
):
    i = pl.program_id(0)
    w = cos_ref.shape[1]
    cos = cos_ref[...]
    sin = sin_ref[...]
    dq = dq_ref[...]
    dk = dk_ref[...]
    gv = dv_ref[...]
    sq = swap(dq)
    sk = swap(dk)
    t = sq * (up(q_ref[...]) * 8.0) + sk * up(k_ref[...])
    g = up(grid_ref[...])
    gq = rnd(dq * cos - sq * sin)
    gk = rnd(dk * cos - sk * sin)
    gp_ref[:, :w] = gq
    gp_ref[:, w : 2 * w] = gk
    gp_ref[:, 2 * w :] = gv
    add = lambda v: jnp.sum(v, axis=0, keepdims=True)

    @pl.when(i == 0)
    def _():
        b_ref[...] = jnp.zeros_like(b_ref)
        f_ref[...] = jnp.zeros_like(f_ref)

    b_ref[0:3, :] += jnp.concatenate([add(up(gq)), add(up(gk)), add(up(gv))], axis=0)
    f_ref[0:2, :] += jnp.concatenate([add(t * g[:, 0:1]), add(t * g[:, 1:2])], axis=0)


def turn_back(part, dq, dk, dv, qkv, cos, sin, grid_t):
    n, L = dq.shape
    g = qkv.shape[1] // 3 // L
    rows = lambda c, j=0: pl.BlockSpec((QT, c), lambda i: (i, j))
    fixed = lambda: pl.BlockSpec((8, L), lambda i: (0, 0))
    return pl.pallas_call(
        turn_back_kernel,
        name="turn_back",
        grid=(n // QT,),
        in_specs=[rows(L), rows(L), rows(L), rows(L, part), rows(L, g + part)]
        + [rows(L, part), rows(L, part), pl.BlockSpec((QT, 2), lambda i: (i, 0))],
        out_specs=[rows(3 * L), fixed(), fixed()],
        out_shape=[shaped((n, 3 * L), bf), shaped((8, L), f32), shaped((8, L), f32)],
        compiler_params=params(16),
        cost_estimate=cost(4e9, 1e7),
    )(dq, dk, dv, qkv, qkv, cos, sin, grid_t)


def first_back_kernel(parts, *refs):
    gp_refs, proj_refs = refs[:parts], refs[parts : 2 * parts]
    w_ref, tok_ref, gr_ref, vec_ref, two_ref, up_ref, down_ref, freq_ref, o_ref, flat_ref, sums = refs[
        2 * parts :
    ]
    i = pl.program_id(0)
    w = tok_ref.shape[1]
    L = w // parts
    gp = [r[:, s * L : (s + 1) * L] for s in range(3) for r in gp_refs]
    grad = nt(jnp.concatenate(gp, axis=1), w_ref[...])
    hat, scale = row_norm(up(tok_ref[...]))
    o_ref[...] = rnd(gr_ref[...] + norm_back(grad, hat, scale, vec_ref[:, :w]))

    @pl.when(i == 0)
    def _():
        sums[...] = jnp.zeros_like(sums)

    sums[0:1, :] += jnp.sum(grad * hat, axis=0, keepdims=True)
    sums[1:2, :] += jnp.sum(grad, axis=0, keepdims=True)

    @pl.when(i == pl.num_programs(0) - 1)
    def _():
        pieces = [sums[0:1, :], sums[1:2, :], two_ref[0:1, :], two_ref[1:2, :]]
        pieces += [r[s : s + 1, :] for s in range(3) for r in proj_refs]
        pieces += [two_ref[2:3, :], up_ref[...], down_ref[...], freq_ref[...]]
        col = 0
        for v in pieces:
            flat_ref[:, col : col + v.shape[1]] = v
            col += v.shape[1]


def first_back(gps, projs, weight, tokens, grad_resid, vec, two, bias_up, bias_down, freq):
    n, w = tokens.shape
    rows = lambda c: pl.BlockSpec((QT, c), lambda i: (i, 0))
    whole = lambda a: pl.BlockSpec(a.shape, lambda i: (0, 0))
    return pl.pallas_call(
        partial(first_back_kernel, len(gps)),
        name="first_back",
        grid=(n // QT,),
        in_specs=[rows(g.shape[1]) for g in gps]
        + [whole(p) for p in projs]
        + [whole(weight), rows(w), rows(w), whole(vec)]
        + [whole(v) for v in (two, bias_up, bias_down, freq)],
        out_specs=[rows(w), whole(vec)],
        out_shape=[shaped((n, w), bf), shaped(vec.shape, f32)],
        scratch_shapes=[pltpu.VMEM((8, w), f32)],
        compiler_params=params(18),
        cost_estimate=cost(7e9, 1e7),
    )(*gps, *projs, weight, tokens, grad_resid, vec, two, bias_up, bias_down, freq)


def over_dp(v, k):
    return lax.ppermute(v, "dp", [(i, i ^ k) for i in range(4)])


def over_core(v):
    return lax.ppermute(v, "fsdp", [(i, i ^ 1) for i in range(8)])


def over_z(v, k):
    return lax.ppermute(v, "fsdp", [(i, i ^ (2 * k)) for i in range(8)])


def spread_dp(v):
    return [v] + [over_dp(v, k) for k in (1, 2, 3)]


def spread_z(v):
    return [v] + [over_z(v, k) for k in (1, 2, 3)]


def pairs(v):
    return (v[0] + v[1]) + (v[2] + v[3])


def tie(*values):
    return lax.optimization_barrier(values)


def place():
    d = lax.axis_index("dp")
    f = lax.axis_index("fsdp")
    return d, f // 2, f % 2


def here():
    return jnp.stack(place()).astype(jnp.int32)


def by_index(got, at):
    rows = []
    for j in range(4):
        rel = lax.bitwise_xor(at, j)
        v = got[3]
        for k in (2, 1, 0):
            v = jnp.where(rel == k, got[k], v)
        rows.append(v)
    return rows


def quarter(shard, j):
    r, cols = shard.shape
    return lax.dynamic_slice(shard, (j * (r // 4), 0), (r // 4, cols))


def arrange_kernel(at, *refs):
    out = refs[-1]
    for side in (0, 1):
        for k in range(4):
            for s in range(4):
                column = lax.bitwise_xor(at[1], s) * 2 + lax.bitwise_xor(at[2], side)
                out[column * 4 + lax.bitwise_xor(at[0], k)] = refs[side * 4 + k][s]


def arrange(own, other):
    r, cols = own[0].shape[1:]
    B = cols // 3
    spec = pltpu.PrefetchScalarGridSpec(
        num_scalar_prefetch=1,
        grid=(3,),
        in_specs=[pl.BlockSpec((4, r, B), lambda j, a: (0, 0, j))] * 8,
        out_specs=pl.BlockSpec((32, r, B), lambda j, a: (0, 0, j)),
    )
    out = pl.pallas_call(
        arrange_kernel,
        name="arrange",
        grid_spec=spec,
        out_shape=shaped((32, r, cols), bf),
        compiler_params=params(10),
        cost_estimate=cost(1e6, 4 * 32 * r * cols),
    )(here(), *own, *other)
    return out.reshape(32 * r, cols)


def fold_core_kernel(parts, extra, at, *refs):
    outs = refs[-4:]
    for k in range(4):
        col = 0
        for p in range(parts):
            a = refs[(k * parts + p) * 2][0, 0]
            b = refs[(k * parts + p) * 2 + 1][0, 0]
            w = a.shape[1]
            outs[k][0, :, col : col + w] = rnd(up(a) + up(b))
            col += w
        if extra and k:
            e = refs[8 * parts]
            v = e[0] if len(e.shape) == 3 else e[...]
            outs[k][0, :, col:] = v


def fold_core(mines, others, extra=None):
    r = mines[0].shape[1] // 4
    wide = sum(m.shape[2] for m in mines)
    more = 0
    args, specs = [], []
    for k in range(4):
        for m, o in zip(mines, others):
            for v in (m, o):
                w = v.shape[2]
                args.append(v.reshape(4, 4, r, w))
                specs.append(
                    pl.BlockSpec((1, 1, r, w), lambda j, a, k=k: (j, lax.bitwise_xor(a[0], k), 0, 0))
                )
    if extra is not None:
        args.append(extra)
        if extra.ndim == 3:
            more = extra.shape[2]
            specs.append(pl.BlockSpec((1, r, more), lambda j, a: (j, 0, 0)))
        else:
            more = extra.shape[1] // 4
            specs.append(pl.BlockSpec((r, more), lambda j, a: (0, j)))
    widths = [wide] + [wide + more] * 3
    spec = pltpu.PrefetchScalarGridSpec(
        num_scalar_prefetch=1,
        grid=(4,),
        in_specs=specs,
        out_specs=[pl.BlockSpec((1, r, w), lambda j, a: (j, 0, 0)) for w in widths],
    )
    return pl.pallas_call(
        partial(fold_core_kernel, len(mines), extra is not None),
        name="fold_core",
        grid_spec=spec,
        out_shape=[shaped((4, r, w), bf) for w in widths],
        compiler_params=params(10),
        cost_estimate=cost(1e6, 48 * r * wide),
    )(here(), *args)


def fold_dp_kernel(at, *refs):
    ins, outs = refs[:-4], refs[-4:]
    w = outs[0].shape[1]
    for k in range(4):
        to = lax.bitwise_xor(at[1], k)
        total = up(ins[0][to])
        for g in ins[1:]:
            total = total + up(g[to][:, :w])
        outs[k][...] = rnd(total)


def fold_dp(own, got):
    whole = lambda v: pl.BlockSpec(v.shape, lambda j, a: (0, 0, 0))
    r, w = own.shape[1:]
    spec = pltpu.PrefetchScalarGridSpec(
        num_scalar_prefetch=1,
        grid=(1,),
        in_specs=[whole(v) for v in [own] + got],
        out_specs=[pl.BlockSpec((r, w), lambda j, a: (0, 0))] * 4,
    )
    return pl.pallas_call(
        fold_dp_kernel,
        name="fold_dp",
        grid_spec=spec,
        out_shape=[shaped((r, w), bf)] * 4,
        compiler_params=params(10),
        cost_estimate=cost(1e6, 40 * r * w),
    )(here(), own, *got)


def pack_kernel(size, off, w, at, flat_ref, half_ref, *refs):
    ins, left, outs = refs[:4], refs[4:8], refs[8:]
    rows, wide = left[0].shape
    room = -(-size // 128) * 128
    for k in range(4):
        to = lax.bitwise_xor(at[1], k)
        outs[k][:rows, :wide] = left[k][...]
        outs[k][:rows, wide:] = rnd(pairs([up(g[to]) for g in ins]))
        outs[k][rows:, :] = jnp.zeros((1, outs[k].shape[1]), bf)
        mine = half_ref[:, pl.ds(pl.multiple_of(to * (2 * size), 128), size)]
        outs[k][rows:, :size] = rnd(mine)
        outs[k][rows:, room : room + w] = rnd(flat_ref[:, off : off + w])


def pack(flat, size, off, w, got, left):
    c = place()[2]
    half = lax.dynamic_slice(flat, (0, c * size), (1, 7 * size))
    r, cols = got[0].shape[1:]
    wide = left[0].shape[1] + cols
    whole = lambda v: pl.BlockSpec(v.shape, lambda j, a, n=v.ndim: (0,) * n)
    args = [flat, half, *got, *left]
    spec = pltpu.PrefetchScalarGridSpec(
        num_scalar_prefetch=1,
        grid=(1,),
        in_specs=[whole(v) for v in args],
        out_specs=[pl.BlockSpec((r + 1, wide), lambda j, a: (0, 0))] * 4,
    )
    return pl.pallas_call(
        partial(pack_kernel, size, off, w),
        name="pack",
        grid_spec=spec,
        out_shape=[shaped((r + 1, wide), bf)] * 4,
        compiler_params=params(10),
        cost_estimate=cost(1e6, 40 * r * wide),
    )(here(), *args)


def fold_z(got):
    return rnd(pairs([up(g) for g in got]))


def adam_terms(grad, first, second, master, decay):
    first_new = 0.9 * first + 0.1 * grad
    second_new = 0.999 * second + 0.001 * grad * grad
    first_hat = first_new / (1.0 - 0.9**STEP)
    second_hat = second_new / (1.0 - 0.999**STEP)
    update = first_hat / (jnp.sqrt(second_hat) + 1e-06) + decay * master
    return (first_new, second_new, update)


def step_kernel(plan, base, at, *refs):
    j = pl.program_id(0)
    sources, refs = refs[:4], refs[4:]
    count = len(plan)
    states, outs, sum_ref = refs[: 3 * count], refs[3 * count : 7 * count], refs[7 * count]
    rel = lax.bitwise_xor(at[0], j)

    @pl.when(j == 0)
    def _():
        sum_ref[...] = jnp.zeros_like(sum_ref)

    for t, chunks in enumerate(plan):
        w_ref, m_ref, v_ref = states[3 * t : 3 * t + 3]
        g_out, m_out, v_out, u_out = outs[4 * t : 4 * t + 4]
        total = jnp.zeros((1, 1), f32)
        size = jnp.sum(w_ref[...] * w_ref[...], keepdims=True)
        for row, rows, col, cols, read in chunks:
            g = read(sources[3], 3)
            for k in (2, 1, 0):
                g = jnp.where(rel == k, read(sources[k], k), g)
            g = up(g)
            to = (slice(row, row + rows), slice(col, col + cols))
            first_new, second_new, update = adam_terms(g, m_ref[to], v_ref[to], w_ref[to], 0.01)
            g_out[to] = g
            m_out[to] = first_new
            v_out[to] = second_new
            u_out[to] = update
            total = total + jnp.sum(update * update, keepdims=True)
        sum_ref[base + t : base + t + 1, :] += jnp.broadcast_to(total, (1, 128))
        sum_ref[base + t + 4 : base + t + 5, :] += jnp.broadcast_to(size, (1, 128))


def step(plan, base, sources, states):
    whole = lambda v: pl.BlockSpec(v.shape, lambda j, a, n=v.ndim: (0,) * n)
    rows = lambda v: pl.BlockSpec((v.shape[0] // 4, v.shape[1]), lambda j, a: (j, 0))
    flat = [v for s in states for v in s]
    spec = pltpu.PrefetchScalarGridSpec(
        num_scalar_prefetch=1,
        grid=(4,),
        in_specs=[whole(v) for v in sources] + [rows(v) for v in flat],
        out_specs=[rows(s[0]) for s in states for _ in range(4)]
        + [pl.BlockSpec((8, 128), lambda j, a: (0, 0))],
    )
    out = pl.pallas_call(
        partial(step_kernel, plan, base),
        name="step",
        grid_spec=spec,
        out_shape=[shaped(s[0].shape, f32) for s in states for _ in range(4)]
        + [shaped((8, 128), f32)],
        compiler_params=params(40),
        cost_estimate=cost(1e6, 28 * sum(s[0].size for s in states)),
    )(here(), *sources, *flat)
    return [out[4 * t : 4 * t + 4] for t in range(len(states))], out[-1]


def finish_kernel(*refs):
    norms = jnp.sqrt(refs[0][...] + refs[1][...])
    refs = refs[2:]
    refs[12][...] = norms
    for t in range(4):
        factor = 0.3 * (norms[t + 4 : t + 5, 0:1] / (norms[t : t + 1, 0:1] + 1e-06))
        refs[8 + t][...] = refs[t][...] - factor * refs[4 + t][...]


def finish(masters, updates, parts):
    rows = lambda v: pl.BlockSpec((v.shape[0] // 4, v.shape[1]), lambda j: (j, 0))
    whole = lambda: pl.BlockSpec((8, 128), lambda j: (0, 0))
    out = pl.pallas_call(
        finish_kernel,
        name="finish",
        grid=(4,),
        in_specs=[whole() for _ in parts] + [rows(v) for v in masters + updates],
        out_specs=[rows(v) for v in masters] + [whole()],
        out_shape=[shaped(v.shape, f32) for v in masters] + [shaped((8, 128), f32)],
        compiler_params=params(),
        cost_estimate=cost(1e6, 12 * sum(v.size for v in masters)),
    )(*parts, *masters, *updates)
    return out[:4], out[4]


def body(fast, tokens, cotangent, image_ids, patch_grid, *state):
    masters, vectors = state[:4], state[4]
    firsts, vector_first = state[5:9], state[9]
    seconds, vector_second = state[10:14], state[14]
    n, w = tokens.shape
    size = vectors.shape[0]
    heads = w // HD
    count = w // 128 // PAIRS
    L = 128 * PAIRS
    low = [rnd(m) for m in masters]
    gather = lambda v: lax.all_gather(v, "fsdp", axis=0, tiled=True)
    scatter = lambda v: lax.psum_scatter(v, "fsdp", scatter_dimension=0, tiled=True)
    whole = jnp.zeros((1,), jnp.int32)
    d, z, c = place()
    mine = jnp.stack([c]).astype(jnp.int32)
    halves = lambda x_t, y: (outer(x_t, y, 1 - mine, 4, 2), outer(x_t, y, mine, 4, 2))
    join = lambda rows: jnp.concatenate(rows, axis=-1)

    if fast:
        q_rows = low[0].shape[0] // 4
        row = jnp.pad(rnd(vectors), (0, low[0].shape[1] - size)).reshape(1, -1)
        got = spread_z(jnp.concatenate([quarter(low[0], d), row], 0))
        qkv_column = jnp.stack([g[:q_rows] for g in got])
        packed = jnp.concatenate(by_index([g[q_rows:, :size] for g in got], z), 0)
        other = over_core(packed)
        packed = jnp.stack([jnp.where(c == 0, packed, other), jnp.where(c == 0, other, packed)], 1)
        packed = packed.reshape(-1)
        up_part, out_part, down_part, qkv_column = tie(
            quarter(low[2], d), low[1], low[3], qkv_column
        )
        full_out = gather(out_part)
        qkv_own = spread_dp(qkv_column)
        up_column = jnp.stack(spread_z(up_part))
        full_down = gather(down_part)
    else:
        packed = gather(rnd(vectors))
        full_qkv, full_out, full_up, full_down = [gather(v) for v in low]
    vec = up(packed).reshape(1, -1)
    freq = vec[0, -w:].reshape(2, heads, 1, HD // 2)
    freq = jnp.broadcast_to(freq, (2, heads, 2, HD // 2)).reshape(2, w)
    grid_t = patch_grid.T
    given = jnp.where((image_ids >= 0)[:, None], cotangent, jnp.zeros_like(cotangent))
    grad_bias_down = jnp.sum(up(given), axis=0, keepdims=True)
    aug_q, aug_k, rng = tables(image_ids)

    normed, normed_t, cos, sin = first(tokens, vec, freq, grid_t)
    if fast:
        normed, *qkv_own = tie(normed, *qkv_own)
        full_qkv = arrange(qkv_own, [over_core(v) for v in qkv_own])
        up_column, full_qkv = tie(up_column, full_qkv)
        up_own = spread_dp(up_column)
    qkv = project(normed, full_qkv, vec, cos, sin)
    mix, mix_t, lb = attend(qkv, aug_q, aug_k, rng)
    if fast:
        mix, *up_own = tie(mix, *up_own)
        up_other = [over_core(v) for v in up_own]
    resid, normed_two, normed_two_t = branch(tokens, mix, full_out, vec)
    if fast:
        full_up = arrange(up_own, up_other)
    active, active_t, slope = hidden_units(normed_two, full_up, vec)
    if fast:
        theirs, own = halves(active_t, given)
        pieces = fold_core([own], [over_core(theirs)])
        active, slope, full_down = tie(active, slope, full_down)
        active, slope, *pieces = tie(active, slope, *pieces)
        got = [over_dp(v, k) for k, v in zip((1, 2, 3), pieces[1:])]
    else:
        down_full = outer(active_t, given, whole, 1, 1)[0]
    output = last(active, full_down, resid, vec)
    grad_hidden, grad_bias_up = hidden_back(given, full_down, slope)
    if fast:
        output, grad_hidden, *got = tie(output, grad_hidden, *got)
        down_z = fold_dp(pieces[0], got)
        grad_hidden, *down_z = tie(grad_hidden, *down_z)
        got = [down_z[0]] + [over_z(v, k) for k, v in zip((1, 2, 3), down_z[1:])]
        theirs, own = halves(normed_two_t, grad_hidden)
        own, *got = tie(own, *got)
        down_f = fold_z(got)
        more = down_f.reshape(4, -1, w)
        pieces = fold_core([own], [over_core(theirs)], more)
        grad_hidden, down_f, *pieces = tie(grad_hidden, down_f, *pieces)
        got = [over_dp(v, k) for k, v in zip((1, 2, 3), pieces[1:])]
    else:
        up_full = outer(normed_two_t, grad_hidden, whole, 1, 1)[0]
    grad_resid, grad_branch, grad_mix, sums_two = second_back(
        grad_hidden, full_up, resid, given, vec, full_out
    )
    if fast:
        out_theirs, out_own = halves(mix_t, grad_branch)
        out_sent = over_core(out_theirs)
    else:
        out_full = outer(mix_t, grad_branch, whole, 1, 1)[0]
    projs, sums_proj, sums_freq, qkv_parts = [], [], [], []
    for part in range(count):
        dq, dk, dv = attend_back(part, qkv, grad_mix, mix, lb, aug_q, aug_k, rng)
        if fast and part == 0:
            dq, *got = tie(dq, *got)
            up_width = pieces[0].shape[2]
            q = down_f.shape[0] // 4

            def read_down(i, q, skip, ref, k):
                return ref[i, :, skip:] if k else ref[q * i : q * i + q]

            plan = [[(q * i, q, 0, w, partial(read_down, i, q, up_width)) for i in range(4)]]
            later = [(plan, [down_f] + got, (masters[3], firsts[3], seconds[3]))]
            up_z = fold_dp(pieces[0], got)
            dq, *up_z = tie(dq, *up_z)
            got = [up_z[0]] + [over_z(v, k) for k, v in zip((1, 2, 3), up_z[1:])]
        if fast and part > 0:
            dq, *got = tie(dq, *got)
        gp, bs, fs = turn_back(part, dq, dk, dv, qkv, cos, sin, grid_t)
        projs.append(gp)
        sums_proj.append(bs)
        sums_freq.append(fs)
        if not fast:
            qkv_parts.append(outer(normed_t, gp, whole, 1, 1)[0])
        elif part == 0:
            theirs, own = halves(normed_t, gp)
            own, *got = tie(own, *got)
            up_f = fold_z(got)
            pieces = fold_core([own, out_own], [over_core(theirs), out_sent], up_f)
            grad_mix, up_f, *pieces = tie(grad_mix, up_f, *pieces)
            got = [over_dp(v, k) for k, v in zip((1, 2, 3), pieces[1:])]
        else:
            a_width = pieces[0].shape[2]
            q, wide = up_f.shape[0], up_f.shape[1] // 4

            def read_up(i, wide, skip, ref, k):
                return ref[i, :, skip:] if k else ref[:, wide * i : wide * i + wide]

            plan = [
                [(0, q, wide * i, wide, partial(read_up, i, wide, a_width)) for i in range(4)]
            ]
            later.append((plan, [up_f] + got, (masters[2], firsts[2], seconds[2])))
            theirs, own = halves(normed_t, gp)
            a_z = fold_dp(pieces[0], got)
            pieces = fold_core([own], [over_core(theirs)])
            projs[-1], *pieces = tie(gp, *pieces)
            got = [over_dp(v, k) for k, v in zip((1, 2, 3), pieces[1:])]
    freq_sums = join([s[:2] for s in sums_freq]).reshape(2, heads, 2, HD // 2)
    freq_grad = (freq_sums[:, :, 0] - freq_sums[:, :, 1]).reshape(1, -1)
    if fast:
        projs[-1], freq_grad = tie(projs[-1], freq_grad)
    tokens_grad, vector_full = first_back(
        projs, sums_proj, full_qkv, tokens, grad_resid, vec, sums_two, grad_bias_up, grad_bias_down, freq_grad
    )
    if fast:
        vector_full, *got = tie(vector_full, *got)
    off = vector_full.shape[1] - 2 * w
    if fast:
        flat = vector_full + over_core(vector_full)
        sends = pack(flat, size, off, w, [pieces[0]] + got, a_z)
        got = [sends[0]] + [over_z(s, k) for k, s in zip((1, 2, 3), sends[1:])]
        held = tie(*[v for entry in later for v in entry[1]], *sends)
        (down_step, down_square), (up_step, up_square) = [
            step(entry[0], 3 - i, list(held[4 * i : 4 * i + 4]), [entry[2]])
            for i, entry in enumerate(later)
        ]
        up_square, down_square, *got = tie(up_square, down_square, *got)
        got = spread_dp(rnd(pairs([up(g) for g in got])))
        tail = pairs([up(g[q_rows:]) for g in got])[0]
        room = -(-size // 128) * 128
        vector_grad = tail[:size]
        down_bias_grad = tail[room : room + w]

        def read(col, ref, k):
            return ref[:q_rows, col : col + L]

        plan = [
            [
                (0, q_rows, (s * count + p) * L, L, partial(read, p * (3 * L + w) + s * L))
                for p in range(count)
                for s in range(3)
            ],
            [(0, q_rows, i * L, L, partial(read, 3 * L + i * L)) for i in range(w // L)],
        ]
        states = [(masters[k], firsts[k], seconds[k]) for k in (0, 1)]
        last_steps, last_squares = step(plan, 0, got, states)
        steps = last_steps + up_step + down_step
        squares = last_squares + up_square + down_square
        squares = squares + over_core(squares)
        squares = squares + over_z(squares, 1)
        squares = [squares, over_z(squares, 2)]
        new_list, norms = finish(list(masters), [s[3] for s in steps], squares)
        update_norms, weight_norms = norms[:4, 0], norms[4:, 0]
    else:
        give = lambda v: lax.psum(scatter(up(v)), "dp")
        up_grad, down_grad, out_grad = give(up_full), give(down_full), give(out_full)
        done = [give(v) for v in qkv_parts]
        vector_grad = give(vector_full[0])
        down_bias_grad = lax.psum(grad_bias_down[0], ("dp", "fsdp"))
        qkv_grad = join([g[:, s * L : (s + 1) * L] for s in range(3) for g in done])
        steps = [
            (g, *adam_terms(g, firsts[k], seconds[k], masters[k], 0.01))
            for k, g in enumerate((qkv_grad, out_grad, up_grad, down_grad))
        ]
        weight_local = jnp.stack([jnp.sum(m * m) for m in masters])
        update_local = jnp.stack([jnp.sum(s[3] * s[3]) for s in steps])
        both = jnp.sqrt(lax.psum(jnp.stack([weight_local, update_local]), "fsdp"))
        weight_norms, update_norms = both[0], both[1]
        factor = 0.3 * (weight_norms / (update_norms + 1e-06))
        new_list = [masters[k] - factor[k] * steps[k][3] for k in range(4)]
    vector_step = adam_terms(vector_grad, vector_first, vector_second, vectors, 0.0)
    return (
        output,
        tokens_grad,
        *[s[0] for s in steps],
        vector_grad,
        down_bias_grad,
        *[s[1] for s in steps],
        vector_step[0],
        *[s[2] for s in steps],
        vector_step[1],
        *new_list,
        vectors - 0.2 * vector_step[2],
        weight_norms,
        update_norms,
    )


def solution(mesh):
    both = P(("dp", "fsdp"), None)
    mat = [P("fsdp", None)] * 4 + [P("fsdp")]
    in_specs = (both, both, P(("dp", "fsdp")), P(None, ("dp", "fsdp")), *mat, *mat, *mat)
    out_specs = (both, both, *mat, P(), *mat, *mat, *mat, P(), P())
    fast = mesh.shape["dp"] == 4 and mesh.shape["fsdp"] == 8
    return jax.shard_map(
        partial(body, fast), mesh=mesh, in_specs=in_specs, out_specs=out_specs, check_vma=False
    )
```

```python
from functools import partial

import jax
import jax.numpy as jnp
from jax import lax
from jax.experimental import pallas as pl
from jax.experimental.pallas import tpu as pltpu
from jax.sharding import PartitionSpec as P

H = 12
HD = 64
STEP = 10
QT = 256
KT = 128
PAIRS = 3
VARIANTS = (2, 3, 4, 5, 7, 8)
norm_eps = 1e-06
bf = jnp.bfloat16
f32 = jnp.float32


def nt(a, b):
    return lax.dot_general(a, b, (((1,), (1,)), ((), ())), preferred_element_type=f32)


def nn(a, b):
    return lax.dot_general(a, b, (((1,), (0,)), ((), ())), preferred_element_type=f32)


def rnd(v):
    return v.astype(bf)


def up(v):
    return v.astype(f32)


def params(mib=22):
    return pltpu.CompilerParams(vmem_limit_bytes=mib << 20)


def cost(flops, moved):
    return pl.CostEstimate(flops=int(flops), bytes_accessed=int(moved), transcendentals=0)


def shaped(shape, kind):
    return jax.ShapeDtypeStruct(shape, kind)


def row_norm(v):
    centre = jnp.mean(v, axis=-1, keepdims=True)
    centred = v - centre
    spread = jnp.mean(centred * centred, axis=-1, keepdims=True)
    scale = lax.rsqrt(spread + norm_eps)
    return centred * scale, scale


def split3(x):
    a = rnd(x)
    r = x - up(a)
    b = rnd(r)
    return jnp.concatenate([a, b, rnd(r - up(b))], axis=0)


def first_kernel(tok_ref, vec_ref, freq_ref, grid_ref, n_ref, nt_ref, cos_ref, sin_ref, table):
    w = tok_ref.shape[1]

    @pl.when(pl.program_id(0) == 0)
    def _():
        place_of = lax.broadcasted_iota(jnp.int32, (32, w), 0).astype(f32)
        for axis in (0, 1):
            angle = place_of * freq_ref[axis : axis + 1, :]
            table[2 * axis] = split3(jnp.cos(angle))
            table[2 * axis + 1] = split3(jnp.sin(angle))

    hat, scale = row_norm(up(tok_ref[...]))
    normed = hat * vec_ref[:, :w] + vec_ref[:, w : 2 * w]
    n_ref[...] = rnd(normed)
    nt_ref[...] = rnd(normed.T)
    g = grid_ref[...]
    index = lax.broadcasted_iota(jnp.int32, (1, 96), 1) & 31
    hot = [rnd(jnp.where(g[:, axis : axis + 1] == index, 1.0, 0.0)) for axis in (0, 1)]
    cos_row, sin_row = nn(hot[0], table[0]), nn(hot[0], table[1])
    cos_col, sin_col = nn(hot[1], table[2]), nn(hot[1], table[3])
    lane = lax.broadcasted_iota(jnp.int32, (1, w), 1)
    cos_ref[...] = cos_row * cos_col - sin_row * sin_col
    s = sin_row * cos_col + cos_row * sin_col
    sin_ref[...] = jnp.where(lane & 63 < 32, -s, s)


def first(tokens, vec, freq, grid_t):
    n, w = tokens.shape
    rows = lambda: pl.BlockSpec((QT, w), lambda i: (i, 0))
    whole = lambda a: pl.BlockSpec(a.shape, lambda i: (0, 0))
    return pl.pallas_call(
        first_kernel,
        name="first",
        grid=(n // QT,),
        in_specs=[rows(), whole(vec), whole(freq), pl.BlockSpec((QT, 2), lambda i: (i, 0))],
        out_specs=[rows(), pl.BlockSpec((w, QT), lambda i: (0, i)), rows(), rows()],
        out_shape=[shaped((n, w), bf), shaped((w, n), bf), shaped((n, w), f32), shaped((n, w), f32)],
        scratch_shapes=[pltpu.VMEM((4, 96, w), bf)],
        compiler_params=params(),
        cost_estimate=cost(5e9, 1e7),
    )(tokens, vec, freq, grid_t)


def swap(v):
    w = v.shape[1]
    lane = lax.broadcasted_iota(jnp.int32, (1, w), 1)
    return jnp.where(lane & 63 < 32, pltpu.roll(v, w - 32, 1), pltpu.roll(v, 32, 1))


def project_kernel(n_ref, w_ref, b_ref, cos_ref, sin_ref, o_ref):
    j = pl.program_id(0)
    u = nn(n_ref[...], w_ref[...]) + b_ref[...]

    @pl.when(j < 2)
    def _():
        turned = u * cos_ref[...] + swap(u) * sin_ref[...]
        o_ref[...] = rnd(turned * jnp.where(j < 1, 0.125, 1.0))

    @pl.when(j >= 2)
    def _():
        o_ref[...] = rnd(u)


def project(normed, weight, vec, cos, sin):
    n, w = normed.shape
    whole = lambda: pl.BlockSpec((n, w), lambda j: (0, 0))
    return pl.pallas_call(
        project_kernel,
        name="project",
        grid=(3,),
        in_specs=[
            whole(),
            pl.BlockSpec((w, w), lambda j: (0, j)),
            pl.BlockSpec((1, w), lambda j: (0, 4 + j)),
            whole(),
            whole(),
        ],
        out_specs=pl.BlockSpec((n, w), lambda j: (0, j)),
        out_shape=shaped((n, 3 * w), bf),
        compiler_params=params(22),
        cost_estimate=cost(8e9, 1e7),
    )(normed, weight, vec, cos, sin)


def tables(ids):
    n = ids.shape[0]
    lane = jnp.arange(128) & 63
    one = (ids[:, None] + 1 == lane[None]).astype(f32)
    small = (lane < 8)[None]
    aug_q = rnd(jnp.where(small, one, 0.0))
    aug_k = rnd(jnp.where(small, (one - 1.0) * 1e30, jnp.where((lane < 11)[None], 1.0, 0.0)))
    tiles = n // QT
    hit = (ids.reshape(tiles, QT, 1) == ids[None, None, :]).any(1)
    pos = jnp.arange(n)[None]
    lo = jnp.min(jnp.where(hit, pos, n), 1) // KT
    hi = jnp.max(jnp.where(hit, pos, -1), 1) // KT + 1
    need = hi - lo
    width = jnp.full_like(need, VARIANTS[-1])
    for v in VARIANTS[::-1]:
        width = jnp.where(need <= v, v, width)
    start = jnp.minimum(lo, n // KT - width)
    return aug_q, aug_k, jnp.stack([start, width]).astype(jnp.int32)


def low_lanes():
    return lax.broadcasted_iota(jnp.int32, (1, 128), 1) < 64


def attend_kernel(rng, q_ref, k_ref, v_ref, aq_ref, ak_ref, mix_ref, mixt_ref, lb_ref, vt):
    i = pl.program_id(1)
    n = k_ref.shape[0]
    start = rng[0, i]
    width = rng[1, i]
    low = low_lanes()

    @pl.when(i == 0)
    def _():
        one = jnp.ones((16, n), bf)
        for p in range(PAIRS):
            t = v_ref[:, 128 * p : 128 * p + 128].T
            for h in (0, 1):
                vt[2 * p + h, :64, :] = t[64 * h : 64 * h + 64]
                vt[2 * p + h, 64:, :] = one

    aq = aq_ref[...]
    for W in VARIANTS:

        @pl.when(width == W)
        def _():
            at = pl.ds(pl.multiple_of(start * KT, KT), W * KT)
            ak = ak_ref[at, :]
            scores = []
            for p in range(PAIRS):
                c = slice(128 * p, 128 * p + 128)
                q = q_ref[:, c]
                k = k_ref[at, c]
                scores.append(nt(jnp.where(low, k, ak), jnp.where(low, q, aq)))
                scores.append(nt(jnp.where(low, ak, k), jnp.where(low, aq, q)))
            for p in range(PAIRS):
                c = slice(128 * p, 128 * p + 128)
                outs = []
                for h in (0, 1):
                    s = scores[2 * p + h]
                    m = jnp.max(s, axis=0, keepdims=True)
                    e = rnd(jnp.exp(s - m))
                    o = nn(vt[2 * p + h, :, at], e)
                    t = o[64:65]
                    outs.append(o[:64] * (1.0 / t))
                    lb_ref[p, h : h + 1, :] = m + jnp.log(t)
                both = jnp.concatenate(outs, 0)
                mix_ref[:, c] = rnd(both.T)
                mixt_ref[c, :] = rnd(both)


def attend(qkv, aug_q, aug_k, rng):
    n, w3 = qkv.shape
    w = w3 // 3
    L = 128 * PAIRS
    g = w // L
    spec = pltpu.PrefetchScalarGridSpec(
        num_scalar_prefetch=1,
        grid=(g, n // QT),
        in_specs=[
            pl.BlockSpec((QT, L), lambda p, i, r: (i, p)),
            pl.BlockSpec((n, L), lambda p, i, r: (0, g + p)),
            pl.BlockSpec((n, L), lambda p, i, r: (0, 2 * g + p)),
            pl.BlockSpec((QT, 128), lambda p, i, r: (i, 0)),
            pl.BlockSpec((n, 128), lambda p, i, r: (0, 0)),
        ],
        out_specs=[
            pl.BlockSpec((QT, L), lambda p, i, r: (i, p)),
            pl.BlockSpec((L, QT), lambda p, i, r: (p, i)),
            pl.BlockSpec((PAIRS, 8, QT), lambda p, i, r: (p, 0, i)),
        ],
        scratch_shapes=[pltpu.VMEM((2 * PAIRS, 80, n), bf)],
    )
    return pl.pallas_call(
        attend_kernel,
        name="attend",
        grid_spec=spec,
        out_shape=[shaped((n, w), bf), shaped((w, n), bf), shaped((w // 128, 8, n), f32)],
        compiler_params=params(),
        cost_estimate=cost(2.3e10, 1e7),
    )(rng, qkv, qkv, qkv, aug_q, aug_k)


def fill(aug, x):
    lane = lax.broadcasted_iota(jnp.int32, (1, 128), 1) & 63
    a = rnd(x)
    r = x - up(a)
    b = rnd(r)
    c = rnd(r - up(b))
    return jnp.where(lane == 8, a, jnp.where(lane == 9, b, jnp.where(lane == 10, c, aug)))


def attend_back_kernel(
    rng, q_ref, k_ref, v_ref, g_ref, mix_ref, lb_ref, aq_ref, ak_ref,
    dq_ref, dk_ref, dv_ref, dk_acc, dv_acc,
):
    i = pl.program_id(0)
    start = rng[0, i]
    width = rng[1, i]

    @pl.when(i == 0)
    def _():
        dk_acc[...] = jnp.zeros_like(dk_acc)
        dv_acc[...] = jnp.zeros_like(dv_acc)

    low = low_lanes()
    aq0 = aq_ref[...]
    zero = jnp.zeros((1, 128), bf)
    held = []
    for p in range(PAIRS):
        c = slice(128 * p, 128 * p + 128)
        q = q_ref[:, c]
        g = g_ref[:, c]
        prod = up(g) * up(mix_ref[:, c])
        even = jnp.sum(jnp.where(low, prod, 0.0), axis=1, keepdims=True)
        odd = jnp.sum(jnp.where(low, 0.0, prod), axis=1, keepdims=True)
        lt = lb_ref[p].T
        aq = fill(aq0, -jnp.where(low, lt[:, 1:2], lt[:, 0:1]))
        ag = fill(zero, -jnp.where(low, odd, even))
        held.append(
            (
                (jnp.where(low, q, aq), jnp.where(low, aq, q)),
                (jnp.where(low, g, ag), jnp.where(low, ag, g)),
                q.T,
                g.T,
            )
        )
    for W in VARIANTS:

        @pl.when(width == W)
        def _():
            at = pl.ds(pl.multiple_of(start * KT, KT), W * KT)
            ak = ak_ref[at, :]
            for p in range(PAIRS):
                c = slice(128 * p, 128 * p + 128)
                qs, gs, qt, gt = held[p]
                k = k_ref[at, c]
                v = v_ref[at, c]
                one = jnp.ones_like(v)
                ks = (jnp.where(low, k, ak), jnp.where(low, ak, k))
                vs = (jnp.where(low, v, one), jnp.where(low, one, v))
                dqs = []
                for h in (0, 1):
                    e = jnp.exp(nt(qs[h], ks[h]))
                    ds = rnd(e * nt(gs[h], vs[h]))
                    e = rnd(e)
                    half = slice(64 * h, 64 * h + 64)
                    to = slice(128 * p + 64 * h, 128 * p + 64 * h + 64)
                    dqs.append(nn(ds, k))
                    dk_acc[to, at] += nn(qt[half], ds)
                    dv_acc[to, at] += nn(gt[half], e)
                dq_ref[:, c] = jnp.where(low, dqs[0], dqs[1]) * 0.125

    @pl.when(i == pl.num_programs(0) - 1)
    def _():
        dk_ref[...] = dk_acc[...].T
        dv_ref[...] = rnd(dv_acc[...].T)


def attend_back(part, qkv, g_mix, mix, lb, aug_q, aug_k, rng):
    n, w3 = qkv.shape
    L = 128 * PAIRS
    g = w3 // 3 // L
    spec = pltpu.PrefetchScalarGridSpec(
        num_scalar_prefetch=1,
        grid=(n // QT,),
        in_specs=[
            pl.BlockSpec((QT, L), lambda i, r: (i, part)),
            pl.BlockSpec((n, L), lambda i, r: (0, g + part)),
            pl.BlockSpec((n, L), lambda i, r: (0, 2 * g + part)),
            pl.BlockSpec((QT, L), lambda i, r: (i, part)),
            pl.BlockSpec((QT, L), lambda i, r: (i, part)),
            pl.BlockSpec((PAIRS, 8, QT), lambda i, r: (part, 0, i)),
            pl.BlockSpec((QT, 128), lambda i, r: (i, 0)),
            pl.BlockSpec((n, 128), lambda i, r: (0, 0)),
        ],
        out_specs=[
            pl.BlockSpec((QT, L), lambda i, r: (i, 0)),
            pl.BlockSpec((n, L), lambda i, r: (0, 0)),
            pl.BlockSpec((n, L), lambda i, r: (0, 0)),
        ],
        scratch_shapes=[pltpu.VMEM((L, n), f32), pltpu.VMEM((L, n), f32)],
    )
    return pl.pallas_call(
        attend_back_kernel,
        name="attend_back",
        grid_spec=spec,
        out_shape=[shaped((n, L), f32), shaped((n, L), f32), shaped((n, L), bf)],
        compiler_params=params(),
        cost_estimate=cost(2.2e10, 1e7),
    )(rng, qkv, qkv, qkv, g_mix, mix, lb, aug_q, aug_k)


def branch_kernel(tok_ref, mix_ref, w_ref, vec_ref, res_ref, n_ref, nt_ref):
    w = tok_ref.shape[1]
    resid = up(tok_ref[...]) + nn(mix_ref[...], w_ref[...]) + vec_ref[:, 7 * w : 8 * w]
    res_ref[...] = resid
    hat, scale = row_norm(resid)
    normed = hat * vec_ref[:, 2 * w : 3 * w] + vec_ref[:, 3 * w : 4 * w]
    n_ref[...] = rnd(normed)
    nt_ref[...] = rnd(normed.T)


def branch(tokens, mix, weight, vec):
    n, w = tokens.shape
    rows = lambda: pl.BlockSpec((QT, w), lambda i: (i, 0))
    whole = lambda a: pl.BlockSpec(a.shape, lambda i: (0, 0))
    return pl.pallas_call(
        branch_kernel,
        name="branch",
        grid=(n // QT,),
        in_specs=[rows(), rows(), whole(weight), whole(vec)],
        out_specs=[rows(), rows(), pl.BlockSpec((w, QT), lambda i: (0, i))],
        out_shape=[shaped((n, w), f32), shaped((n, w), bf), shaped((w, n), bf)],
        compiler_params=params(22),
        cost_estimate=cost(4e9, 1e7),
    )(tokens, mix, weight, vec)


def gelu_parts(x):
    cdf = 0.5 + 0.5 * lax.erf(x * 0.7071067811865476)
    return x * cdf, cdf + x * (jnp.exp(x * x * -0.5) * 0.3989422804014327)


def hidden_kernel(n_ref, w_ref, b_ref, a_ref, at_ref, d_ref):
    x = nn(n_ref[...], w_ref[...]) + b_ref[...]
    active, slope = gelu_parts(x)
    active = rnd(active)
    a_ref[...] = active
    at_ref[...] = active.T
    d_ref[...] = rnd(slope)


def hidden_units(normed, weight, vec):
    n, w = normed.shape
    ff = weight.shape[1]
    B = 768
    off = 8 * w // B
    return pl.pallas_call(
        hidden_kernel,
        name="hidden",
        grid=(ff // B,),
        in_specs=[
            pl.BlockSpec((n, w), lambda j: (0, 0)),
            pl.BlockSpec((w, B), lambda j: (0, j)),
            pl.BlockSpec((1, B), lambda j: (0, off + j)),
        ],
        out_specs=[
            pl.BlockSpec((n, B), lambda j: (0, j)),
            pl.BlockSpec((B, n), lambda j: (j, 0)),
            pl.BlockSpec((n, B), lambda j: (0, j)),
        ],
        out_shape=[shaped((n, ff), bf), shaped((ff, n), bf), shaped((n, ff), bf)],
        compiler_params=params(30),
        cost_estimate=cost(1.5e10, 1e7),
    )(normed, weight, vec)


def last_kernel(a_ref, w_ref, res_ref, b_ref, o_ref):
    o_ref[...] = rnd(res_ref[...] + nn(a_ref[...], w_ref[...]) + b_ref[...])


def last(active, weight, resid, vec):
    n, ff = active.shape
    w = resid.shape[1]
    off = (8 * w + ff) // w
    return pl.pallas_call(
        last_kernel,
        name="last",
        grid=(n // QT,),
        in_specs=[
            pl.BlockSpec((QT, ff), lambda i: (i, 0)),
            pl.BlockSpec((ff, w), lambda i: (0, 0)),
            pl.BlockSpec((QT, w), lambda i: (i, 0)),
            pl.BlockSpec((1, w), lambda i: (0, off)),
        ],
        out_specs=pl.BlockSpec((QT, w), lambda i: (i, 0)),
        out_shape=shaped((n, w), bf),
        compiler_params=params(),
        cost_estimate=cost(6e9, 1e7),
    )(active, weight, resid, vec)


def hidden_back_kernel(g_ref, w_ref, d_ref, gh_ref, sum_ref):
    gh = rnd(nt(g_ref[...], w_ref[...]) * up(d_ref[...]))
    gh_ref[...] = gh
    sum_ref[...] = jnp.sum(up(gh), axis=0, keepdims=True)


def hidden_back(given, weight, slope):
    n, w = given.shape
    ff = weight.shape[0]
    B = 768
    return pl.pallas_call(
        hidden_back_kernel,
        name="hidden_back",
        grid=(ff // B,),
        in_specs=[
            pl.BlockSpec((n, w), lambda j: (0, 0)),
            pl.BlockSpec((B, w), lambda j: (j, 0)),
            pl.BlockSpec((n, B), lambda j: (0, j)),
        ],
        out_specs=[pl.BlockSpec((n, B), lambda j: (0, j)), pl.BlockSpec((1, B), lambda j: (0, j))],
        out_shape=[shaped((n, ff), bf), shaped((1, ff), f32)],
        compiler_params=params(),
        cost_estimate=cost(8e9, 1e7),
    )(given, weight, slope)


def norm_back(grad, hat, scale, gain):
    d = grad * gain
    a = jnp.mean(d, axis=-1, keepdims=True)
    b = jnp.mean(d * hat, axis=-1, keepdims=True)
    return (d - a - hat * b) * scale


def second_back_kernel(gh_ref, w_ref, res_ref, cot_ref, vec_ref, wo_ref, gr_ref, gb_ref, gm_ref, sum_ref):
    i = pl.program_id(0)
    w = res_ref.shape[1]
    grad = nt(gh_ref[...], w_ref[...])
    hat, scale = row_norm(res_ref[...])
    total = up(cot_ref[...]) + norm_back(grad, hat, scale, vec_ref[:, 2 * w : 3 * w])
    gr_ref[...] = total
    low = rnd(total)
    gb_ref[...] = low
    gm_ref[...] = rnd(nt(low, wo_ref[...]))
    sums = jnp.concatenate(
        [
            jnp.sum(grad * hat, axis=0, keepdims=True),
            jnp.sum(grad, axis=0, keepdims=True),
            jnp.sum(up(low), axis=0, keepdims=True),
        ],
        axis=0,
    )

    @pl.when(i == 0)
    def _():
        sum_ref[...] = jnp.zeros_like(sum_ref)

    sum_ref[0:3, :] += sums


def second_back(gh, weight, resid, given, vec, out_w):
    n, ff = gh.shape
    w = resid.shape[1]
    rows = lambda c: pl.BlockSpec((QT, c), lambda i: (i, 0))
    whole = lambda a: pl.BlockSpec(a.shape, lambda i: (0, 0))
    return pl.pallas_call(
        second_back_kernel,
        name="second_back",
        grid=(n // QT,),
        in_specs=[rows(ff), whole(weight), rows(w), rows(w), whole(vec), whole(out_w)],
        out_specs=[rows(w), rows(w), rows(w), pl.BlockSpec((8, w), lambda i: (0, 0))],
        out_shape=[shaped((n, w), f32), shaped((n, w), bf), shaped((n, w), bf), shaped((8, w), f32)],
        compiler_params=params(),
        cost_estimate=cost(9e9, 1e7),
    )(gh, weight, resid, given, vec, out_w)


def outer_kernel(sel, x_ref, y_ref, o_ref):
    z, one, r, n = x_ref.shape
    got = nn(x_ref[...].reshape(z * r, n), y_ref[...])
    o_ref[...] = rnd(got).reshape(o_ref.shape)


def outer(x_t, y, sel, groups, share):
    rows, n = x_t.shape
    c = y.shape[1]
    r = rows // (groups * share)
    B = 768 if c % 768 == 0 else c if c < 1536 and c % 128 == 0 else 256
    spec = pltpu.PrefetchScalarGridSpec(
        num_scalar_prefetch=1,
        grid=(c // B,),
        in_specs=[
            pl.BlockSpec((groups, 1, r, n), lambda j, s: (0, s[0], 0, 0)),
            pl.BlockSpec((n, B), lambda j, s: (0, j)),
        ],
        out_specs=pl.BlockSpec((groups, r, B), lambda j, s: (0, 0, j)),
    )
    return pl.pallas_call(
        outer_kernel,
        name="outer",
        grid_spec=spec,
        out_shape=shaped((groups, r, c), bf),
        compiler_params=params(),
        cost_estimate=cost(4 * groups * r * c * n, 1e7),
    )(sel, x_t.reshape(groups, share, r, n), y)


def turn_back_kernel(
    dq_ref, dk_ref, dv_ref, q_ref, k_ref, cos_ref, sin_ref, grid_ref, gp_ref, b_ref, f_ref
):
    i = pl.program_id(0)
    w = cos_ref.shape[1]
    cos = cos_ref[...]
    sin = sin_ref[...]
    dq = dq_ref[...]
    dk = dk_ref[...]
    gv = dv_ref[...]
    sq = swap(dq)
    sk = swap(dk)
    t = sq * (up(q_ref[...]) * 8.0) + sk * up(k_ref[...])
    g = up(grid_ref[...])
    gq = rnd(dq * cos - sq * sin)
    gk = rnd(dk * cos - sk * sin)
    gp_ref[:, :w] = gq
    gp_ref[:, w : 2 * w] = gk
    gp_ref[:, 2 * w :] = gv
    add = lambda v: jnp.sum(v, axis=0, keepdims=True)

    @pl.when(i == 0)
    def _():
        b_ref[...] = jnp.zeros_like(b_ref)
        f_ref[...] = jnp.zeros_like(f_ref)

    b_ref[0:3, :] += jnp.concatenate([add(up(gq)), add(up(gk)), add(up(gv))], axis=0)
    f_ref[0:2, :] += jnp.concatenate([add(t * g[:, 0:1]), add(t * g[:, 1:2])], axis=0)


def turn_back(part, dq, dk, dv, qkv, cos, sin, grid_t):
    n, L = dq.shape
    g = qkv.shape[1] // 3 // L
    rows = lambda c, j=0: pl.BlockSpec((QT, c), lambda i: (i, j))
    fixed = lambda: pl.BlockSpec((8, L), lambda i: (0, 0))
    return pl.pallas_call(
        turn_back_kernel,
        name="turn_back",
        grid=(n // QT,),
        in_specs=[rows(L), rows(L), rows(L), rows(L, part), rows(L, g + part)]
        + [rows(L, part), rows(L, part), pl.BlockSpec((QT, 2), lambda i: (i, 0))],
        out_specs=[rows(3 * L), fixed(), fixed()],
        out_shape=[shaped((n, 3 * L), bf), shaped((8, L), f32), shaped((8, L), f32)],
        compiler_params=params(16),
        cost_estimate=cost(4e9, 1e7),
    )(dq, dk, dv, qkv, qkv, cos, sin, grid_t)


def first_back_kernel(parts, *refs):
    gp_refs, proj_refs = refs[:parts], refs[parts : 2 * parts]
    w_ref, tok_ref, gr_ref, vec_ref, two_ref, up_ref, down_ref, freq_ref, o_ref, flat_ref, sums = refs[
        2 * parts :
    ]
    i = pl.program_id(0)
    w = tok_ref.shape[1]
    L = w // parts
    gp = [r[:, s * L : (s + 1) * L] for s in range(3) for r in gp_refs]
    grad = nt(jnp.concatenate(gp, axis=1), w_ref[...])
    hat, scale = row_norm(up(tok_ref[...]))
    o_ref[...] = rnd(gr_ref[...] + norm_back(grad, hat, scale, vec_ref[:, :w]))

    @pl.when(i == 0)
    def _():
        sums[...] = jnp.zeros_like(sums)

    sums[0:1, :] += jnp.sum(grad * hat, axis=0, keepdims=True)
    sums[1:2, :] += jnp.sum(grad, axis=0, keepdims=True)

    @pl.when(i == pl.num_programs(0) - 1)
    def _():
        pieces = [sums[0:1, :], sums[1:2, :], two_ref[0:1, :], two_ref[1:2, :]]
        pieces += [r[s : s + 1, :] for s in range(3) for r in proj_refs]
        pieces += [two_ref[2:3, :], up_ref[...], down_ref[...], freq_ref[...]]
        col = 0
        for v in pieces:
            flat_ref[:, col : col + v.shape[1]] = v
            col += v.shape[1]


def first_back(gps, projs, weight, tokens, grad_resid, vec, two, bias_up, bias_down, freq):
    n, w = tokens.shape
    rows = lambda c: pl.BlockSpec((QT, c), lambda i: (i, 0))
    whole = lambda a: pl.BlockSpec(a.shape, lambda i: (0, 0))
    return pl.pallas_call(
        partial(first_back_kernel, len(gps)),
        name="first_back",
        grid=(n // QT,),
        in_specs=[rows(g.shape[1]) for g in gps]
        + [whole(p) for p in projs]
        + [whole(weight), rows(w), rows(w), whole(vec)]
        + [whole(v) for v in (two, bias_up, bias_down, freq)],
        out_specs=[rows(w), whole(vec)],
        out_shape=[shaped((n, w), bf), shaped(vec.shape, f32)],
        scratch_shapes=[pltpu.VMEM((8, w), f32)],
        compiler_params=params(18),
        cost_estimate=cost(7e9, 1e7),
    )(*gps, *projs, weight, tokens, grad_resid, vec, two, bias_up, bias_down, freq)


def over_dp(v, k):
    return lax.ppermute(v, "dp", [(i, i ^ k) for i in range(4)])


def over_core(v):
    return lax.ppermute(v, "fsdp", [(i, i ^ 1) for i in range(8)])


def over_z(v, k):
    return lax.ppermute(v, "fsdp", [(i, i ^ (2 * k)) for i in range(8)])


def spread_dp(v):
    return [v] + [over_dp(v, k) for k in (1, 2, 3)]


def spread_z(v):
    return [v] + [over_z(v, k) for k in (1, 2, 3)]


def pairs(v):
    return (v[0] + v[1]) + (v[2] + v[3])


def tie(*values):
    return lax.optimization_barrier(values)


def place():
    d = lax.axis_index("dp")
    f = lax.axis_index("fsdp")
    return d, f // 2, f % 2


def here():
    return jnp.stack(place()).astype(jnp.int32)


def by_index(got, at):
    rows = []
    for j in range(4):
        rel = lax.bitwise_xor(at, j)
        v = got[3]
        for k in (2, 1, 0):
            v = jnp.where(rel == k, got[k], v)
        rows.append(v)
    return rows


def quarter(shard, j):
    r, cols = shard.shape
    return lax.dynamic_slice(shard, (j * (r // 4), 0), (r // 4, cols))


def arrange_kernel(at, *refs):
    out = refs[-1]
    for side in (0, 1):
        for k in range(4):
            for s in range(4):
                column = lax.bitwise_xor(at[1], s) * 2 + lax.bitwise_xor(at[2], side)
                out[column * 4 + lax.bitwise_xor(at[0], k)] = refs[side * 4 + k][s]


def arrange(own, other):
    r, cols = own[0].shape[1:]
    B = cols // 3
    spec = pltpu.PrefetchScalarGridSpec(
        num_scalar_prefetch=1,
        grid=(3,),
        in_specs=[pl.BlockSpec((4, r, B), lambda j, a: (0, 0, j))] * 8,
        out_specs=pl.BlockSpec((32, r, B), lambda j, a: (0, 0, j)),
    )
    out = pl.pallas_call(
        arrange_kernel,
        name="arrange",
        grid_spec=spec,
        out_shape=shaped((32, r, cols), bf),
        compiler_params=params(10),
        cost_estimate=cost(1e6, 4 * 32 * r * cols),
    )(here(), *own, *other)
    return out.reshape(32 * r, cols)


def fold_core_kernel(parts, extra, at, *refs):
    outs = refs[-4:]
    for k in range(4):
        col = 0
        for p in range(parts):
            a = refs[(k * parts + p) * 2][0, 0]
            b = refs[(k * parts + p) * 2 + 1][0, 0]
            w = a.shape[1]
            outs[k][0, :, col : col + w] = rnd(up(a) + up(b))
            col += w
        if extra and k:
            e = refs[8 * parts]
            v = e[0] if len(e.shape) == 3 else e[...]
            outs[k][0, :, col:] = v


def fold_core(mines, others, extra=None):
    r = mines[0].shape[1] // 4
    wide = sum(m.shape[2] for m in mines)
    more = 0
    args, specs = [], []
    for k in range(4):
        for m, o in zip(mines, others):
            for v in (m, o):
                w = v.shape[2]
                args.append(v.reshape(4, 4, r, w))
                specs.append(
                    pl.BlockSpec((1, 1, r, w), lambda j, a, k=k: (j, lax.bitwise_xor(a[0], k), 0, 0))
                )
    if extra is not None:
        args.append(extra)
        if extra.ndim == 3:
            more = extra.shape[2]
            specs.append(pl.BlockSpec((1, r, more), lambda j, a: (j, 0, 0)))
        else:
            more = extra.shape[1] // 4
            specs.append(pl.BlockSpec((r, more), lambda j, a: (0, j)))
    widths = [wide] + [wide + more] * 3
    spec = pltpu.PrefetchScalarGridSpec(
        num_scalar_prefetch=1,
        grid=(4,),
        in_specs=specs,
        out_specs=[pl.BlockSpec((1, r, w), lambda j, a: (j, 0, 0)) for w in widths],
    )
    return pl.pallas_call(
        partial(fold_core_kernel, len(mines), extra is not None),
        name="fold_core",
        grid_spec=spec,
        out_shape=[shaped((4, r, w), bf) for w in widths],
        compiler_params=params(10),
        cost_estimate=cost(1e6, 48 * r * wide),
    )(here(), *args)


def fold_dp_kernel(at, *refs):
    ins, outs = refs[:-4], refs[-4:]
    w = outs[0].shape[1]
    for k in range(4):
        to = lax.bitwise_xor(at[1], k)
        total = up(ins[0][to])
        for g in ins[1:]:
            total = total + up(g[to][:, :w])
        outs[k][...] = rnd(total)


def fold_dp(own, got):
    whole = lambda v: pl.BlockSpec(v.shape, lambda j, a: (0, 0, 0))
    r, w = own.shape[1:]
    spec = pltpu.PrefetchScalarGridSpec(
        num_scalar_prefetch=1,
        grid=(1,),
        in_specs=[whole(v) for v in [own] + got],
        out_specs=[pl.BlockSpec((r, w), lambda j, a: (0, 0))] * 4,
    )
    return pl.pallas_call(
        fold_dp_kernel,
        name="fold_dp",
        grid_spec=spec,
        out_shape=[shaped((r, w), bf)] * 4,
        compiler_params=params(10),
        cost_estimate=cost(1e6, 40 * r * w),
    )(here(), own, *got)


def pack_kernel(size, off, w, at, flat_ref, half_ref, *refs):
    ins, left, outs = refs[:4], refs[4:8], refs[8:]
    rows, wide = left[0].shape
    room = -(-size // 128) * 128
    for k in range(4):
        to = lax.bitwise_xor(at[1], k)
        outs[k][:rows, :wide] = left[k][...]
        outs[k][:rows, wide:] = rnd(pairs([up(g[to]) for g in ins]))
        outs[k][rows:, :] = jnp.zeros((1, outs[k].shape[1]), bf)
        mine = half_ref[:, pl.ds(pl.multiple_of(to * (2 * size), 128), size)]
        outs[k][rows:, :size] = rnd(mine)
        outs[k][rows:, room : room + w] = rnd(flat_ref[:, off : off + w])


def pack(flat, size, off, w, got, left):
    c = place()[2]
    half = lax.dynamic_slice(flat, (0, c * size), (1, 7 * size))
    r, cols = got[0].shape[1:]
    wide = left[0].shape[1] + cols
    whole = lambda v: pl.BlockSpec(v.shape, lambda j, a, n=v.ndim: (0,) * n)
    args = [flat, half, *got, *left]
    spec = pltpu.PrefetchScalarGridSpec(
        num_scalar_prefetch=1,
        grid=(1,),
        in_specs=[whole(v) for v in args],
        out_specs=[pl.BlockSpec((r + 1, wide), lambda j, a: (0, 0))] * 4,
    )
    return pl.pallas_call(
        partial(pack_kernel, size, off, w),
        name="pack",
        grid_spec=spec,
        out_shape=[shaped((r + 1, wide), bf)] * 4,
        compiler_params=params(10),
        cost_estimate=cost(1e6, 40 * r * wide),
    )(here(), *args)


def fold_z(got):
    return rnd(pairs([up(g) for g in got]))


def adam_terms(grad, first, second, master, decay):
    first_new = 0.9 * first + 0.1 * grad
    second_new = 0.999 * second + 0.001 * grad * grad
    first_hat = first_new / (1.0 - 0.9**STEP)
    second_hat = second_new / (1.0 - 0.999**STEP)
    update = first_hat / (jnp.sqrt(second_hat) + 1e-06) + decay * master
    return (first_new, second_new, update)


def step_kernel(plan, base, at, *refs):
    j = pl.program_id(0)
    sources, refs = refs[:4], refs[4:]
    count = len(plan)
    states, outs, sum_ref = refs[: 3 * count], refs[3 * count : 7 * count], refs[7 * count]
    rel = lax.bitwise_xor(at[0], j)

    @pl.when(j == 0)
    def _():
        sum_ref[...] = jnp.zeros_like(sum_ref)

    for t, chunks in enumerate(plan):
        w_ref, m_ref, v_ref = states[3 * t : 3 * t + 3]
        g_out, m_out, v_out, u_out = outs[4 * t : 4 * t + 4]
        total = jnp.zeros((1, 1), f32)
        size = jnp.sum(w_ref[...] * w_ref[...], keepdims=True)
        for row, rows, col, cols, read in chunks:
            g = read(sources[3], 3)
            for k in (2, 1, 0):
                g = jnp.where(rel == k, read(sources[k], k), g)
            g = up(g)
            to = (slice(row, row + rows), slice(col, col + cols))
            first_new, second_new, update = adam_terms(g, m_ref[to], v_ref[to], w_ref[to], 0.01)
            g_out[to] = g
            m_out[to] = first_new
            v_out[to] = second_new
            u_out[to] = update
            total = total + jnp.sum(update * update, keepdims=True)
        sum_ref[base + t : base + t + 1, :] += jnp.broadcast_to(total, (1, 128))
        sum_ref[base + t + 4 : base + t + 5, :] += jnp.broadcast_to(size, (1, 128))


def step(plan, base, sources, states):
    whole = lambda v: pl.BlockSpec(v.shape, lambda j, a, n=v.ndim: (0,) * n)
    rows = lambda v: pl.BlockSpec((v.shape[0] // 4, v.shape[1]), lambda j, a: (j, 0))
    flat = [v for s in states for v in s]
    spec = pltpu.PrefetchScalarGridSpec(
        num_scalar_prefetch=1,
        grid=(4,),
        in_specs=[whole(v) for v in sources] + [rows(v) for v in flat],
        out_specs=[rows(s[0]) for s in states for _ in range(4)]
        + [pl.BlockSpec((8, 128), lambda j, a: (0, 0))],
    )
    out = pl.pallas_call(
        partial(step_kernel, plan, base),
        name="step",
        grid_spec=spec,
        out_shape=[shaped(s[0].shape, f32) for s in states for _ in range(4)]
        + [shaped((8, 128), f32)],
        compiler_params=params(40),
        cost_estimate=cost(1e6, 28 * sum(s[0].size for s in states)),
    )(here(), *sources, *flat)
    return [out[4 * t : 4 * t + 4] for t in range(len(states))], out[-1]


def finish_kernel(*refs):
    norms = jnp.sqrt(refs[0][...] + refs[1][...])
    refs = refs[2:]
    refs[12][...] = norms
    for t in range(4):
        factor = 0.3 * (norms[t + 4 : t + 5, 0:1] / (norms[t : t + 1, 0:1] + 1e-06))
        refs[8 + t][...] = refs[t][...] - factor * refs[4 + t][...]


def finish(masters, updates, parts):
    rows = lambda v: pl.BlockSpec((v.shape[0] // 4, v.shape[1]), lambda j: (j, 0))
    whole = lambda: pl.BlockSpec((8, 128), lambda j: (0, 0))
    out = pl.pallas_call(
        finish_kernel,
        name="finish",
        grid=(4,),
        in_specs=[whole() for _ in parts] + [rows(v) for v in masters + updates],
        out_specs=[rows(v) for v in masters] + [whole()],
        out_shape=[shaped(v.shape, f32) for v in masters] + [shaped((8, 128), f32)],
        compiler_params=params(),
        cost_estimate=cost(1e6, 12 * sum(v.size for v in masters)),
    )(*parts, *masters, *updates)
    return out[:4], out[4]


def body(fast, tokens, cotangent, image_ids, patch_grid, *state):
    masters, vectors = state[:4], state[4]
    firsts, vector_first = state[5:9], state[9]
    seconds, vector_second = state[10:14], state[14]
    n, w = tokens.shape
    size = vectors.shape[0]
    heads = w // HD
    count = w // 128 // PAIRS
    L = 128 * PAIRS
    low = [rnd(m) for m in masters]
    gather = lambda v: lax.all_gather(v, "fsdp", axis=0, tiled=True)
    scatter = lambda v: lax.psum_scatter(v, "fsdp", scatter_dimension=0, tiled=True)
    whole = jnp.zeros((1,), jnp.int32)
    d, z, c = place()
    mine = jnp.stack([c]).astype(jnp.int32)
    halves = lambda x_t, y: (outer(x_t, y, 1 - mine, 4, 2), outer(x_t, y, mine, 4, 2))
    join = lambda rows: jnp.concatenate(rows, axis=-1)

    if fast:
        q_rows = low[0].shape[0] // 4
        row = jnp.pad(rnd(vectors), (0, low[0].shape[1] - size)).reshape(1, -1)
        got = spread_z(jnp.concatenate([quarter(low[0], d), row], 0))
        qkv_column = jnp.stack([g[:q_rows] for g in got])
        packed = jnp.concatenate(by_index([g[q_rows:, :size] for g in got], z), 0)
        other = over_core(packed)
        packed = jnp.stack([jnp.where(c == 0, packed, other), jnp.where(c == 0, other, packed)], 1)
        packed = packed.reshape(-1)
        up_part, out_part, down_part, qkv_column = tie(
            quarter(low[2], d), low[1], low[3], qkv_column
        )
        full_out = gather(out_part)
        qkv_own = spread_dp(qkv_column)
        up_column = jnp.stack(spread_z(up_part))
        full_down = gather(down_part)
    else:
        packed = gather(rnd(vectors))
        full_qkv, full_out, full_up, full_down = [gather(v) for v in low]
    vec = up(packed).reshape(1, -1)
    freq = vec[0, -w:].reshape(2, heads, 1, HD // 2)
    freq = jnp.broadcast_to(freq, (2, heads, 2, HD // 2)).reshape(2, w)
    grid_t = patch_grid.T
    given = jnp.where((image_ids >= 0)[:, None], cotangent, jnp.zeros_like(cotangent))
    grad_bias_down = jnp.sum(up(given), axis=0, keepdims=True)
    aug_q, aug_k, rng = tables(image_ids)

    normed, normed_t, cos, sin = first(tokens, vec, freq, grid_t)
    if fast:
        normed, *qkv_own = tie(normed, *qkv_own)
        full_qkv = arrange(qkv_own, [over_core(v) for v in qkv_own])
        up_column, full_qkv = tie(up_column, full_qkv)
        up_own = spread_dp(up_column)
    qkv = project(normed, full_qkv, vec, cos, sin)
    mix, mix_t, lb = attend(qkv, aug_q, aug_k, rng)
    if fast:
        mix, *up_own = tie(mix, *up_own)
        up_other = [over_core(v) for v in up_own]
    resid, normed_two, normed_two_t = branch(tokens, mix, full_out, vec)
    if fast:
        full_up = arrange(up_own, up_other)
    active, active_t, slope = hidden_units(normed_two, full_up, vec)
    if fast:
        theirs, own = halves(active_t, given)
        pieces = fold_core([own], [over_core(theirs)])
        active, slope, full_down = tie(active, slope, full_down)
        active, slope, *pieces = tie(active, slope, *pieces)
        got = [over_dp(v, k) for k, v in zip((1, 2, 3), pieces[1:])]
    else:
        down_full = outer(active_t, given, whole, 1, 1)[0]
    output = last(active, full_down, resid, vec)
    grad_hidden, grad_bias_up = hidden_back(given, full_down, slope)
    if fast:
        output, grad_hidden, *got = tie(output, grad_hidden, *got)
        down_z = fold_dp(pieces[0], got)
        grad_hidden, *down_z = tie(grad_hidden, *down_z)
        got = [down_z[0]] + [over_z(v, k) for k, v in zip((1, 2, 3), down_z[1:])]
        theirs, own = halves(normed_two_t, grad_hidden)
        own, *got = tie(own, *got)
        down_f = fold_z(got)
        more = down_f.reshape(4, -1, w)
        pieces = fold_core([own], [over_core(theirs)], more)
        grad_hidden, down_f, *pieces = tie(grad_hidden, down_f, *pieces)
        got = [over_dp(v, k) for k, v in zip((1, 2, 3), pieces[1:])]
    else:
        up_full = outer(normed_two_t, grad_hidden, whole, 1, 1)[0]
    grad_resid, grad_branch, grad_mix, sums_two = second_back(
        grad_hidden, full_up, resid, given, vec, full_out
    )
    if fast:
        out_theirs, out_own = halves(mix_t, grad_branch)
        out_sent = over_core(out_theirs)
    else:
        out_full = outer(mix_t, grad_branch, whole, 1, 1)[0]
    projs, sums_proj, sums_freq, qkv_parts = [], [], [], []
    for part in range(count):
        dq, dk, dv = attend_back(part, qkv, grad_mix, mix, lb, aug_q, aug_k, rng)
        if fast and part == 0:
            dq, *got = tie(dq, *got)
            up_width = pieces[0].shape[2]
            q = down_f.shape[0] // 4

            def read_down(i, q, skip, ref, k):
                return ref[i, :, skip:] if k else ref[q * i : q * i + q]

            plan = [[(q * i, q, 0, w, partial(read_down, i, q, up_width)) for i in range(4)]]
            later = [(plan, [down_f] + got, (masters[3], firsts[3], seconds[3]))]
            up_z = fold_dp(pieces[0], got)
            dq, *up_z = tie(dq, *up_z)
            got = [up_z[0]] + [over_z(v, k) for k, v in zip((1, 2, 3), up_z[1:])]
        if fast and part > 0:
            dq, *got = tie(dq, *got)
        gp, bs, fs = turn_back(part, dq, dk, dv, qkv, cos, sin, grid_t)
        projs.append(gp)
        sums_proj.append(bs)
        sums_freq.append(fs)
        if not fast:
            qkv_parts.append(outer(normed_t, gp, whole, 1, 1)[0])
        elif part == 0:
            theirs, own = halves(normed_t, gp)
            own, *got = tie(own, *got)
            up_f = fold_z(got)
            pieces = fold_core([own, out_own], [over_core(theirs), out_sent], up_f)
            grad_mix, up_f, *pieces = tie(grad_mix, up_f, *pieces)
            got = [over_dp(v, k) for k, v in zip((1, 2, 3), pieces[1:])]
        else:
            a_width = pieces[0].shape[2]
            q, wide = up_f.shape[0], up_f.shape[1] // 4

            def read_up(i, wide, skip, ref, k):
                return ref[i, :, skip:] if k else ref[:, wide * i : wide * i + wide]

            plan = [
                [(0, q, wide * i, wide, partial(read_up, i, wide, a_width)) for i in range(4)]
            ]
            later.append((plan, [up_f] + got, (masters[2], firsts[2], seconds[2])))
            theirs, own = halves(normed_t, gp)
            a_z = fold_dp(pieces[0], got)
            pieces = fold_core([own], [over_core(theirs)])
            projs[-1], *pieces = tie(gp, *pieces)
            got = [over_dp(v, k) for k, v in zip((1, 2, 3), pieces[1:])]
    freq_sums = join([s[:2] for s in sums_freq]).reshape(2, heads, 2, HD // 2)
    freq_grad = (freq_sums[:, :, 0] - freq_sums[:, :, 1]).reshape(1, -1)
    if fast:
        projs[-1], freq_grad = tie(projs[-1], freq_grad)
    tokens_grad, vector_full = first_back(
        projs, sums_proj, full_qkv, tokens, grad_resid, vec, sums_two, grad_bias_up, grad_bias_down, freq_grad
    )
    if fast:
        vector_full, *got = tie(vector_full, *got)
    off = vector_full.shape[1] - 2 * w
    if fast:
        flat = vector_full + over_core(vector_full)
        sends = pack(flat, size, off, w, [pieces[0]] + got, a_z)
        got = [sends[0]] + [over_z(s, k) for k, s in zip((1, 2, 3), sends[1:])]
        held = tie(*[v for entry in later for v in entry[1]], *sends)
        (down_step, down_square), (up_step, up_square) = [
            step(entry[0], 3 - i, list(held[4 * i : 4 * i + 4]), [entry[2]])
            for i, entry in enumerate(later)
        ]
        up_square, down_square, *got = tie(up_square, down_square, *got)
        got = spread_dp(rnd(pairs([up(g) for g in got])))
        tail = pairs([up(g[q_rows:]) for g in got])[0]
        room = -(-size // 128) * 128
        vector_grad = tail[:size]
        down_bias_grad = tail[room : room + w]

        def read(col, ref, k):
            return ref[:q_rows, col : col + L]

        plan = [
            [
                (0, q_rows, (s * count + p) * L, L, partial(read, p * (3 * L + w) + s * L))
                for p in range(count)
                for s in range(3)
            ],
            [(0, q_rows, i * L, L, partial(read, 3 * L + i * L)) for i in range(w // L)],
        ]
        states = [(masters[k], firsts[k], seconds[k]) for k in (0, 1)]
        last_steps, last_squares = step(plan, 0, got, states)
        steps = last_steps + up_step + down_step
        squares = last_squares + up_square + down_square
        squares = squares + over_core(squares)
        squares = squares + over_z(squares, 1)
        squares = [squares, over_z(squares, 2)]
        new_list, norms = finish(list(masters), [s[3] for s in steps], squares)
        update_norms, weight_norms = norms[:4, 0], norms[4:, 0]
    else:
        give = lambda v: lax.psum(scatter(up(v)), "dp")
        up_grad, down_grad, out_grad = give(up_full), give(down_full), give(out_full)
        done = [give(v) for v in qkv_parts]
        vector_grad = give(vector_full[0])
        down_bias_grad = lax.psum(grad_bias_down[0], ("dp", "fsdp"))
        qkv_grad = join([g[:, s * L : (s + 1) * L] for s in range(3) for g in done])
        steps = [
            (g, *adam_terms(g, firsts[k], seconds[k], masters[k], 0.01))
            for k, g in enumerate((qkv_grad, out_grad, up_grad, down_grad))
        ]
        weight_local = jnp.stack([jnp.sum(m * m) for m in masters])
        update_local = jnp.stack([jnp.sum(s[3] * s[3]) for s in steps])
        both = jnp.sqrt(lax.psum(jnp.stack([weight_local, update_local]), "fsdp"))
        weight_norms, update_norms = both[0], both[1]
        factor = 0.3 * (weight_norms / (update_norms + 1e-06))
        new_list = [masters[k] - factor[k] * steps[k][3] for k in range(4)]
    vector_step = adam_terms(vector_grad, vector_first, vector_second, vectors, 0.0)
    return (
        output,
        tokens_grad,
        *[s[0] for s in steps],
        vector_grad,
        down_bias_grad,
        *[s[1] for s in steps],
        vector_step[0],
        *[s[2] for s in steps],
        vector_step[1],
        *new_list,
        vectors - 0.2 * vector_step[2],
        weight_norms,
        update_norms,
    )


def solution(mesh):
    both = P(("dp", "fsdp"), None)
    mat = [P("fsdp", None)] * 4 + [P("fsdp")]
    in_specs = (both, both, P(("dp", "fsdp")), P(None, ("dp", "fsdp")), *mat, *mat, *mat)
    out_specs = (both, both, *mat, P(), *mat, *mat, *mat, P(), P())
    fast = mesh.shape["dp"] == 4 and mesh.shape["fsdp"] == 8
    return jax.shard_map(
        partial(body, fast), mesh=mesh, in_specs=in_specs, out_specs=out_specs, check_vma=False
    )
```

```python
from functools import partial

import jax
import jax.numpy as jnp
from jax import lax
from jax.experimental import pallas as pl
from jax.experimental.pallas import tpu as pltpu
from jax.sharding import PartitionSpec as P

H = 12
HD = 64
STEP = 10
QT = 256
KT = 128
PAIRS = 3
VARIANTS = (2, 3, 4, 5, 7, 8)
norm_eps = 1e-06
bf = jnp.bfloat16
f32 = jnp.float32


def nt(a, b):
    return lax.dot_general(a, b, (((1,), (1,)), ((), ())), preferred_element_type=f32)


def nn(a, b):
    return lax.dot_general(a, b, (((1,), (0,)), ((), ())), preferred_element_type=f32)


def rnd(v):
    return v.astype(bf)


def up(v):
    return v.astype(f32)


def params(mib=22):
    return pltpu.CompilerParams(vmem_limit_bytes=mib << 20)


def cost(flops, moved):
    return pl.CostEstimate(flops=int(flops), bytes_accessed=int(moved), transcendentals=0)


def shaped(shape, kind):
    return jax.ShapeDtypeStruct(shape, kind)


def row_norm(v):
    centre = jnp.mean(v, axis=-1, keepdims=True)
    centred = v - centre
    spread = jnp.mean(centred * centred, axis=-1, keepdims=True)
    scale = lax.rsqrt(spread + norm_eps)
    return centred * scale, scale


def split3(x):
    a = rnd(x)
    r = x - up(a)
    b = rnd(r)
    return jnp.concatenate([a, b, rnd(r - up(b))], axis=0)


def first_kernel(tok_ref, vec_ref, freq_ref, grid_ref, n_ref, nt_ref, cos_ref, sin_ref, table):
    w = tok_ref.shape[1]

    @pl.when(pl.program_id(0) == 0)
    def _():
        place_of = lax.broadcasted_iota(jnp.int32, (32, w), 0).astype(f32)
        for axis in (0, 1):
            angle = place_of * freq_ref[axis : axis + 1, :]
            table[2 * axis] = split3(jnp.cos(angle))
            table[2 * axis + 1] = split3(jnp.sin(angle))

    hat, scale = row_norm(up(tok_ref[...]))
    normed = hat * vec_ref[:, :w] + vec_ref[:, w : 2 * w]
    n_ref[...] = rnd(normed)
    nt_ref[...] = rnd(normed.T)
    g = grid_ref[...]
    index = lax.broadcasted_iota(jnp.int32, (1, 96), 1) & 31
    hot = [rnd(jnp.where(g[:, axis : axis + 1] == index, 1.0, 0.0)) for axis in (0, 1)]
    cos_row, sin_row = nn(hot[0], table[0]), nn(hot[0], table[1])
    cos_col, sin_col = nn(hot[1], table[2]), nn(hot[1], table[3])
    lane = lax.broadcasted_iota(jnp.int32, (1, w), 1)
    cos_ref[...] = cos_row * cos_col - sin_row * sin_col
    s = sin_row * cos_col + cos_row * sin_col
    sin_ref[...] = jnp.where(lane & 63 < 32, -s, s)


def first(tokens, vec, freq, grid_t):
    n, w = tokens.shape
    rows = lambda: pl.BlockSpec((QT, w), lambda i: (i, 0))
    whole = lambda a: pl.BlockSpec(a.shape, lambda i: (0, 0))
    return pl.pallas_call(
        first_kernel,
        name="first",
        grid=(n // QT,),
        in_specs=[rows(), whole(vec), whole(freq), pl.BlockSpec((QT, 2), lambda i: (i, 0))],
        out_specs=[rows(), pl.BlockSpec((w, QT), lambda i: (0, i)), rows(), rows()],
        out_shape=[shaped((n, w), bf), shaped((w, n), bf), shaped((n, w), f32), shaped((n, w), f32)],
        scratch_shapes=[pltpu.VMEM((4, 96, w), bf)],
        compiler_params=params(),
        cost_estimate=cost(5e9, 1e7),
    )(tokens, vec, freq, grid_t)


def swap(v):
    w = v.shape[1]
    lane = lax.broadcasted_iota(jnp.int32, (1, w), 1)
    return jnp.where(lane & 63 < 32, pltpu.roll(v, w - 32, 1), pltpu.roll(v, 32, 1))


def project_kernel(n_ref, w_ref, b_ref, cos_ref, sin_ref, o_ref):
    j = pl.program_id(0)
    u = nn(n_ref[...], w_ref[...]) + b_ref[...]

    @pl.when(j < 2)
    def _():
        turned = u * cos_ref[...] + swap(u) * sin_ref[...]
        o_ref[...] = rnd(turned * jnp.where(j < 1, 0.125, 1.0))

    @pl.when(j >= 2)
    def _():
        o_ref[...] = rnd(u)


def project(normed, weight, vec, cos, sin):
    n, w = normed.shape
    whole = lambda: pl.BlockSpec((n, w), lambda j: (0, 0))
    return pl.pallas_call(
        project_kernel,
        name="project",
        grid=(3,),
        in_specs=[
            whole(),
            pl.BlockSpec((w, w), lambda j: (0, j)),
            pl.BlockSpec((1, w), lambda j: (0, 4 + j)),
            whole(),
            whole(),
        ],
        out_specs=pl.BlockSpec((n, w), lambda j: (0, j)),
        out_shape=shaped((n, 3 * w), bf),
        compiler_params=params(22),
        cost_estimate=cost(8e9, 1e7),
    )(normed, weight, vec, cos, sin)


def tables(ids):
    n = ids.shape[0]
    lane = jnp.arange(128) & 63
    one = (ids[:, None] + 1 == lane[None]).astype(f32)
    small = (lane < 8)[None]
    aug_q = rnd(jnp.where(small, one, 0.0))
    aug_k = rnd(jnp.where(small, (one - 1.0) * 1e30, jnp.where((lane < 11)[None], 1.0, 0.0)))
    tiles = n // QT
    hit = (ids.reshape(tiles, QT, 1) == ids[None, None, :]).any(1)
    pos = jnp.arange(n)[None]
    lo = jnp.min(jnp.where(hit, pos, n), 1) // KT
    hi = jnp.max(jnp.where(hit, pos, -1), 1) // KT + 1
    need = hi - lo
    width = jnp.full_like(need, VARIANTS[-1])
    for v in VARIANTS[::-1]:
        width = jnp.where(need <= v, v, width)
    start = jnp.minimum(lo, n // KT - width)
    return aug_q, aug_k, jnp.stack([start, width]).astype(jnp.int32)


def low_lanes():
    return lax.broadcasted_iota(jnp.int32, (1, 128), 1) < 64


def attend_kernel(rng, q_ref, k_ref, v_ref, aq_ref, ak_ref, mix_ref, mixt_ref, lb_ref, vt):
    i = pl.program_id(1)
    n = k_ref.shape[0]
    start = rng[0, i]
    width = rng[1, i]
    low = low_lanes()

    @pl.when(i == 0)
    def _():
        one = jnp.ones((16, n), bf)
        for p in range(PAIRS):
            t = v_ref[:, 128 * p : 128 * p + 128].T
            for h in (0, 1):
                vt[2 * p + h, :64, :] = t[64 * h : 64 * h + 64]
                vt[2 * p + h, 64:, :] = one

    aq = aq_ref[...]
    for W in VARIANTS:

        @pl.when(width == W)
        def _():
            at = pl.ds(pl.multiple_of(start * KT, KT), W * KT)
            ak = ak_ref[at, :]
            scores = []
            for p in range(PAIRS):
                c = slice(128 * p, 128 * p + 128)
                q = q_ref[:, c]
                k = k_ref[at, c]
                scores.append(nt(jnp.where(low, k, ak), jnp.where(low, q, aq)))
                scores.append(nt(jnp.where(low, ak, k), jnp.where(low, aq, q)))
            for p in range(PAIRS):
                c = slice(128 * p, 128 * p + 128)
                outs = []
                for h in (0, 1):
                    s = scores[2 * p + h]
                    m = jnp.max(s, axis=0, keepdims=True)
                    e = rnd(jnp.exp(s - m))
                    o = nn(vt[2 * p + h, :, at], e)
                    t = o[64:65]
                    outs.append(o[:64] * (1.0 / t))
                    lb_ref[p, h : h + 1, :] = m + jnp.log(t)
                both = jnp.concatenate(outs, 0)
                mix_ref[:, c] = rnd(both.T)
                mixt_ref[c, :] = rnd(both)


def attend(qkv, aug_q, aug_k, rng):
    n, w3 = qkv.shape
    w = w3 // 3
    L = 128 * PAIRS
    g = w // L
    spec = pltpu.PrefetchScalarGridSpec(
        num_scalar_prefetch=1,
        grid=(g, n // QT),
        in_specs=[
            pl.BlockSpec((QT, L), lambda p, i, r: (i, p)),
            pl.BlockSpec((n, L), lambda p, i, r: (0, g + p)),
            pl.BlockSpec((n, L), lambda p, i, r: (0, 2 * g + p)),
            pl.BlockSpec((QT, 128), lambda p, i, r: (i, 0)),
            pl.BlockSpec((n, 128), lambda p, i, r: (0, 0)),
        ],
        out_specs=[
            pl.BlockSpec((QT, L), lambda p, i, r: (i, p)),
            pl.BlockSpec((L, QT), lambda p, i, r: (p, i)),
            pl.BlockSpec((PAIRS, 8, QT), lambda p, i, r: (p, 0, i)),
        ],
        scratch_shapes=[pltpu.VMEM((2 * PAIRS, 80, n), bf)],
    )
    return pl.pallas_call(
        attend_kernel,
        name="attend",
        grid_spec=spec,
        out_shape=[shaped((n, w), bf), shaped((w, n), bf), shaped((w // 128, 8, n), f32)],
        compiler_params=params(),
        cost_estimate=cost(2.3e10, 1e7),
    )(rng, qkv, qkv, qkv, aug_q, aug_k)


def fill(aug, x):
    lane = lax.broadcasted_iota(jnp.int32, (1, 128), 1) & 63
    a = rnd(x)
    r = x - up(a)
    b = rnd(r)
    c = rnd(r - up(b))
    return jnp.where(lane == 8, a, jnp.where(lane == 9, b, jnp.where(lane == 10, c, aug)))


def attend_back_kernel(
    rng, q_ref, k_ref, v_ref, g_ref, mix_ref, lb_ref, aq_ref, ak_ref,
    dq_ref, dk_ref, dv_ref, dk_acc, dv_acc,
):
    i = pl.program_id(0)
    start = rng[0, i]
    width = rng[1, i]

    @pl.when(i == 0)
    def _():
        dk_acc[...] = jnp.zeros_like(dk_acc)
        dv_acc[...] = jnp.zeros_like(dv_acc)

    low = low_lanes()
    aq0 = aq_ref[...]
    zero = jnp.zeros((1, 128), bf)
    held = []
    for p in range(PAIRS):
        c = slice(128 * p, 128 * p + 128)
        q = q_ref[:, c]
        g = g_ref[:, c]
        prod = up(g) * up(mix_ref[:, c])
        even = jnp.sum(jnp.where(low, prod, 0.0), axis=1, keepdims=True)
        odd = jnp.sum(jnp.where(low, 0.0, prod), axis=1, keepdims=True)
        lt = lb_ref[p].T
        aq = fill(aq0, -jnp.where(low, lt[:, 1:2], lt[:, 0:1]))
        ag = fill(zero, -jnp.where(low, odd, even))
        held.append(
            (
                (jnp.where(low, q, aq), jnp.where(low, aq, q)),
                (jnp.where(low, g, ag), jnp.where(low, ag, g)),
                q.T,
                g.T,
            )
        )
    for W in VARIANTS:

        @pl.when(width == W)
        def _():
            at = pl.ds(pl.multiple_of(start * KT, KT), W * KT)
            ak = ak_ref[at, :]
            for p in range(PAIRS):
                c = slice(128 * p, 128 * p + 128)
                qs, gs, qt, gt = held[p]
                k = k_ref[at, c]
                v = v_ref[at, c]
                one = jnp.ones_like(v)
                ks = (jnp.where(low, k, ak), jnp.where(low, ak, k))
                vs = (jnp.where(low, v, one), jnp.where(low, one, v))
                dqs = []
                for h in (0, 1):
                    e = jnp.exp(nt(qs[h], ks[h]))
                    ds = rnd(e * nt(gs[h], vs[h]))
                    e = rnd(e)
                    half = slice(64 * h, 64 * h + 64)
                    to = slice(128 * p + 64 * h, 128 * p + 64 * h + 64)
                    dqs.append(nn(ds, k))
                    dk_acc[to, at] += nn(qt[half], ds)
                    dv_acc[to, at] += nn(gt[half], e)
                dq_ref[:, c] = jnp.where(low, dqs[0], dqs[1]) * 0.125

    @pl.when(i == pl.num_programs(0) - 1)
    def _():
        dk_ref[...] = dk_acc[...].T
        dv_ref[...] = rnd(dv_acc[...].T)


def attend_back(part, qkv, g_mix, mix, lb, aug_q, aug_k, rng):
    n, w3 = qkv.shape
    L = 128 * PAIRS
    g = w3 // 3 // L
    spec = pltpu.PrefetchScalarGridSpec(
        num_scalar_prefetch=1,
        grid=(n // QT,),
        in_specs=[
            pl.BlockSpec((QT, L), lambda i, r: (i, part)),
            pl.BlockSpec((n, L), lambda i, r: (0, g + part)),
            pl.BlockSpec((n, L), lambda i, r: (0, 2 * g + part)),
            pl.BlockSpec((QT, L), lambda i, r: (i, part)),
            pl.BlockSpec((QT, L), lambda i, r: (i, part)),
            pl.BlockSpec((PAIRS, 8, QT), lambda i, r: (part, 0, i)),
            pl.BlockSpec((QT, 128), lambda i, r: (i, 0)),
            pl.BlockSpec((n, 128), lambda i, r: (0, 0)),
        ],
        out_specs=[
            pl.BlockSpec((QT, L), lambda i, r: (i, 0)),
            pl.BlockSpec((n, L), lambda i, r: (0, 0)),
            pl.BlockSpec((n, L), lambda i, r: (0, 0)),
        ],
        scratch_shapes=[pltpu.VMEM((L, n), f32), pltpu.VMEM((L, n), f32)],
    )
    return pl.pallas_call(
        attend_back_kernel,
        name="attend_back",
        grid_spec=spec,
        out_shape=[shaped((n, L), f32), shaped((n, L), f32), shaped((n, L), bf)],
        compiler_params=params(),
        cost_estimate=cost(2.2e10, 1e7),
    )(rng, qkv, qkv, qkv, g_mix, mix, lb, aug_q, aug_k)


def branch_kernel(tok_ref, mix_ref, w_ref, vec_ref, res_ref, n_ref, nt_ref):
    w = tok_ref.shape[1]
    resid = up(tok_ref[...]) + nn(mix_ref[...], w_ref[...]) + vec_ref[:, 7 * w : 8 * w]
    res_ref[...] = resid
    hat, scale = row_norm(resid)
    normed = hat * vec_ref[:, 2 * w : 3 * w] + vec_ref[:, 3 * w : 4 * w]
    n_ref[...] = rnd(normed)
    nt_ref[...] = rnd(normed.T)


def branch(tokens, mix, weight, vec):
    n, w = tokens.shape
    rows = lambda: pl.BlockSpec((QT, w), lambda i: (i, 0))
    whole = lambda a: pl.BlockSpec(a.shape, lambda i: (0, 0))
    return pl.pallas_call(
        branch_kernel,
        name="branch",
        grid=(n // QT,),
        in_specs=[rows(), rows(), whole(weight), whole(vec)],
        out_specs=[rows(), rows(), pl.BlockSpec((w, QT), lambda i: (0, i))],
        out_shape=[shaped((n, w), f32), shaped((n, w), bf), shaped((w, n), bf)],
        compiler_params=params(22),
        cost_estimate=cost(4e9, 1e7),
    )(tokens, mix, weight, vec)


def gelu_parts(x):
    cdf = 0.5 + 0.5 * lax.erf(x * 0.7071067811865476)
    return x * cdf, cdf + x * (jnp.exp(x * x * -0.5) * 0.3989422804014327)


def hidden_kernel(n_ref, w_ref, b_ref, a_ref, at_ref, d_ref):
    x = nn(n_ref[...], w_ref[...]) + b_ref[...]
    active, slope = gelu_parts(x)
    active = rnd(active)
    a_ref[...] = active
    at_ref[...] = active.T
    d_ref[...] = rnd(slope)


def hidden_units(normed, weight, vec):
    n, w = normed.shape
    ff = weight.shape[1]
    B = 768
    off = 8 * w // B
    return pl.pallas_call(
        hidden_kernel,
        name="hidden",
        grid=(ff // B,),
        in_specs=[
            pl.BlockSpec((n, w), lambda j: (0, 0)),
            pl.BlockSpec((w, B), lambda j: (0, j)),
            pl.BlockSpec((1, B), lambda j: (0, off + j)),
        ],
        out_specs=[
            pl.BlockSpec((n, B), lambda j: (0, j)),
            pl.BlockSpec((B, n), lambda j: (j, 0)),
            pl.BlockSpec((n, B), lambda j: (0, j)),
        ],
        out_shape=[shaped((n, ff), bf), shaped((ff, n), bf), shaped((n, ff), bf)],
        compiler_params=params(30),
        cost_estimate=cost(1.5e10, 1e7),
    )(normed, weight, vec)


def last_kernel(a_ref, w_ref, res_ref, b_ref, o_ref):
    o_ref[...] = rnd(res_ref[...] + nn(a_ref[...], w_ref[...]) + b_ref[...])


def last(active, weight, resid, vec):
    n, ff = active.shape
    w = resid.shape[1]
    off = (8 * w + ff) // w
    return pl.pallas_call(
        last_kernel,
        name="last",
        grid=(n // QT,),
        in_specs=[
            pl.BlockSpec((QT, ff), lambda i: (i, 0)),
            pl.BlockSpec((ff, w), lambda i: (0, 0)),
            pl.BlockSpec((QT, w), lambda i: (i, 0)),
            pl.BlockSpec((1, w), lambda i: (0, off)),
        ],
        out_specs=pl.BlockSpec((QT, w), lambda i: (i, 0)),
        out_shape=shaped((n, w), bf),
        compiler_params=params(),
        cost_estimate=cost(6e9, 1e7),
    )(active, weight, resid, vec)


def hidden_back_kernel(g_ref, w_ref, d_ref, gh_ref, sum_ref):
    gh = rnd(nt(g_ref[...], w_ref[...]) * up(d_ref[...]))
    gh_ref[...] = gh
    sum_ref[...] = jnp.sum(up(gh), axis=0, keepdims=True)


def hidden_back(given, weight, slope):
    n, w = given.shape
    ff = weight.shape[0]
    B = 768
    return pl.pallas_call(
        hidden_back_kernel,
        name="hidden_back",
        grid=(ff // B,),
        in_specs=[
            pl.BlockSpec((n, w), lambda j: (0, 0)),
            pl.BlockSpec((B, w), lambda j: (j, 0)),
            pl.BlockSpec((n, B), lambda j: (0, j)),
        ],
        out_specs=[pl.BlockSpec((n, B), lambda j: (0, j)), pl.BlockSpec((1, B), lambda j: (0, j))],
        out_shape=[shaped((n, ff), bf), shaped((1, ff), f32)],
        compiler_params=params(),
        cost_estimate=cost(8e9, 1e7),
    )(given, weight, slope)


def norm_back(grad, hat, scale, gain):
    d = grad * gain
    a = jnp.mean(d, axis=-1, keepdims=True)
    b = jnp.mean(d * hat, axis=-1, keepdims=True)
    return (d - a - hat * b) * scale


def second_back_kernel(gh_ref, w_ref, res_ref, cot_ref, vec_ref, wo_ref, gr_ref, gb_ref, gm_ref, sum_ref):
    i = pl.program_id(0)
    w = res_ref.shape[1]
    grad = nt(gh_ref[...], w_ref[...])
    hat, scale = row_norm(res_ref[...])
    total = up(cot_ref[...]) + norm_back(grad, hat, scale, vec_ref[:, 2 * w : 3 * w])
    gr_ref[...] = total
    low = rnd(total)
    gb_ref[...] = low
    gm_ref[...] = rnd(nt(low, wo_ref[...]))
    sums = jnp.concatenate(
        [
            jnp.sum(grad * hat, axis=0, keepdims=True),
            jnp.sum(grad, axis=0, keepdims=True),
            jnp.sum(up(low), axis=0, keepdims=True),
        ],
        axis=0,
    )

    @pl.when(i == 0)
    def _():
        sum_ref[...] = jnp.zeros_like(sum_ref)

    sum_ref[0:3, :] += sums


def second_back(gh, weight, resid, given, vec, out_w):
    n, ff = gh.shape
    w = resid.shape[1]
    rows = lambda c: pl.BlockSpec((QT, c), lambda i: (i, 0))
    whole = lambda a: pl.BlockSpec(a.shape, lambda i: (0, 0))
    return pl.pallas_call(
        second_back_kernel,
        name="second_back",
        grid=(n // QT,),
        in_specs=[rows(ff), whole(weight), rows(w), rows(w), whole(vec), whole(out_w)],
        out_specs=[rows(w), rows(w), rows(w), pl.BlockSpec((8, w), lambda i: (0, 0))],
        out_shape=[shaped((n, w), f32), shaped((n, w), bf), shaped((n, w), bf), shaped((8, w), f32)],
        compiler_params=params(),
        cost_estimate=cost(9e9, 1e7),
    )(gh, weight, resid, given, vec, out_w)


def outer_kernel(sel, x_ref, y_ref, o_ref):
    z, one, r, n = x_ref.shape
    got = nn(x_ref[...].reshape(z * r, n), y_ref[...])
    o_ref[...] = rnd(got).reshape(o_ref.shape)


def outer(x_t, y, sel, groups, share):
    rows, n = x_t.shape
    c = y.shape[1]
    r = rows // (groups * share)
    B = 1536 if c % 1536 == 0 and groups > 1 else 768 if c % 768 == 0 else c if c < 1536 and c % 128 == 0 else 256
    spec = pltpu.PrefetchScalarGridSpec(
        num_scalar_prefetch=1,
        grid=(c // B,),
        in_specs=[
            pl.BlockSpec((groups, 1, r, n), lambda j, s: (0, s[0], 0, 0)),
            pl.BlockSpec((n, B), lambda j, s: (0, j)),
        ],
        out_specs=pl.BlockSpec((groups, r, B), lambda j, s: (0, 0, j)),
    )
    return pl.pallas_call(
        outer_kernel,
        name="outer",
        grid_spec=spec,
        out_shape=shaped((groups, r, c), bf),
        compiler_params=params(),
        cost_estimate=cost(4 * groups * r * c * n, 1e7),
    )(sel, x_t.reshape(groups, share, r, n), y)


def turn_back_kernel(
    dq_ref, dk_ref, dv_ref, q_ref, k_ref, cos_ref, sin_ref, grid_ref, gp_ref, b_ref, f_ref
):
    i = pl.program_id(0)
    w = cos_ref.shape[1]
    cos = cos_ref[...]
    sin = sin_ref[...]
    dq = dq_ref[...]
    dk = dk_ref[...]
    gv = dv_ref[...]
    sq = swap(dq)
    sk = swap(dk)
    t = sq * (up(q_ref[...]) * 8.0) + sk * up(k_ref[...])
    g = up(grid_ref[...])
    gq = rnd(dq * cos - sq * sin)
    gk = rnd(dk * cos - sk * sin)
    gp_ref[:, :w] = gq
    gp_ref[:, w : 2 * w] = gk
    gp_ref[:, 2 * w :] = gv
    add = lambda v: jnp.sum(v, axis=0, keepdims=True)

    @pl.when(i == 0)
    def _():
        b_ref[...] = jnp.zeros_like(b_ref)
        f_ref[...] = jnp.zeros_like(f_ref)

    b_ref[0:3, :] += jnp.concatenate([add(up(gq)), add(up(gk)), add(up(gv))], axis=0)
    f_ref[0:2, :] += jnp.concatenate([add(t * g[:, 0:1]), add(t * g[:, 1:2])], axis=0)


def turn_back(part, dq, dk, dv, qkv, cos, sin, grid_t):
    n, L = dq.shape
    g = qkv.shape[1] // 3 // L
    rows = lambda c, j=0: pl.BlockSpec((QT, c), lambda i: (i, j))
    fixed = lambda: pl.BlockSpec((8, L), lambda i: (0, 0))
    return pl.pallas_call(
        turn_back_kernel,
        name="turn_back",
        grid=(n // QT,),
        in_specs=[rows(L), rows(L), rows(L), rows(L, part), rows(L, g + part)]
        + [rows(L, part), rows(L, part), pl.BlockSpec((QT, 2), lambda i: (i, 0))],
        out_specs=[rows(3 * L), fixed(), fixed()],
        out_shape=[shaped((n, 3 * L), bf), shaped((8, L), f32), shaped((8, L), f32)],
        compiler_params=params(16),
        cost_estimate=cost(4e9, 1e7),
    )(dq, dk, dv, qkv, qkv, cos, sin, grid_t)


def first_back_kernel(parts, *refs):
    gp_refs, proj_refs = refs[:parts], refs[parts : 2 * parts]
    w_ref, tok_ref, gr_ref, vec_ref, two_ref, up_ref, down_ref, freq_ref, o_ref, flat_ref, sums = refs[
        2 * parts :
    ]
    i = pl.program_id(0)
    w = tok_ref.shape[1]
    L = w // parts
    gp = [r[:, s * L : (s + 1) * L] for s in range(3) for r in gp_refs]
    grad = nt(jnp.concatenate(gp, axis=1), w_ref[...])
    hat, scale = row_norm(up(tok_ref[...]))
    o_ref[...] = rnd(gr_ref[...] + norm_back(grad, hat, scale, vec_ref[:, :w]))

    @pl.when(i == 0)
    def _():
        sums[...] = jnp.zeros_like(sums)

    sums[0:1, :] += jnp.sum(grad * hat, axis=0, keepdims=True)
    sums[1:2, :] += jnp.sum(grad, axis=0, keepdims=True)

    @pl.when(i == pl.num_programs(0) - 1)
    def _():
        pieces = [sums[0:1, :], sums[1:2, :], two_ref[0:1, :], two_ref[1:2, :]]
        pieces += [r[s : s + 1, :] for s in range(3) for r in proj_refs]
        pieces += [two_ref[2:3, :], up_ref[...], down_ref[...], freq_ref[...]]
        col = 0
        for v in pieces:
            flat_ref[:, col : col + v.shape[1]] = v
            col += v.shape[1]


def first_back(gps, projs, weight, tokens, grad_resid, vec, two, bias_up, bias_down, freq):
    n, w = tokens.shape
    rows = lambda c: pl.BlockSpec((QT, c), lambda i: (i, 0))
    whole = lambda a: pl.BlockSpec(a.shape, lambda i: (0, 0))
    return pl.pallas_call(
        partial(first_back_kernel, len(gps)),
        name="first_back",
        grid=(n // QT,),
        in_specs=[rows(g.shape[1]) for g in gps]
        + [whole(p) for p in projs]
        + [whole(weight), rows(w), rows(w), whole(vec)]
        + [whole(v) for v in (two, bias_up, bias_down, freq)],
        out_specs=[rows(w), whole(vec)],
        out_shape=[shaped((n, w), bf), shaped(vec.shape, f32)],
        scratch_shapes=[pltpu.VMEM((8, w), f32)],
        compiler_params=params(18),
        cost_estimate=cost(7e9, 1e7),
    )(*gps, *projs, weight, tokens, grad_resid, vec, two, bias_up, bias_down, freq)


def over_dp(v, k):
    return lax.ppermute(v, "dp", [(i, i ^ k) for i in range(4)])


def over_core(v):
    return lax.ppermute(v, "fsdp", [(i, i ^ 1) for i in range(8)])


def over_z(v, k):
    return lax.ppermute(v, "fsdp", [(i, i ^ (2 * k)) for i in range(8)])


def spread_dp(v):
    return [v] + [over_dp(v, k) for k in (1, 2, 3)]


def spread_z(v):
    return [v] + [over_z(v, k) for k in (1, 2, 3)]


def pairs(v):
    return (v[0] + v[1]) + (v[2] + v[3])


def tie(*values):
    return lax.optimization_barrier(values)


def place():
    d = lax.axis_index("dp")
    f = lax.axis_index("fsdp")
    return d, f // 2, f % 2


def here():
    return jnp.stack(place()).astype(jnp.int32)


def by_index(got, at):
    rows = []
    for j in range(4):
        rel = lax.bitwise_xor(at, j)
        v = got[3]
        for k in (2, 1, 0):
            v = jnp.where(rel == k, got[k], v)
        rows.append(v)
    return rows


def quarter(shard, j):
    r, cols = shard.shape
    return lax.dynamic_slice(shard, (j * (r // 4), 0), (r // 4, cols))


def arrange_kernel(at, *refs):
    out = refs[-1]
    for side in (0, 1):
        for k in range(4):
            for s in range(4):
                column = lax.bitwise_xor(at[1], s) * 2 + lax.bitwise_xor(at[2], side)
                out[column * 4 + lax.bitwise_xor(at[0], k)] = refs[side * 4 + k][s]


def arrange(own, other):
    r, cols = own[0].shape[1:]
    B = cols // 3
    spec = pltpu.PrefetchScalarGridSpec(
        num_scalar_prefetch=1,
        grid=(3,),
        in_specs=[pl.BlockSpec((4, r, B), lambda j, a: (0, 0, j))] * 8,
        out_specs=pl.BlockSpec((32, r, B), lambda j, a: (0, 0, j)),
    )
    out = pl.pallas_call(
        arrange_kernel,
        name="arrange",
        grid_spec=spec,
        out_shape=shaped((32, r, cols), bf),
        compiler_params=params(10),
        cost_estimate=cost(1e6, 4 * 32 * r * cols),
    )(here(), *own, *other)
    return out.reshape(32 * r, cols)


def fold_core_kernel(parts, extra, at, *refs):
    outs = refs[-4:]
    for k in range(4):
        col = 0
        for p in range(parts):
            a = refs[(k * parts + p) * 2][0, 0]
            b = refs[(k * parts + p) * 2 + 1][0, 0]
            w = a.shape[1]
            outs[k][0, :, col : col + w] = rnd(up(a) + up(b))
            col += w
        if extra and k:
            e = refs[8 * parts]
            v = e[0] if len(e.shape) == 3 else e[...]
            outs[k][0, :, col:] = v


def fold_core(mines, others, extra=None):
    r = mines[0].shape[1] // 4
    wide = sum(m.shape[2] for m in mines)
    more = 0
    args, specs = [], []
    for k in range(4):
        for m, o in zip(mines, others):
            for v in (m, o):
                w = v.shape[2]
                args.append(v.reshape(4, 4, r, w))
                specs.append(
                    pl.BlockSpec((1, 1, r, w), lambda j, a, k=k: (j, lax.bitwise_xor(a[0], k), 0, 0))
                )
    if extra is not None:
        args.append(extra)
        if extra.ndim == 3:
            more = extra.shape[2]
            specs.append(pl.BlockSpec((1, r, more), lambda j, a: (j, 0, 0)))
        else:
            more = extra.shape[1] // 4
            specs.append(pl.BlockSpec((r, more), lambda j, a: (0, j)))
    widths = [wide] + [wide + more] * 3
    spec = pltpu.PrefetchScalarGridSpec(
        num_scalar_prefetch=1,
        grid=(4,),
        in_specs=specs,
        out_specs=[pl.BlockSpec((1, r, w), lambda j, a: (j, 0, 0)) for w in widths],
    )
    return pl.pallas_call(
        partial(fold_core_kernel, len(mines), extra is not None),
        name="fold_core",
        grid_spec=spec,
        out_shape=[shaped((4, r, w), bf) for w in widths],
        compiler_params=params(10),
        cost_estimate=cost(1e6, 48 * r * wide),
    )(here(), *args)


def fold_dp_kernel(at, *refs):
    ins, outs = refs[:-4], refs[-4:]
    w = outs[0].shape[1]
    for k in range(4):
        to = lax.bitwise_xor(at[1], k)
        total = up(ins[0][to])
        for g in ins[1:]:
            total = total + up(g[to][:, :w])
        outs[k][...] = rnd(total)


def fold_dp(own, got):
    whole = lambda v: pl.BlockSpec(v.shape, lambda j, a: (0, 0, 0))
    r, w = own.shape[1:]
    spec = pltpu.PrefetchScalarGridSpec(
        num_scalar_prefetch=1,
        grid=(1,),
        in_specs=[whole(v) for v in [own] + got],
        out_specs=[pl.BlockSpec((r, w), lambda j, a: (0, 0))] * 4,
    )
    return pl.pallas_call(
        fold_dp_kernel,
        name="fold_dp",
        grid_spec=spec,
        out_shape=[shaped((r, w), bf)] * 4,
        compiler_params=params(10),
        cost_estimate=cost(1e6, 40 * r * w),
    )(here(), own, *got)


def pack_kernel(size, off, w, at, flat_ref, half_ref, *refs):
    ins, left, outs = refs[:4], refs[4:8], refs[8:]
    rows, wide = left[0].shape
    room = -(-size // 128) * 128
    for k in range(4):
        to = lax.bitwise_xor(at[1], k)
        outs[k][:rows, :wide] = left[k][...]
        outs[k][:rows, wide:] = rnd(pairs([up(g[to]) for g in ins]))
        outs[k][rows:, :] = jnp.zeros((1, outs[k].shape[1]), bf)
        mine = half_ref[:, pl.ds(pl.multiple_of(to * (2 * size), 128), size)]
        outs[k][rows:, :size] = rnd(mine)
        outs[k][rows:, room : room + w] = rnd(flat_ref[:, off : off + w])


def pack(flat, size, off, w, got, left):
    c = place()[2]
    half = lax.dynamic_slice(flat, (0, c * size), (1, 7 * size))
    r, cols = got[0].shape[1:]
    wide = left[0].shape[1] + cols
    whole = lambda v: pl.BlockSpec(v.shape, lambda j, a, n=v.ndim: (0,) * n)
    args = [flat, half, *got, *left]
    spec = pltpu.PrefetchScalarGridSpec(
        num_scalar_prefetch=1,
        grid=(1,),
        in_specs=[whole(v) for v in args],
        out_specs=[pl.BlockSpec((r + 1, wide), lambda j, a: (0, 0))] * 4,
    )
    return pl.pallas_call(
        partial(pack_kernel, size, off, w),
        name="pack",
        grid_spec=spec,
        out_shape=[shaped((r + 1, wide), bf)] * 4,
        compiler_params=params(10),
        cost_estimate=cost(1e6, 40 * r * wide),
    )(here(), *args)


def fold_z(got):
    return rnd(pairs([up(g) for g in got]))


def adam_terms(grad, first, second, master, decay):
    first_new = 0.9 * first + 0.1 * grad
    second_new = 0.999 * second + 0.001 * grad * grad
    first_hat = first_new / (1.0 - 0.9**STEP)
    second_hat = second_new / (1.0 - 0.999**STEP)
    update = first_hat / (jnp.sqrt(second_hat) + 1e-06) + decay * master
    return (first_new, second_new, update)


def step_kernel(plan, base, at, *refs):
    j = pl.program_id(0)
    sources, refs = refs[:4], refs[4:]
    count = len(plan)
    states, outs, sum_ref = refs[: 3 * count], refs[3 * count : 7 * count], refs[7 * count]
    rel = lax.bitwise_xor(at[0], j)

    @pl.when(j == 0)
    def _():
        sum_ref[...] = jnp.zeros_like(sum_ref)

    for t, chunks in enumerate(plan):
        w_ref, m_ref, v_ref = states[3 * t : 3 * t + 3]
        g_out, m_out, v_out, u_out = outs[4 * t : 4 * t + 4]
        total = jnp.zeros((1, 1), f32)
        size = jnp.sum(w_ref[...] * w_ref[...], keepdims=True)
        for row, rows, col, cols, read in chunks:
            g = read(sources[3], 3)
            for k in (2, 1, 0):
                g = jnp.where(rel == k, read(sources[k], k), g)
            g = up(g)
            to = (slice(row, row + rows), slice(col, col + cols))
            first_new, second_new, update = adam_terms(g, m_ref[to], v_ref[to], w_ref[to], 0.01)
            g_out[to] = g
            m_out[to] = first_new
            v_out[to] = second_new
            u_out[to] = update
            total = total + jnp.sum(update * update, keepdims=True)
        sum_ref[base + t : base + t + 1, :] += jnp.broadcast_to(total, (1, 128))
        sum_ref[base + t + 4 : base + t + 5, :] += jnp.broadcast_to(size, (1, 128))


def step(plan, base, sources, states):
    whole = lambda v: pl.BlockSpec(v.shape, lambda j, a, n=v.ndim: (0,) * n)
    rows = lambda v: pl.BlockSpec((v.shape[0] // 4, v.shape[1]), lambda j, a: (j, 0))
    flat = [v for s in states for v in s]
    spec = pltpu.PrefetchScalarGridSpec(
        num_scalar_prefetch=1,
        grid=(4,),
        in_specs=[whole(v) for v in sources] + [rows(v) for v in flat],
        out_specs=[rows(s[0]) for s in states for _ in range(4)]
        + [pl.BlockSpec((8, 128), lambda j, a: (0, 0))],
    )
    out = pl.pallas_call(
        partial(step_kernel, plan, base),
        name="step",
        grid_spec=spec,
        out_shape=[shaped(s[0].shape, f32) for s in states for _ in range(4)]
        + [shaped((8, 128), f32)],
        compiler_params=params(40),
        cost_estimate=cost(1e6, 28 * sum(s[0].size for s in states)),
    )(here(), *sources, *flat)
    return [out[4 * t : 4 * t + 4] for t in range(len(states))], out[-1]


def finish_kernel(*refs):
    norms = jnp.sqrt(refs[0][...] + refs[1][...])
    refs = refs[2:]
    refs[12][...] = norms
    for t in range(4):
        factor = 0.3 * (norms[t + 4 : t + 5, 0:1] / (norms[t : t + 1, 0:1] + 1e-06))
        refs[8 + t][...] = refs[t][...] - factor * refs[4 + t][...]


def finish(masters, updates, parts):
    rows = lambda v: pl.BlockSpec((v.shape[0] // 4, v.shape[1]), lambda j: (j, 0))
    whole = lambda: pl.BlockSpec((8, 128), lambda j: (0, 0))
    out = pl.pallas_call(
        finish_kernel,
        name="finish",
        grid=(4,),
        in_specs=[whole() for _ in parts] + [rows(v) for v in masters + updates],
        out_specs=[rows(v) for v in masters] + [whole()],
        out_shape=[shaped(v.shape, f32) for v in masters] + [shaped((8, 128), f32)],
        compiler_params=params(),
        cost_estimate=cost(1e6, 12 * sum(v.size for v in masters)),
    )(*parts, *masters, *updates)
    return out[:4], out[4]


def body(fast, tokens, cotangent, image_ids, patch_grid, *state):
    masters, vectors = state[:4], state[4]
    firsts, vector_first = state[5:9], state[9]
    seconds, vector_second = state[10:14], state[14]
    n, w = tokens.shape
    size = vectors.shape[0]
    heads = w // HD
    count = w // 128 // PAIRS
    L = 128 * PAIRS
    low = [rnd(m) for m in masters]
    gather = lambda v: lax.all_gather(v, "fsdp", axis=0, tiled=True)
    scatter = lambda v: lax.psum_scatter(v, "fsdp", scatter_dimension=0, tiled=True)
    whole = jnp.zeros((1,), jnp.int32)
    d, z, c = place()
    mine = jnp.stack([c]).astype(jnp.int32)
    halves = lambda x_t, y: (outer(x_t, y, 1 - mine, 4, 2), outer(x_t, y, mine, 4, 2))
    join = lambda rows: jnp.concatenate(rows, axis=-1)

    if fast:
        q_rows = low[0].shape[0] // 4
        row = jnp.pad(rnd(vectors), (0, low[0].shape[1] - size)).reshape(1, -1)
        got = spread_z(jnp.concatenate([quarter(low[0], d), row], 0))
        qkv_column = jnp.stack([g[:q_rows] for g in got])
        packed = jnp.concatenate(by_index([g[q_rows:, :size] for g in got], z), 0)
        other = over_core(packed)
        packed = jnp.stack([jnp.where(c == 0, packed, other), jnp.where(c == 0, other, packed)], 1)
        packed = packed.reshape(-1)
        up_part, out_part, down_part, qkv_column = tie(
            quarter(low[2], d), low[1], low[3], qkv_column
        )
        full_out = gather(out_part)
        qkv_own = spread_dp(qkv_column)
        up_column = jnp.stack(spread_z(up_part))
        full_down = gather(down_part)
    else:
        packed = gather(rnd(vectors))
        full_qkv, full_out, full_up, full_down = [gather(v) for v in low]
    vec = up(packed).reshape(1, -1)
    freq = vec[0, -w:].reshape(2, heads, 1, HD // 2)
    freq = jnp.broadcast_to(freq, (2, heads, 2, HD // 2)).reshape(2, w)
    grid_t = patch_grid.T
    given = jnp.where((image_ids >= 0)[:, None], cotangent, jnp.zeros_like(cotangent))
    grad_bias_down = jnp.sum(up(given), axis=0, keepdims=True)
    aug_q, aug_k, rng = tables(image_ids)

    normed, normed_t, cos, sin = first(tokens, vec, freq, grid_t)
    if fast:
        normed, *qkv_own = tie(normed, *qkv_own)
        full_qkv = arrange(qkv_own, [over_core(v) for v in qkv_own])
        up_column, full_qkv = tie(up_column, full_qkv)
        up_own = spread_dp(up_column)
    qkv = project(normed, full_qkv, vec, cos, sin)
    mix, mix_t, lb = attend(qkv, aug_q, aug_k, rng)
    if fast:
        mix, *up_own = tie(mix, *up_own)
        up_other = [over_core(v) for v in up_own]
    resid, normed_two, normed_two_t = branch(tokens, mix, full_out, vec)
    if fast:
        full_up = arrange(up_own, up_other)
    active, active_t, slope = hidden_units(normed_two, full_up, vec)
    if fast:
        theirs, own = halves(active_t, given)
        pieces = fold_core([own], [over_core(theirs)])
        active, slope, full_down = tie(active, slope, full_down)
        active, slope, *pieces = tie(active, slope, *pieces)
        got = [over_dp(v, k) for k, v in zip((1, 2, 3), pieces[1:])]
    else:
        down_full = outer(active_t, given, whole, 1, 1)[0]
    output = last(active, full_down, resid, vec)
    grad_hidden, grad_bias_up = hidden_back(given, full_down, slope)
    if fast:
        output, grad_hidden, *got = tie(output, grad_hidden, *got)
        down_z = fold_dp(pieces[0], got)
        grad_hidden, *down_z = tie(grad_hidden, *down_z)
        got = [down_z[0]] + [over_z(v, k) for k, v in zip((1, 2, 3), down_z[1:])]
        theirs, own = halves(normed_two_t, grad_hidden)
        own, *got = tie(own, *got)
        down_f = fold_z(got)
        more = down_f.reshape(4, -1, w)
        pieces = fold_core([own], [over_core(theirs)], more)
        grad_hidden, down_f, *pieces = tie(grad_hidden, down_f, *pieces)
        got = [over_dp(v, k) for k, v in zip((1, 2, 3), pieces[1:])]
    else:
        up_full = outer(normed_two_t, grad_hidden, whole, 1, 1)[0]
    grad_resid, grad_branch, grad_mix, sums_two = second_back(
        grad_hidden, full_up, resid, given, vec, full_out
    )
    if fast:
        out_theirs, out_own = halves(mix_t, grad_branch)
        out_sent = over_core(out_theirs)
    else:
        out_full = outer(mix_t, grad_branch, whole, 1, 1)[0]
    projs, sums_proj, sums_freq, qkv_parts = [], [], [], []
    for part in range(count):
        dq, dk, dv = attend_back(part, qkv, grad_mix, mix, lb, aug_q, aug_k, rng)
        if fast and part == 0:
            dq, *got = tie(dq, *got)
            up_width = pieces[0].shape[2]
            q = down_f.shape[0] // 4

            def read_down(i, q, skip, ref, k):
                return ref[i, :, skip:] if k else ref[q * i : q * i + q]

            plan = [[(q * i, q, 0, w, partial(read_down, i, q, up_width)) for i in range(4)]]
            later = [(plan, [down_f] + got, (masters[3], firsts[3], seconds[3]))]
            up_z = fold_dp(pieces[0], got)
            dq, *up_z = tie(dq, *up_z)
            got = [up_z[0]] + [over_z(v, k) for k, v in zip((1, 2, 3), up_z[1:])]
        if fast and part > 0:
            dq, *got = tie(dq, *got)
        gp, bs, fs = turn_back(part, dq, dk, dv, qkv, cos, sin, grid_t)
        projs.append(gp)
        sums_proj.append(bs)
        sums_freq.append(fs)
        if not fast:
            qkv_parts.append(outer(normed_t, gp, whole, 1, 1)[0])
        elif part == 0:
            theirs, own = halves(normed_t, gp)
            own, *got = tie(own, *got)
            up_f = fold_z(got)
            pieces = fold_core([own, out_own], [over_core(theirs), out_sent], up_f)
            grad_mix, up_f, *pieces = tie(grad_mix, up_f, *pieces)
            got = [over_dp(v, k) for k, v in zip((1, 2, 3), pieces[1:])]
        else:
            a_width = pieces[0].shape[2]
            q, wide = up_f.shape[0], up_f.shape[1] // 4

            def read_up(i, wide, skip, ref, k):
                return ref[i, :, skip:] if k else ref[:, wide * i : wide * i + wide]

            plan = [
                [(0, q, wide * i, wide, partial(read_up, i, wide, a_width)) for i in range(4)]
            ]
            later.append((plan, [up_f] + got, (masters[2], firsts[2], seconds[2])))
            theirs, own = halves(normed_t, gp)
            a_z = fold_dp(pieces[0], got)
            pieces = fold_core([own], [over_core(theirs)])
            projs[-1], *pieces = tie(gp, *pieces)
            got = [over_dp(v, k) for k, v in zip((1, 2, 3), pieces[1:])]
    freq_sums = join([s[:2] for s in sums_freq]).reshape(2, heads, 2, HD // 2)
    freq_grad = (freq_sums[:, :, 0] - freq_sums[:, :, 1]).reshape(1, -1)
    if fast:
        projs[-1], freq_grad = tie(projs[-1], freq_grad)
    tokens_grad, vector_full = first_back(
        projs, sums_proj, full_qkv, tokens, grad_resid, vec, sums_two, grad_bias_up, grad_bias_down, freq_grad
    )
    if fast:
        vector_full, *got = tie(vector_full, *got)
    off = vector_full.shape[1] - 2 * w
    if fast:
        flat = vector_full + over_core(vector_full)
        sends = pack(flat, size, off, w, [pieces[0]] + got, a_z)
        got = [sends[0]] + [over_z(s, k) for k, s in zip((1, 2, 3), sends[1:])]
        held = tie(*[v for entry in later for v in entry[1]], *sends)
        (down_step, down_square), (up_step, up_square) = [
            step(entry[0], 3 - i, list(held[4 * i : 4 * i + 4]), [entry[2]])
            for i, entry in enumerate(later)
        ]
        up_square, down_square, *got = tie(up_square, down_square, *got)
        got = spread_dp(rnd(pairs([up(g) for g in got])))
        tail = pairs([up(g[q_rows:]) for g in got])[0]
        room = -(-size // 128) * 128
        vector_grad = tail[:size]
        down_bias_grad = tail[room : room + w]

        def read(col, ref, k):
            return ref[:q_rows, col : col + L]

        plan = [
            [
                (0, q_rows, (s * count + p) * L, L, partial(read, p * (3 * L + w) + s * L))
                for p in range(count)
                for s in range(3)
            ],
            [(0, q_rows, i * L, L, partial(read, 3 * L + i * L)) for i in range(w // L)],
        ]
        states = [(masters[k], firsts[k], seconds[k]) for k in (0, 1)]
        last_steps, last_squares = step(plan, 0, got, states)
        steps = last_steps + up_step + down_step
        squares = last_squares + up_square + down_square
        squares = squares + over_core(squares)
        squares = squares + over_z(squares, 1)
        squares = [squares, over_z(squares, 2)]
        new_list, norms = finish(list(masters), [s[3] for s in steps], squares)
        update_norms, weight_norms = norms[:4, 0], norms[4:, 0]
    else:
        give = lambda v: lax.psum(scatter(up(v)), "dp")
        up_grad, down_grad, out_grad = give(up_full), give(down_full), give(out_full)
        done = [give(v) for v in qkv_parts]
        vector_grad = give(vector_full[0])
        down_bias_grad = lax.psum(grad_bias_down[0], ("dp", "fsdp"))
        qkv_grad = join([g[:, s * L : (s + 1) * L] for s in range(3) for g in done])
        steps = [
            (g, *adam_terms(g, firsts[k], seconds[k], masters[k], 0.01))
            for k, g in enumerate((qkv_grad, out_grad, up_grad, down_grad))
        ]
        weight_local = jnp.stack([jnp.sum(m * m) for m in masters])
        update_local = jnp.stack([jnp.sum(s[3] * s[3]) for s in steps])
        both = jnp.sqrt(lax.psum(jnp.stack([weight_local, update_local]), "fsdp"))
        weight_norms, update_norms = both[0], both[1]
        factor = 0.3 * (weight_norms / (update_norms + 1e-06))
        new_list = [masters[k] - factor[k] * steps[k][3] for k in range(4)]
    vector_step = adam_terms(vector_grad, vector_first, vector_second, vectors, 0.0)
    return (
        output,
        tokens_grad,
        *[s[0] for s in steps],
        vector_grad,
        down_bias_grad,
        *[s[1] for s in steps],
        vector_step[0],
        *[s[2] for s in steps],
        vector_step[1],
        *new_list,
        vectors - 0.2 * vector_step[2],
        weight_norms,
        update_norms,
    )


def solution(mesh):
    both = P(("dp", "fsdp"), None)
    mat = [P("fsdp", None)] * 4 + [P("fsdp")]
    in_specs = (both, both, P(("dp", "fsdp")), P(None, ("dp", "fsdp")), *mat, *mat, *mat)
    out_specs = (both, both, *mat, P(), *mat, *mat, *mat, P(), P())
    fast = mesh.shape["dp"] == 4 and mesh.shape["fsdp"] == 8
    return jax.shard_map(
        partial(body, fast), mesh=mesh, in_specs=in_specs, out_specs=out_specs, check_vma=False
    )
```
